128 devices in a mesh: ctx: 32 (over x, z, y_lo), fsdp: 4 (over y_hi, core).
Axes of the slice: x: 4, y: 4 (y_hi: 2, y_lo: 2; y = y_hi * 2 + y_lo), z: 4, core: 2. Of those that a mesh axis runs over, the one named last changes fastest.
Arguments:
- tokens: bfloat16 [4, 4096, 1536], P('fsdp', 'ctx'), may hold values from -6 to 6
- teacher: bfloat16 [4, 4096, 1536], P('fsdp', 'ctx'), may hold values from -27 to 27
- valid_mask: int32 [4, 4096], P('fsdp', 'ctx'), may hold values 0 or 1
- token_count: int32 [1], replicated, may hold values from 8192 to 16383
- routes: int32 [4, 4096, 4], P('fsdp', 'ctx'), may hold values from 0 to 5, all different within a row
- span_order: int32 [64], replicated, may hold values from 0 to 63, as said below
- w_query: bfloat16 [1536, 1536], P('fsdp'), may hold values from -0.3125 to 0.3125
- w_key: bfloat16 [1536, 256], P('fsdp'), may hold values from -0.15625 to 0.15625
- w_value: bfloat16 [1536, 256], P('fsdp'), may hold values from -0.15625 to 0.15625
- w_out: bfloat16 [1536, 1536], P('fsdp'), may hold values from -3.5 to 3.5
- norm_gain: bfloat16 [1536], P('fsdp'), may hold values from 0.25 to 1.75
- w_router: bfloat16 [1536, 6], P('fsdp'), may hold values from -0.078125 to 0.078125
- moe_gain: bfloat16 [1536], P('fsdp'), may hold values from 0.25 to 1.75
- w_gate: bfloat16 [6, 1536, 768], P(None, 'fsdp'), may hold values from -0.15625 to 0.15625
- w_up: bfloat16 [6, 1536, 768], P(None, 'fsdp'), may hold values from -0.15625 to 0.15625
- w_down: bfloat16 [6, 768, 1536], P(None, None, 'fsdp'), may hold values from -1 to 1
Outputs:
- output: bfloat16 [4, 4096, 1536], P('fsdp', 'ctx')
- loss: float32 [1], replicated
- grad_tokens: float32 [4, 4096, 1536], P('fsdp', 'ctx')
- grad_w_query: float32 [1536, 1536], P('fsdp')
- grad_w_key: float32 [1536, 256], P('fsdp')
- grad_w_value: float32 [1536, 256], P('fsdp')
- grad_w_out: float32 [1536, 1536], P('fsdp')
- grad_norm_gain: float32 [1536], P('fsdp')
- grad_w_router: float32 [1536, 6], P('fsdp')
- grad_moe_gain: float32 [1536], P('fsdp')
- grad_w_gate: float32 [6, 1536, 768], P(None, 'fsdp')
- grad_w_up: float32 [6, 1536, 768], P(None, 'fsdp')
- grad_w_down: float32 [6, 768, 1536], P(None, None, 'fsdp')
The draws below stay inside these ranges and needn't reach their ends.
Inputs may be any that keep to these rules, and one draw needn't show every extreme that they name: `routes`: each token names 4 different experts, and every expert is named by some token. Every span number appears once; stored span s (rows s * 64 to s * 64 + 63 of each sequence) holds the tokens from position span_order[s] * 64 on, the same for every sequence; stored spans 2 j and 2 j + 1 hold span numbers c and (the largest span number) - c for some c.
All inputs are finite; a program needn't handle non-finite values. No bound on the sum of `valid_mask` on one device may be relied on, other than what follows from the above.
Results may differ from the reference program's by a relative error of at most 0.03.
Values may be sent and summed in bfloat16 or wider, within the bound.
A program may use at most 256 MiB of HBM per device.

```python
import math
import jax
import jax.numpy as jnp
from jax import lax

D = 1536
H = 12
KV = 2
HD = 128
FF = 768
TOPK = 4
E = 6
SPAN = 64
LEN = 4096
SEQS = 4
HQ = 1536
KVW = 256


def draw_span_order(key, part):
    key = jax.random.fold_in(key, 7)
    spans = LEN // SPAN
    half_count = spans // 2
    first_spans = jax.random.permutation(key, half_count).astype(jnp.int32)
    paired = jnp.stack([first_spans, spans - 1 - first_spans], axis=1)
    return paired.reshape(spans).astype(jnp.int32)


def draw_teacher(key, part):
    key = jax.random.fold_in(key, 11)
    stored_row = jnp.arange(LEN, dtype=jnp.float32) / max(LEN - 1, 1)
    base = jnp.clip(jax.random.normal(key, (SEQS, LEN, D), jnp.float32), -2.2, 2.2)
    scale = 0.3 * jnp.exp(stored_row * 3.6888795)
    return (base * scale[None, :, None]).astype(jnp.bfloat16)


def plant(entries, key, least, top_value):
    longest = entries.shape.index(max(entries.shape))
    spots = []
    for shift in (0, 1):
        where = [jax.random.randint(jax.random.fold_in(key, axis), (), 0, length) for axis, length in enumerate(entries.shape)]
        where[longest] = (where[longest] + shift) % entries.shape[longest]
        spots.append(tuple(where))
    return entries.at[spots[0]].set(least).at[spots[1]].set(top_value)


def level_of(rng, dims, cuts, least, high):
    level = 1.0
    for dim, blocks in cuts:
        steps = jax.random.uniform(jax.random.fold_in(jax.random.fold_in(rng, 6), dim), (blocks,), jnp.float32, least / len(cuts), high / len(cuts))
        level = level * jnp.repeat(jnp.exp(steps), dims[dim] // blocks).reshape((-1,) + (1,) * (len(dims) - 1 - dim))
    return level


def picks_of(key, rows, number_of, top, lift):
    ranking = jax.random.permutation(jax.random.fold_in(key, 1), number_of)
    pull = ranking
    for power in range(3):
        pull = pull * pull // number_of
    pull = pull * lift // number_of
    lots = jax.random.randint(jax.random.fold_in(key, 2), (rows, number_of), 0, 4096) + pull
    holders = jax.random.permutation(jax.random.fold_in(key, 3), rows)[jnp.arange(number_of) % rows]
    lots = jnp.where(jnp.arange(rows)[:, None] == holders[None, :], 1 << 14, lots)
    score = lots * number_of + jnp.arange(number_of)
    return lax.top_k(score.astype(jnp.int32), top)[1].astype(jnp.int32)


def centred(key, shape, scale, most, split=(), kind=jnp.bfloat16):
    values = scale * jax.random.normal(key, shape, jnp.float32)
    if split:
        values = values * level_of(key, shape, split, -0.22, 0.18)
    return jnp.clip(values, -most, most).astype(kind)


def setup_inputs(seed: int = 0) -> dict:
    keys = jax.random.split(jax.random.key(seed), 17)
    tokens = centred(keys[0], (SEQS, LEN, D), 1.0, 6.0, ((0, 4), (1, 32)))
    teacher = draw_teacher(jax.random.fold_in(keys[16], 71), 0)
    valid_mask = plant((jax.random.randint(keys[2], (SEQS, LEN), 0, 4) < 3).astype(jnp.int32), jax.random.fold_in(keys[2], 1), 0, 1)
    token_count = jax.random.randint(keys[3], (1,), SEQS * LEN // 2, SEQS * LEN).astype(jnp.int32)
    routes = picks_of(keys[4], SEQS * LEN, E, TOPK, 5461).reshape((SEQS, LEN, TOPK))
    span_order = draw_span_order(jax.random.fold_in(keys[16], 71), 0)
    w_query = centred(keys[6], (D, HQ), (D // 4) ** -0.5, 0.3125, ((0, 4),))
    w_key = centred(keys[7], (D, KVW), D ** -0.5, 0.15625, ((0, 4),))
    w_value = centred(keys[8], (D, KVW), D ** -0.5, 0.15625, ((0, 4),))
    w_out = centred(keys[9], (HQ, D), (max(HQ // 512, 1)) ** -0.5, 3.5, ((0, 4),))
    norm_gain = jnp.clip(1.0 + 0.15 * jax.random.normal(keys[10], (D,), jnp.float32), 0.25, 1.75).astype(jnp.bfloat16)
    w_router = centred(keys[11], (D, E), (4 * D) ** -0.5, 0.078125, ((0, 4),))
    moe_gain = jnp.clip(1.0 + 0.15 * jax.random.normal(keys[12], (D,), jnp.float32), 0.25, 1.75).astype(jnp.bfloat16)
    w_gate = centred(keys[13], (E, D, FF), D ** -0.5, 0.15625, ((1, 4),))
    w_up = centred(keys[14], (E, D, FF), D ** -0.5, 0.15625, ((1, 4),))
    w_down = centred(keys[15], (E, FF, D), (max(FF // 24, 1)) ** -0.5, 1.0, ((2, 4),))
    return {"tokens": tokens, "teacher": teacher, "valid_mask": valid_mask, "token_count": token_count, "routes": routes, "span_order": span_order, "w_query": w_query, "w_key": w_key, "w_value": w_value, "w_out": w_out, "norm_gain": norm_gain, "w_router": w_router, "moe_gain": moe_gain, "w_gate": w_gate, "w_up": w_up, "w_down": w_down}


@jax.custom_vjp
def low(v):
    return lax.optimization_barrier(v.astype(jnp.bfloat16)).astype(jnp.float32)

@jax.custom_vjp
def low_back(v):
    return v

def low_keep(v):
    return (low(v), None)

def low_pass(kept, grad):
    return (grad,)

def back_keep(v):
    return (v, None)

def back_low(kept, grad):
    return (low(grad),)
low.defvjp(low_keep, low_pass)
low_back.defvjp(back_keep, back_low)
EPS = 1e-06
BASE = 1000000.0
NEGATIVE = -1e+30
HIGH = lax.Precision.HIGHEST

def rms_norm(values, gain):
    return values * lax.rsqrt(lax.optimization_barrier(jnp.mean(values * values, axis=-1, keepdims=True)) + EPS) * gain

def angle_tables(position, head_size):
    half_size = head_size // 2
    frequency = jnp.exp(-(jnp.arange(half_size, dtype=jnp.float32) * 2.0 / head_size) * math.log(BASE))
    angles = position.astype(jnp.float32)[:, None] * frequency[None, :]
    return (jnp.cos(angles)[:, None, :], jnp.sin(angles)[:, None, :])

def rotate(values, cosine, sine_part):
    half_size = values.shape[-1] // 2
    first_half = values[..., :half_size]
    second_half = values[..., half_size:]
    return jnp.concatenate([first_half * cosine - second_half * sine_part, second_half * cosine + first_half * sine_part], axis=-1)

def attend(query_rows, key_rows, value_rows, position):
    length = query_rows.shape[0]
    groups = H // KV
    head_values = query_rows.reshape(length, KV, groups, HD)
    block_rows = math.gcd(512, length)
    score_scale = HD ** (-0.5)

    def one_block(block_index):
        row_start = block_index * block_rows
        query_block = lax.dynamic_slice_in_dim(head_values, row_start, block_rows, 0)
        query_pos = lax.dynamic_slice_in_dim(position, row_start, block_rows, 0)
        logits = low_back(jnp.einsum('qkgd,tkd->kgqt', query_block, key_rows, precision=HIGH) * score_scale)
        allowed = position[None, :] <= query_pos[:, None]
        logits = jnp.where(allowed, logits, NEGATIVE)
        largest = lax.optimization_barrier(jnp.max(logits, axis=-1, keepdims=True))
        weights = jnp.exp(logits - largest)
        probabilities = low(weights / lax.optimization_barrier(jnp.sum(weights, axis=-1, keepdims=True)))
        return jnp.einsum('kgqt,tkd->qkgd', probabilities, value_rows, precision=HIGH)
    outputs = lax.map(jax.checkpoint(one_block), jnp.arange(length // block_rows, dtype=jnp.int32))
    return outputs.reshape(length, H * HD)

def block_layer(inputs, selected, parameters, cosine, sine_part, position):
    w_query, w_key, w_value, w_out, norm_gain, w_router, moe_gain, w_gate, w_up, w_down = parameters
    length = inputs.shape[0]
    normed_one = low(rms_norm(inputs, norm_gain))
    query_raw = low_back(jnp.dot(normed_one, w_query, precision=HIGH))
    key_raw = low_back(jnp.dot(normed_one, w_key, precision=HIGH))
    value_rows = low(low_back(jnp.dot(normed_one, w_value, precision=HIGH))).reshape(length, KV, HD)
    query_rows = low(rotate(query_raw.reshape(length, H, HD), cosine, sine_part))
    key_rows = low(rotate(key_raw.reshape(length, KV, HD), cosine, sine_part))
    attended = low(low_back(attend(query_rows, key_rows, value_rows, position)))
    hidden = inputs + low_back(jnp.dot(attended, w_out, precision=HIGH))
    normed_two = low(rms_norm(hidden, moe_gain))
    router_logits = low_back(jnp.dot(normed_two, w_router, precision=HIGH))
    router_probs = jax.nn.softmax(router_logits, axis=-1)
    gate_weights = router_probs * selected
    gate_raw = low_back(jnp.einsum('ld,edf->elf', normed_two, w_gate, precision=HIGH))
    up_raw = low_back(jnp.einsum('ld,edf->elf', normed_two, w_up, precision=HIGH))
    expert_hidden = low(jax.nn.gelu(gate_raw, approximate=True) * up_raw)
    expert_out = low_back(jnp.einsum('elf,efd->eld', expert_hidden, w_down, precision=HIGH))
    mixture = jnp.einsum('le,eld->ld', gate_weights, expert_out, precision=HIGH)
    return hidden + mixture

def reference(tokens, teacher, valid_mask, token_count, routes, span_order, w_query, w_key, w_value, w_out, norm_gain, w_router, moe_gain, w_gate, w_up, w_down):
    parameters = tuple((item.astype(jnp.float32) for item in (w_query, w_key, w_value, w_out, norm_gain, w_router, moe_gain, w_gate, w_up, w_down)))
    inputs = tokens.astype(jnp.float32)
    target = teacher.astype(jnp.float32)
    valid_rows = valid_mask.astype(jnp.float32)[..., None]
    expert_ids = jnp.arange(E, dtype=jnp.int32)
    selected = lax.optimization_barrier(jnp.sum((routes[..., None] == expert_ids).astype(jnp.float32), axis=-2))
    row_ids = jnp.arange(LEN, dtype=jnp.int32)
    position = (span_order[row_ids // SPAN] * SPAN + row_ids % SPAN).astype(jnp.int32)
    cosine, sine_part = angle_tables(position, HD)
    norm_factor = token_count[0].astype(jnp.float32) * D

    def whole_layer(layer_inputs, *layer_parameters):

        def one_sequence(sequence_item):
            return block_layer(sequence_item[0], sequence_item[1], layer_parameters, cosine, sine_part, position)
        result = lax.map(jax.checkpoint(one_sequence), (layer_inputs, selected))
        error_rows = result - target
        loss_value = jnp.sum(valid_rows * error_rows * error_rows) / norm_factor
        return (result, loss_value)
    (result, loss_value), pull_back = jax.vjp(whole_layer, inputs, *parameters)
    gradients = pull_back((jnp.zeros_like(result), jnp.ones_like(loss_value)))
    return (result.astype(jnp.bfloat16), loss_value.reshape(1), gradients[0], gradients[1], gradients[2], gradients[3], gradients[4], gradients[5], gradients[6], gradients[7], gradients[8], gradients[9], gradients[10])
```

```python
import math

import jax
import jax.numpy as jnp
from jax import lax
from jax.experimental import pallas as pl
from jax.experimental.pallas import tpu as pltpu
from jax.sharding import PartitionSpec as P

H = 12
KV = 2
HD = 128
E = 6
D = 1536
FF = 768
GROUPS = H // KV
ROWS = 128
SPAN = 64
HALF = 384
SLICE = 3 * HALF
QKV = 2048
SHARD = 384
EPS = 1e-06
BASE = 1000000.0
NEGATIVE = -1e30
SCALE = HD**-0.5
MESH = pl.DeviceIdType.MESH
BF = jnp.bfloat16
F32 = jnp.float32


def place():
    ctx = lax.axis_index("ctx")
    shard = lax.axis_index("fsdp")
    return ctx // 8, (ctx // 2) % 4, ctx % 2, shard // 2, shard % 2


def device(x, z, y_lo, y_hi, core):
    return (x * 8 + z * 2 + y_lo, y_hi * 2 + core)


def x_peers(at):
    x, z, y_lo, y_hi, core = at
    return [device((x + k) % 4, z, y_lo, y_hi, core) for k in (1, 2, 3)]


def z_peers(at):
    x, z, y_lo, y_hi, core = at
    return [device(x, (z + k) % 4, y_lo, y_hi, core) for k in (1, 2, 3)]


def group_member(at, shard_hi, core):
    x, z, y_lo, y_hi, _ = at
    y_lo_there = (y_lo + y_hi + shard_hi) % 2
    return device(x, z, y_lo_there, shard_hi, core)


class Net:
    def __init__(self, send_sem, recv_sem, local_sem):
        self.sems = (send_sem, recv_sem, local_sem)
        self.remote = 0
        self.locals = 0
        self.open = {}
        self.copies = []

    def greet(self, peers):
        barrier = pltpu.get_barrier_semaphore()
        for peer in peers:
            pl.semaphore_signal(barrier, inc=1, device_id=peer, device_id_type=MESH)
        pl.semaphore_wait(barrier, len(peers))

    def send(self, src, dst, peer):
        slot = self.remote
        self.remote += 1
        copy = pltpu.make_async_remote_copy(
            src_ref=src,
            dst_ref=dst,
            send_sem=self.sems[0].at[slot],
            recv_sem=self.sems[1].at[slot],
            device_id=peer,
            device_id_type=MESH,
        )
        copy.start()
        self.open[id(copy)] = copy.wait
        self.copies.append(copy)
        return copy

    def keep(self, src, dst):
        slot = self.locals
        self.locals += 1
        copy = pltpu.make_async_copy(src, dst, self.sems[2].at[slot])
        copy.start()
        self.open[id(copy)] = copy.wait
        self.copies.append(copy)
        return copy

    def arrived(self, copy):
        copy.wait_recv()
        self.open[id(copy)] = copy.wait_send

    def kept(self, copy):
        copy.wait()
        del self.open[id(copy)]

    def finish(self):
        for wait in self.open.values():
            wait()


def exchange(body, inputs, outs, remote, local, number, name):
    count = len(inputs)

    def kernel(*refs):
        net = Net(*refs[-3:])
        body(net, refs[:count], refs[count:-3])
        net.finish()

    any_spec = pl.BlockSpec(memory_space=pl.ANY)
    return pl.pallas_call(
        kernel,
        out_shape=[jax.ShapeDtypeStruct(shape, kind) for shape, kind in outs],
        in_specs=[any_spec] * count,
        out_specs=[any_spec] * len(outs),
        scratch_shapes=[
            pltpu.SemaphoreType.DMA((remote,)),
            pltpu.SemaphoreType.DMA((remote,)),
            pltpu.SemaphoreType.DMA((max(local, 1),)),
        ],
        compiler_params=pltpu.CompilerParams(collective_id=number, has_side_effects=True),
        name=name,
    )(*inputs)


def gather_attention_weights(parts, number):
    def body(net, ins, outs):
        at = place()
        x, z, y_lo, y_hi, core = at
        shard = y_hi * 2 + core
        sibling = device(x, z, y_lo, y_hi, 1 - core)
        partner = device(x, z, 1 - y_lo, 1 - y_hi, core)
        here = lax.select(core == 0, x, z)
        ring = []
        for k in (1, 2, 3):
            ring.append(
                device(
                    lax.select(core == 0, (x + k) % 4, x),
                    lax.select(core == 0, z, (z + k) % 4),
                    y_lo,
                    y_hi,
                    core,
                )
            )
        net.greet([sibling, partner] + ring)

        def block(array, owner, start, size):
            width = ins[array].shape[1]
            return outs[array].at[pl.ds(pl.multiple_of(owner * SHARD + start, 32), size), pl.ds(0, width)]

        count = len(ins)
        quarter = SHARD // 4
        first = []
        for a in range(count):
            rows = pl.ds(pl.multiple_of(here * quarter, 32), quarter)
            first.append(net.send(ins[a].at[rows, :], block(a, shard, here * quarter, quarter), partner))
        for a in range(count):
            net.send(ins[a], block(a, shard, 0, SHARD), sibling)
            net.keep(ins[a], block(a, shard, 0, SHARD))
        far = (1 - y_hi) * 2 + core
        around = []
        for a in range(count):
            net.arrived(first[a])
            mine = block(a, far, here * quarter, quarter)
            around.append([net.send(mine, mine, peer) for peer in ring])
            net.send(mine, mine, sibling)
        for k in (1, 3, 2):
            origin = (here + 4 - k) % 4
            for a in range(count):
                net.arrived(around[a][k - 1])
                piece = block(a, far, origin * quarter, quarter)
                net.send(piece, piece, sibling)

    n = len(parts)
    return exchange(
        body, parts, [((D, part.shape[1]), BF) for part in parts], n * 9, n, number, "attention_weights"
    )


def gather_expert_weights(w_gate, w_up, w_down, number):
    quarter = HALF // 4

    def body(net, ins, outs):
        gate, up, down = ins
        wide, low = outs
        at = place()
        x, z, y_lo, y_hi, core = at
        shard = y_hi * 2 + core
        sibling = device(x, z, y_lo, y_hi, 1 - core)
        partners = [device(x, z, 1 - y_lo, 1 - y_hi, c) for c in (0, 1)]
        ring = []
        for k in (1, 2, 3):
            ring.append(
                device(
                    lax.select(core == 0, (x + k) % 4, x),
                    lax.select(core == 0, z, (z + k) % 4),
                    y_lo,
                    y_hi,
                    core,
                )
            )
        net.greet([sibling] + partners + ring)

        def source(owner, h, kind, start, size):
            index = owner * 3 + h
            expert = index // 2
            offset = pl.multiple_of((index % 2) * HALF, 128)
            if kind < 2:
                return ins[kind].at[expert, pl.ds(start, size), pl.ds(offset, HALF)]
            return down.at[expert, pl.ds(pl.multiple_of(offset + start, 32), size), :]

        def target(from_shard, h, kind, start, size):
            if kind < 2:
                rows = pl.multiple_of(from_shard * SHARD + start, 32)
                return wide.at[pl.ds(rows, size), pl.ds(kind * SLICE + h * HALF, HALF)]
            columns = pl.multiple_of(from_shard * SHARD, 128)
            return low.at[pl.ds(pl.multiple_of(h * HALF + start, 32), size), pl.ds(columns, SHARD)]

        cells = [(h, kind) for kind in range(3) for h in range(3)]
        first = []
        for step in (0, 1):
            far_core = (core + step) % 2
            start = pl.multiple_of(lax.select(far_core == 0, x, z) * quarter, 32)
            owner = (1 - y_hi) * 2 + far_core
            peer = device(x, z, 1 - y_lo, 1 - y_hi, far_core)
            first.append(
                [
                    net.send(source(owner, h, kind, start, quarter), target(shard, h, kind, start, quarter), peer)
                    for h, kind in cells
                ]
            )
        for h, kind in cells:
            other = y_hi * 2 + 1 - core
            net.send(source(other, h, kind, 0, HALF), target(shard, h, kind, 0, HALF), sibling)
            net.keep(source(shard, h, kind, 0, HALF), target(shard, h, kind, 0, HALF))
        here = pl.multiple_of(lax.select(core == 0, x, z) * quarter, 32)
        for step in (0, 1):
            from_shard = (1 - y_hi) * 2 + (core + step) % 2
            for n, (h, kind) in enumerate(cells):
                net.arrived(first[step][n])
                mine = target(from_shard, h, kind, here, quarter)
                for peer in ring:
                    net.send(mine, mine, peer)

    return exchange(
        body,
        (w_gate, w_up, w_down),
        [((D, 2 * SLICE), BF), ((SLICE, D), BF)],
        9 * 9,
        9,
        number,
        "expert_weights",
    )


def gather_keys(local, number):
    def body(net, ins, outs):
        (mine,), (whole,) = ins, outs
        at = place()
        x, z, y_lo, y_hi, core = at
        partner = device(x, z, 1 - y_lo, y_hi, core)
        peers = (x_peers(at), z_peers(at))
        net.greet([partner] + peers[0] + peers[1])
        spot = whole.at[x, z, y_lo]
        own = net.keep(mine, spot)
        near = net.send(mine, spot, partner)
        net.kept(own)
        net.arrived(near)
        half = KV * HD
        order = (1, 0)
        stage = []
        for part in (0, 1):
            block = whole.at[x, z, :, :, pl.ds(part * half, half)]
            stage.append([net.send(block, block, peer) for peer in peers[order[part]]])
        for part in (0, 1):
            for copy in stage[part]:
                net.arrived(copy)
            if part == 0:
                block = whole.at[x, :, :, :, pl.ds(0, half)]
            else:
                block = whole.at[:, z, :, :, pl.ds(half, half)]
            for peer in peers[part]:
                net.send(block, block, peer)

    return exchange(
        body, (local,), [((4, 4, 2, ROWS, 2 * KV * HD), BF)], 13, 1, number, "keys_values"
    )[0]


def group_peers(at):
    x, z, y_lo, y_hi, core = at
    return [
        (y_hi * 2 + 1 - core, device(x, z, y_lo, y_hi, 1 - core)),
        ((1 - y_hi) * 2 + core, device(x, z, 1 - y_lo, 1 - y_hi, core)),
        ((1 - y_hi) * 2 + 1 - core, device(x, z, 1 - y_lo, 1 - y_hi, 1 - core)),
    ]


def group_gather(parts, number, name):
    def body(net, ins, outs):
        at = place()
        shard = at[3] * 2 + at[4]
        peers = group_peers(at)
        net.greet([peer for _, peer in peers])
        for mine, whole in zip(ins, outs):
            spot = whole.at[shard]
            net.keep(mine, spot)
            for _, peer in peers:
                net.send(mine, spot, peer)

    n = len(parts)
    return exchange(
        body, parts, [((4,) + part.shape, part.dtype) for part in parts], 3 * n, n, number, name
    )


def group_swap(parts, number, name):
    def body(net, ins, outs):
        at = place()
        shard = at[3] * 2 + at[4]
        peers = group_peers(at)
        net.greet([peer for _, peer in peers])
        for mine, whole in zip(ins, outs):
            net.keep(mine.at[shard], whole.at[shard])
            for there, peer in peers:
                net.send(mine.at[there], whole.at[shard], peer)

    n = len(parts)
    return exchange(
        body, parts, [(part.shape, part.dtype) for part in parts], 3 * n, n, number, name
    )


def add_up(pieces, axis):
    return jnp.sum(pieces.astype(F32), axis=axis).astype(BF)


def reduce_keys(grads, number):
    half = KV * HD

    def first(net, ins, outs):
        (whole,), (got,) = ins, outs
        at = place()
        x, z = at[0], at[1]
        peers = (x_peers(at), z_peers(at))
        net.greet(peers[0] + peers[1])
        net.keep(whole.at[x, :, :, :, pl.ds(0, half)], got.at[0, 0])
        net.keep(whole.at[:, z, :, :, pl.ds(half, half)], got.at[1, 0])
        for k in (1, 2, 3):
            net.send(whole.at[(x + k) % 4, :, :, :, pl.ds(0, half)], got.at[0, k], peers[0][k - 1])
            net.send(whole.at[:, (z + k) % 4, :, :, pl.ds(half, half)], got.at[1, k], peers[1][k - 1])

    (got,) = exchange(first, (grads,), [((2, 4, 4, 2, ROWS, half), BF)], 6, 2, number, "kv_first")
    part = add_up(got, 1)

    def second(net, ins, outs):
        (whole,), (got,) = ins, outs
        at = place()
        x, z = at[0], at[1]
        peers = (x_peers(at), z_peers(at))
        net.greet(peers[0] + peers[1])
        net.keep(whole.at[0, z], got.at[0, 0])
        net.keep(whole.at[1, x], got.at[1, 0])
        for k in (1, 2, 3):
            net.send(whole.at[0, (z + k) % 4], got.at[0, k], peers[1][k - 1])
            net.send(whole.at[1, (x + k) % 4], got.at[1, k], peers[0][k - 1])

    (got,) = exchange(second, (part,), [((2, 4, 2, ROWS, half), BF)], 6, 2, number + 1, "kv_second")
    part = add_up(got, 1)

    def third(net, ins, outs):
        (whole,), (got,) = ins, outs
        x, z, y_lo, y_hi, core = place()
        partner = device(x, z, 1 - y_lo, y_hi, core)
        net.greet([partner])
        net.keep(whole.at[:, y_lo], got.at[0])
        net.send(whole.at[:, 1 - y_lo], got.at[1], partner)

    (got,) = exchange(third, (part,), [((2, 2, ROWS, half), BF)], 1, 1, number + 2, "kv_third")
    total = jnp.sum(got.astype(F32), axis=0)
    return total[0], total[1]


def reduce_grads(grads, number, name):
    columns = grads.shape[2]
    half, cell = columns // 2, columns // 4

    def first(net, ins, outs):
        (whole,), (got,) = ins, outs
        at = place()
        own = (at[0], at[1])
        peers = (x_peers(at), z_peers(at))
        net.greet(peers[0] + peers[1])
        for k in (0, 1, 3, 2):
            for part in (0, 1):
                rows = pl.ds(pl.multiple_of(((own[part] + k) % 4) * 96, 32), 96)
                block = whole.at[:, rows, pl.ds(part * half, half)]
                if k == 0:
                    net.keep(block, got.at[part, 0])
                else:
                    net.send(block, got.at[part, k], peers[part][k - 1])

    (got,) = exchange(first, (grads,), [((2, 4, 4, 96, half), BF)], 6, 2, number, name + "_first")
    part_sum = add_up(got, 1)

    def second(net, ins, outs):
        (whole,), (got,) = ins, outs
        at = place()
        own = (at[1], at[0])
        peers = (z_peers(at), x_peers(at))
        net.greet(peers[0] + peers[1])
        for k in (0, 1, 3, 2):
            for part in (0, 1):
                j = (own[part] + k) % 4
                rows = pl.ds(pl.multiple_of((j // 2) * 48, 16), 48)
                block = whole.at[part, :, rows, pl.ds(pl.multiple_of((j % 2) * cell, 128), cell)]
                if k == 0:
                    net.keep(block, got.at[part, 0])
                else:
                    net.send(block, got.at[part, k], peers[part][k - 1])

    (got,) = exchange(second, (part_sum,), [((2, 4, 4, 48, cell), BF)], 6, 2, number + 1, name + "_second")
    part_sum = add_up(got, 1)

    def third(net, ins, outs):
        (whole,), (got,) = ins, outs
        x, z, y_lo, y_hi, core = place()
        others = [
            device(x, z, (y_lo + k // 4) % 2, (y_hi + (k // 2) % 2) % 2, (core + k) % 2) for k in range(1, 8)
        ]
        net.greet(others)
        for k in (1, 2, 3):
            hi, low = k // 2, k % 2
            there_hi, there_core = (y_lo + hi) % 2, (core + low) % 2
            shard = there_hi * 2 + there_core
            net.send(whole.at[:, shard], got.at[y_lo, core], device(x, z, y_hi, there_hi, there_core))
        mine = whole.at[:, y_lo * 2 + core]
        spot = got.at[y_lo, core]

        @pl.when(y_lo == y_hi)
        def _():
            copy = pltpu.make_async_copy(mine, spot, net.sems[2].at[0])
            copy.start()
            copy.wait()

        @pl.when(y_lo != y_hi)
        def _():
            copy = pltpu.make_async_remote_copy(
                src_ref=mine,
                dst_ref=spot,
                send_sem=net.sems[0].at[3],
                recv_sem=net.sems[1].at[3],
                device_id=device(x, z, y_hi, y_lo, core),
                device_id_type=MESH,
            )
            copy.start()
            copy.wait()

    (got,) = exchange(third, (part_sum,), [((2, 2, 2, 48, cell), BF)], 4, 1, number + 2, name + "_third")
    part_sum = add_up(got, 0)

    def gather(net, ins, outs):
        (mine,), (whole,) = ins, outs
        at = place()
        x, z, y_lo, y_hi, core = at
        partner = device(x, z, 1 - y_lo, y_hi, core)
        peers = (x_peers(at), z_peers(at))
        net.greet([partner] + peers[0] + peers[1])
        coordinates = ((x, z), (z, x))

        def rows_of(i, j):
            return pl.ds(pl.multiple_of(i * 96 + (j // 2) * 48, 16), 48)

        def columns_of(part, j):
            return pl.ds(pl.multiple_of(part * half + (j % 2) * cell, 128), cell)

        near, own = [], []
        for part in (0, 1):
            i, j = coordinates[part]
            spot = whole.at[pl.ds(2 * y_lo, 2), rows_of(i, j), columns_of(part, j)]
            own.append(net.keep(mine.at[:, part], spot))
            near.append(net.send(mine.at[:, part], spot, partner))
        for copy in own:
            net.kept(copy)
        stage = []
        for part in (0, 1):
            i, j = coordinates[part]
            net.arrived(near[part])
            block = whole.at[:, rows_of(i, j), columns_of(part, j)]
            stage.append([net.send(block, block, peer) for peer in peers[1 - part]])
        for part in (0, 1):
            i, j = coordinates[part]
            for copy in stage[part]:
                net.arrived(copy)
            rows = pl.ds(pl.multiple_of(i * 96, 32), 96)
            block = whole.at[:, rows, pl.ds(part * half, half)]
            for peer in peers[part]:
                net.send(block, block, peer)

    return exchange(gather, (part_sum,), [((4, SHARD, columns), BF)], 14, 2, number + 3, name + "_gather")[0]


BLOCK = 4 * SPAN
QUERIES = GROUPS * SPAN


def stack_heads(ref, span, kv):
    rows = slice(span * SPAN, (span + 1) * SPAN)
    return jnp.concatenate(
        [ref[rows, (kv * GROUPS + g) * HD : (kv * GROUPS + g + 1) * HD] for g in range(GROUPS)], axis=0
    )


def unstack_heads(ref, span, kv, values):
    rows = slice(span * SPAN, (span + 1) * SPAN)
    for g in range(GROUPS):
        head = kv * GROUPS + g
        ref[rows, head * HD : (head + 1) * HD] = values[g * SPAN : (g + 1) * SPAN, :]


def nt(a, b):
    return lax.dot_general(a, b, (((1,), (1,)), ((), ())), preferred_element_type=F32)


def tn(a, b):
    return lax.dot_general(a, b, (((0,), (0,)), ((), ())), preferred_element_type=F32)


def block_rows(where, b, ref):
    return jnp.concatenate(
        [ref[pl.ds(pl.multiple_of(where[b * 4 + i] * SPAN, SPAN), SPAN), :] for i in range(4)], axis=0
    )


def lead_of_keys():
    keys = lax.broadcasted_iota(jnp.int32, (BLOCK, QUERIES), 0)
    queries = lax.broadcasted_iota(jnp.int32, (BLOCK, QUERIES), 1)
    return keys - queries % SPAN


def attend_kernel(where, spans, q_ref, kv_ref, o_ref, lse_ref):
    lead = lead_of_keys()
    for s in range(2):
        span = spans[s]
        stacked = [stack_heads(q_ref, s, kv) for kv in range(KV)]

        def body(b, carry):
            keys_values = block_rows(where, b, kv_ref)
            allowed = lead <= span * SPAN - b * BLOCK
            out = []
            for kv in range(KV):
                top, total, acc = carry[kv]
                keys = keys_values[:, kv * HD : (kv + 1) * HD]
                values = keys_values[:, (KV + kv) * HD : (KV + kv + 1) * HD]
                logits = jnp.where(allowed, nt(keys, stacked[kv]) * SCALE, NEGATIVE)
                new_top = jnp.maximum(top, jnp.max(logits, axis=0, keepdims=True))
                weights = jnp.exp(logits - new_top)
                shrink = jnp.exp(top - new_top)
                total = total * shrink + jnp.sum(weights, axis=0, keepdims=True)
                acc = acc * shrink + tn(values, weights.astype(BF))
                out.append((new_top, total, acc))
            return tuple(out)

        start = tuple(
            (
                jnp.full((1, QUERIES), NEGATIVE, F32),
                jnp.zeros((1, QUERIES), F32),
                jnp.zeros((HD, QUERIES), F32),
            )
            for _ in range(KV)
        )
        final = lax.fori_loop(0, span // 4 + 1, body, start)
        for kv in range(KV):
            top, total, acc = final[kv]
            unstack_heads(o_ref, s, kv, (acc / total).T)
            lse_ref[2 * s + kv : 2 * s + kv + 1, :] = top + jnp.log(total)
    lse_ref[4:8, :] = jnp.zeros((4, QUERIES), F32)


def attend(where, spans, query, keys_values):
    smem = pl.BlockSpec(memory_space=pltpu.SMEM)
    vmem = pl.BlockSpec(memory_space=pltpu.VMEM)
    return pl.pallas_call(
        attend_kernel,
        out_shape=[jax.ShapeDtypeStruct((ROWS, H * HD), F32), jax.ShapeDtypeStruct((8, QUERIES), F32)],
        in_specs=[smem, smem, vmem, vmem],
        out_specs=[vmem, vmem],
        compiler_params=pltpu.CompilerParams(vmem_limit_bytes=48 << 20),
        cost_estimate=pl.CostEstimate(flops=1_800_000_000, transcendentals=3_400_000, bytes_accessed=6 << 20),
        name="attend",
    )(where, spans, query, keys_values)


def attend_back_kernel(where, spans, q_ref, kv_ref, do_ref, o_ref, lse_ref, dq_ref, dkv_ref, acc_ref):
    lead = lead_of_keys()
    acc_ref[...] = jnp.zeros_like(acc_ref)
    for s in range(2):
        span = spans[s]
        stacked = [stack_heads(q_ref, s, kv) for kv in range(KV)]
        d_out = [stack_heads(do_ref, s, kv) for kv in range(KV)]
        delta = [
            jnp.sum((d_out[kv].astype(F32) * stack_heads(o_ref, s, kv)).T, axis=0, keepdims=True) for kv in range(KV)
        ]
        lse = [lse_ref[2 * s + kv : 2 * s + kv + 1, :] for kv in range(KV)]

        def body(b, carry):
            keys_values = block_rows(where, b, kv_ref)
            allowed = lead <= span * SPAN - b * BLOCK
            out, key_grads, value_grads = [], [], []
            for kv in range(KV):
                keys = keys_values[:, kv * HD : (kv + 1) * HD]
                values = keys_values[:, (KV + kv) * HD : (KV + kv + 1) * HD]
                logits = nt(keys, stacked[kv]) * SCALE
                weights = jnp.where(allowed, jnp.exp(logits - lse[kv]), 0.0)
                d_weights = nt(values, d_out[kv])
                d_logits = (weights * (d_weights - delta[kv])).astype(BF)
                out.append(carry[kv] + tn(keys, d_logits))
                key_grads.append(jnp.dot(d_logits, stacked[kv], preferred_element_type=F32) * SCALE)
                value_grads.append(jnp.dot(weights.astype(BF), d_out[kv], preferred_element_type=F32))
            grads = jnp.concatenate(key_grads + value_grads, axis=1)
            for i in range(4):
                rows = pl.ds(pl.multiple_of(where[b * 4 + i] * SPAN, SPAN), SPAN)
                acc_ref[rows, :] += grads[i * SPAN : (i + 1) * SPAN, :]
            return tuple(out)

        start = tuple(jnp.zeros((HD, QUERIES), F32) for _ in range(KV))
        final = lax.fori_loop(0, span // 4 + 1, body, start)
        for kv in range(KV):
            unstack_heads(dq_ref, s, kv, (final[kv] * SCALE).T)

    def put(i, carry):
        rows = pl.ds(pl.multiple_of(i * 256, 256), 256)
        dkv_ref[rows, :] = acc_ref[rows, :].astype(BF)
        return carry

    lax.fori_loop(0, acc_ref.shape[0] // 256, put, 0)


def attend_back(where, spans, query, keys_values, d_attended, attended, lse):
    smem = pl.BlockSpec(memory_space=pltpu.SMEM)
    vmem = pl.BlockSpec(memory_space=pltpu.VMEM)
    length = keys_values.shape[0]
    return pl.pallas_call(
        attend_back_kernel,
        out_shape=[
            jax.ShapeDtypeStruct((ROWS, H * HD), F32),
            jax.ShapeDtypeStruct((length, 2 * KV * HD), BF),
        ],
        in_specs=[smem, smem] + [vmem] * 5,
        out_specs=[vmem, vmem],
        scratch_shapes=[pltpu.VMEM((length, 2 * KV * HD), F32)],
        compiler_params=pltpu.CompilerParams(vmem_limit_bytes=56 << 20),
        cost_estimate=pl.CostEstimate(flops=4_400_000_000, transcendentals=3_400_000, bytes_accessed=12 << 20),
        name="attend_back",
    )(where, spans, query, keys_values, d_attended, attended, lse)


def rms_norm(values, gain):
    return values * lax.rsqrt(jnp.mean(values * values, axis=-1, keepdims=True) + EPS) * gain


def norm_back(values, gain, grad):
    inv = lax.rsqrt(jnp.mean(values * values, axis=-1, keepdims=True) + EPS)
    scaled = gain * grad
    return inv * (scaled - values * (inv * inv) * jnp.mean(scaled * values, axis=-1, keepdims=True))


def angle_tables(position):
    half_size = HD // 2
    frequency = jnp.exp(-(jnp.arange(half_size, dtype=F32) * 2.0 / HD) * math.log(BASE))
    angles = position.astype(F32)[:, None] * frequency[None, :]
    cosine, sine = jnp.cos(angles), jnp.sin(angles)
    return (
        jnp.concatenate([cosine, cosine], axis=1)[:, None, :],
        jnp.concatenate([-sine, sine], axis=1)[:, None, :],
    )


def rotate(values, cosine, sine):
    half_size = HD // 2
    swapped = jnp.concatenate([values[..., half_size:], values[..., :half_size]], axis=-1)
    return values * cosine + swapped * sine


def split_low(values):
    high = values.astype(BF)
    return high, (values - high.astype(F32)).astype(BF)


def local(
    tokens,
    teacher,
    valid_mask,
    token_count,
    routes,
    span_order,
    w_query,
    w_key,
    w_value,
    w_out,
    norm_gain,
    w_router,
    moe_gain,
    w_gate,
    w_up,
    w_down,
):
    inputs = tokens[0].astype(F32)
    ctx = lax.axis_index("ctx")
    shard = lax.axis_index("fsdp")
    spans = lax.dynamic_slice(span_order, (ctx * 2,), (2,))
    where = jnp.sum(
        jnp.where(
            span_order[None, :] == jnp.arange(2 * 32, dtype=jnp.int32)[:, None],
            jnp.arange(2 * 32, dtype=jnp.int32)[None, :],
            0,
        ),
        axis=1,
    )
    position = (spans[:, None] * SPAN + jnp.arange(SPAN, dtype=jnp.int32)[None, :]).reshape(ROWS)
    cosine, sine = angle_tables(position)

    small = jnp.concatenate(
        [norm_gain[:, None], moe_gain[:, None], w_router, jnp.zeros((SHARD, HD - 2 - E), BF)], axis=1
    )
    full_query, full_key, full_value, full_out, small_all = gather_attention_weights(
        (w_query, w_key, w_value, w_out, small), 1
    )
    gain_first = small_all[:, 0].astype(F32)
    gain_second = small_all[:, 1].astype(F32)
    full_router = small_all[:, 2 : 2 + E]

    input_one = rms_norm(inputs, gain_first).astype(BF)
    query_raw = jnp.dot(input_one, full_query, preferred_element_type=F32)
    key_raw = jnp.dot(input_one, full_key, preferred_element_type=F32)
    value_raw = jnp.dot(input_one, full_value, preferred_element_type=F32)
    query = rotate(query_raw.reshape(ROWS, H, HD), cosine, sine).astype(BF).reshape(ROWS, H * HD)
    key_rot = rotate(key_raw.reshape(ROWS, KV, HD), cosine, sine).astype(BF).reshape(ROWS, KV * HD)
    keys_values = jnp.concatenate([key_rot, value_raw.astype(BF)], axis=1)
    whole = gather_keys(keys_values, 2).reshape(32 * ROWS, 2 * KV * HD)
    attended, lse = attend(where, spans, query, whole)
    attended_low = attended.astype(BF)
    hidden = inputs + jnp.dot(attended_low, full_out, preferred_element_type=F32)

    wide, low = gather_expert_weights(w_gate, w_up, w_down, 3)
    input_two = rms_norm(hidden, gain_second).astype(BF)
    expert_ids = jnp.arange(E, dtype=jnp.int32)
    selected = jnp.sum((routes[0][:, :, None] == expert_ids[None, None, :]).astype(F32), axis=1)
    router_logits = jnp.dot(input_two, full_router, preferred_element_type=F32)
    router_probs = jax.nn.softmax(router_logits, axis=-1)
    gate_weights = router_probs * selected
    gates_high, gates_low = split_low(gate_weights)
    gates_sent = jnp.concatenate([gates_high, gates_low, jnp.zeros((ROWS, HD - 2 * E), BF)], axis=1)
    group_two, gates_all = group_gather((input_two, gates_sent), 4, "group_normed")
    group_two = group_two.reshape(4 * ROWS, D)
    gates_all = gates_all.reshape(4 * ROWS, HD).astype(F32)
    gates_all = gates_all[:, :E] + gates_all[:, E : 2 * E]
    experts_here = (shard * 3 + jnp.arange(3, dtype=jnp.int32)) // 2
    pick = (experts_here[:, None] == expert_ids[None, :]).astype(F32)
    gates_here = jnp.sum(gates_all[:, None, :] * pick[None, :, :], axis=-1)
    gates_wide = jnp.repeat(gates_here, HALF, axis=1)

    raw = jnp.dot(group_two, wide, preferred_element_type=F32)
    gate_raw, up_raw = raw[:, :SLICE], raw[:, SLICE:]
    activated, gelu_pull = jax.vjp(lambda argument: jax.nn.gelu(argument, approximate=True), gate_raw)
    expert_hidden = activated * up_raw
    weighted = (gates_wide * expert_hidden).astype(BF)
    mixed = jnp.dot(weighted, low, preferred_element_type=F32).astype(BF).reshape(4, ROWS, D)
    (mixed_parts,) = group_swap((mixed,), 5, "group_mixture")
    result = hidden + jnp.sum(mixed_parts.astype(F32), axis=0)

    target = teacher[0].astype(F32)
    valid_rows = valid_mask[0].astype(F32)[:, None]
    error_rows = result - target
    squared_total = lax.psum(jnp.sum(valid_rows * error_rows * error_rows), ("ctx", "fsdp"))
    norm_factor = token_count[0].astype(F32) * D
    loss_value = (squared_total / norm_factor).reshape(1)
    d_result = 2.0 * valid_rows * error_rows / norm_factor
    (group_d,) = group_gather((d_result.astype(BF),), 6, "group_d_result")
    group_d = group_d.reshape(4 * ROWS, D)
    back = lax.dot_general(group_d, low, (((1,), (1,)), ((), ())), preferred_element_type=F32)
    d_gates_here = jnp.sum((expert_hidden * back).reshape(4 * ROWS, 3, HALF), axis=-1)
    d_gates_part = jnp.sum(d_gates_here[:, :, None] * pick[None, :, :], axis=1)
    d_expert_hidden = gates_wide * back
    d_gate = gelu_pull(d_expert_hidden * up_raw)[0].astype(BF)
    d_up = (d_expert_hidden * activated).astype(BF)
    d_raw = jnp.concatenate([d_gate, d_up], axis=1)
    d_two = lax.dot_general(d_raw, wide, (((1,), (1,)), ((), ())), preferred_element_type=F32)
    gates_high, gates_low = split_low(d_gates_part)
    d_gates_sent = jnp.concatenate([gates_high, gates_low, jnp.zeros((4 * ROWS, HD - 2 * E), BF)], axis=1)
    two_parts, d_gates_parts = group_swap(
        (d_two.astype(BF).reshape(4, ROWS, D), d_gates_sent.reshape(4, ROWS, HD)), 7, "group_d_normed"
    )
    d_gates_parts = jnp.sum(d_gates_parts.astype(F32), axis=0)
    d_select = (d_gates_parts[:, :E] + d_gates_parts[:, E : 2 * E]) * selected
    d_router = (
        router_probs * (d_select - jnp.sum(router_probs * d_select, axis=-1, keepdims=True))
    ).astype(BF)
    d_normed_two = jnp.sum(two_parts.astype(F32), axis=0) + jnp.dot(
        d_router, full_router.T, preferred_element_type=F32
    )
    d_hidden = d_result + norm_back(hidden, gain_second, d_normed_two)
    d_attn = d_hidden.astype(BF)

    d_attn_blocks = jnp.stack([d_attn[:, f * SHARD : (f + 1) * SHARD] for f in range(4)])
    group_attended, group_one = group_gather((attended_low, input_one), 8, "group_attended")
    (group_d_attn,) = group_swap((d_attn_blocks,), 9, "group_d_attn")
    group_one = group_one.reshape(4 * ROWS, D)
    grad_wide = tn(group_two, d_raw)
    grad_low = tn(group_d, weighted)
    grad_out = tn(group_attended.reshape(4 * ROWS, D), group_d_attn.reshape(4 * ROWS, SHARD))
    grad_router = tn(input_two, jnp.pad(d_router, ((0, 0), (0, 256 - E))))
    grads = jnp.concatenate(
        [grad_wide.astype(BF), grad_low.astype(BF), grad_out.astype(BF), grad_router.astype(BF)], axis=1
    ).reshape(4, SHARD, 4096)
    grads = reduce_grads(grads, 10, "grads")

    d_attended = lax.dot_general(d_attn, full_out, (((1,), (1,)), ((), ())), preferred_element_type=F32).astype(BF)
    d_query, d_whole = attend_back(where, spans, query, whole, d_attended, attended, lse)
    d_key, d_value = reduce_keys(d_whole.reshape(4, 4, 2, ROWS, 2 * KV * HD), 15)
    d_query_raw = rotate(d_query.reshape(ROWS, H, HD), cosine, -sine).reshape(ROWS, H * HD)
    d_key_raw = rotate(d_key.reshape(ROWS, KV, HD), cosine, -sine).reshape(ROWS, KV * HD)
    d_query_raw, d_key_raw, d_value_raw = (part.astype(BF) for part in (d_query_raw, d_key_raw, d_value))
    d_normed_one = lax.dot_general(d_query_raw, full_query, (((1,), (1,)), ((), ())), preferred_element_type=F32)
    d_normed_one = d_normed_one + lax.dot_general(
        d_key_raw, full_key, (((1,), (1,)), ((), ())), preferred_element_type=F32
    )
    d_normed_one = d_normed_one + lax.dot_general(
        d_value_raw, full_value, (((1,), (1,)), ((), ())), preferred_element_type=F32
    )
    d_inputs = d_hidden + norm_back(inputs, gain_first, d_normed_one)
    d_qkv = jnp.concatenate([d_query_raw, d_key_raw, d_value_raw], axis=1)
    d_qkv_blocks = jnp.stack([d_qkv[:, f * 512 : (f + 1) * 512] for f in range(4)])
    (group_d_qkv,) = group_swap((d_qkv_blocks,), 18, "group_d_qkv")
    grad_qkv = tn(group_one, group_d_qkv.reshape(4 * ROWS, 512)).astype(BF).reshape(4, SHARD, 512)
    grad_qkv = reduce_grads(grad_qkv, 19, "qkv")

    def halves(columns):
        cut = columns.reshape(4, SHARD, 3, HALF).transpose(0, 2, 1, 3).reshape(E, 2, SHARD, HALF)
        return cut.transpose(0, 2, 1, 3).reshape(E, SHARD, FF).astype(F32)

    grad_gate = halves(grads[:, :, :SLICE])
    grad_up = halves(grads[:, :, SLICE : 2 * SLICE])
    grad_down = halves(grads[:, :, 2 * SLICE : 3 * SLICE]).transpose(0, 2, 1)
    grad_out = grads[:, :, 3 * SLICE : 3 * SLICE + SHARD].transpose(1, 0, 2).reshape(SHARD, D).astype(F32)
    grad_router = jnp.sum(grads[:, :, 3 * SLICE + SHARD : 3 * SLICE + SHARD + E].astype(F32), axis=0)
    grad_qkv = grad_qkv.transpose(1, 0, 2).reshape(SHARD, QKV).astype(F32)
    grad_query, grad_key, grad_value = grad_qkv[:, :D], grad_qkv[:, D : D + 256], grad_qkv[:, D + 256 :]

    grad_gain_one = (
        jnp.sum(w_query.astype(F32) * grad_query, axis=1)
        + jnp.sum(w_key.astype(F32) * grad_key, axis=1)
        + jnp.sum(w_value.astype(F32) * grad_value, axis=1)
    ) / norm_gain.astype(F32)
    grad_gain_two = (
        jnp.sum(w_gate.astype(F32) * grad_gate + w_up.astype(F32) * grad_up, axis=(0, 2))
        + jnp.sum(w_router.astype(F32) * grad_router, axis=1)
    ) / moe_gain.astype(F32)
    return (
        result.astype(BF)[None],
        loss_value,
        d_inputs[None],
        grad_query,
        grad_key,
        grad_value,
        grad_out,
        grad_gain_one,
        grad_router,
        grad_gain_two,
        grad_gate,
        grad_up,
        grad_down,
    )


def solution(mesh):
    in_specs = (
        P("fsdp", "ctx", None),
        P("fsdp", "ctx", None),
        P("fsdp", "ctx"),
        P(),
        P("fsdp", "ctx", None),
        P(),
        P("fsdp", None),
        P("fsdp", None),
        P("fsdp", None),
        P("fsdp", None),
        P("fsdp"),
        P("fsdp", None),
        P("fsdp"),
        P(None, "fsdp", None),
        P(None, "fsdp", None),
        P(None, None, "fsdp"),
    )
    out_specs = (
        P("fsdp", "ctx", None),
        P(),
        P("fsdp", "ctx", None),
        P("fsdp", None),
        P("fsdp", None),
        P("fsdp", None),
        P("fsdp", None),
        P("fsdp"),
        P("fsdp", None),
        P("fsdp"),
        P(None, "fsdp", None),
        P(None, "fsdp", None),
        P(None, None, "fsdp"),
    )
    return jax.shard_map(local, mesh=mesh, in_specs=in_specs, out_specs=out_specs, check_vma=False)
```

```python
import math

import jax
import jax.numpy as jnp
from jax import lax
from jax.experimental import pallas as pl
from jax.experimental.pallas import tpu as pltpu
from jax.sharding import PartitionSpec as P

H = 12
KV = 2
HD = 128
E = 6
D = 1536
FF = 768
GROUPS = H // KV
ROWS = 128
SPAN = 64
HALF = 384
SLICE = 3 * HALF
QKV = 2048
SHARD = 384
WIDE = 3 * SLICE + 128
TAIL = 1024
PART = SHARD // 2
STRIP = PART // 4
EPS = 1e-06
BASE = 1000000.0
NEGATIVE = -1e30
SCALE = HD**-0.5
MESH = pl.DeviceIdType.MESH
BF = jnp.bfloat16
F32 = jnp.float32


def place():
    ctx = lax.axis_index("ctx")
    shard = lax.axis_index("fsdp")
    return ctx // 8, (ctx // 2) % 4, ctx % 2, shard // 2, shard % 2


def device(x, z, y_lo, y_hi, core):
    return (x * 8 + z * 2 + y_lo, y_hi * 2 + core)


def x_peers(at):
    x, z, y_lo, y_hi, core = at
    return [device((x + k) % 4, z, y_lo, y_hi, core) for k in (1, 2, 3)]


def z_peers(at):
    x, z, y_lo, y_hi, core = at
    return [device(x, (z + k) % 4, y_lo, y_hi, core) for k in (1, 2, 3)]


def group_member(at, shard_hi, core):
    x, z, y_lo, y_hi, _ = at
    y_lo_there = (y_lo + y_hi + shard_hi) % 2
    return device(x, z, y_lo_there, shard_hi, core)


class Net:
    def __init__(self, send_sem, recv_sem, local_sem, stage):
        self.sems = (send_sem, recv_sem, local_sem)
        self.stage = stage
        self.remote = 0
        self.loads = []
        self.kept = 0
        self.open = {}
        self.copies = []

    def greet(self, peers):
        barrier = pltpu.get_barrier_semaphore()
        for peer in peers:
            pl.semaphore_signal(barrier, inc=1, device_id=peer, device_id_type=MESH)
        pl.semaphore_wait(barrier, len(peers))

    def _open(self, copy):
        copy.start()
        self.open[id(copy)] = copy.wait
        self.copies.append(copy)
        return copy

    def send(self, src, dst, peer):
        slot = self.remote
        self.remote += 1
        return self._open(
            pltpu.make_async_remote_copy(
                src_ref=src,
                dst_ref=dst,
                send_sem=self.sems[0].at[slot],
                recv_sem=self.sems[1].at[slot],
                device_id=peer,
                device_id_type=MESH,
            )
        )

    def keep(self, src, dst):
        slot = self.kept
        self.kept += 1
        load = pltpu.make_async_copy(src, self.stage[slot], self.sems[2].at[slot])
        load.start()
        self.loads.append((load, slot, dst))

    def settle(self):
        stores = []
        for load, slot, dst in self.loads:
            load.wait()
            stores.append(self._open(pltpu.make_async_copy(self.stage[slot], dst, self.sems[2].at[slot])))
        self.loads = []
        return stores

    def done(self, copies):
        for copy in copies:
            copy.wait()
            del self.open[id(copy)]

    def arrived(self, copy):
        copy.wait_recv()
        self.open[id(copy)] = copy.wait_send

    def finish(self):
        self.settle()
        for wait in self.open.values():
            wait()


def exchange(body, inputs, outs, remote, keeps, number, name, scratch=()):
    count = len(inputs)
    total = count + len(outs)

    def kernel(*refs):
        net = Net(*refs[total : total + 3], refs[total + 3 :])
        body(net, refs[:count], refs[count:total])
        net.finish()

    any_spec = pl.BlockSpec(memory_space=pl.ANY)
    return pl.pallas_call(
        kernel,
        out_shape=[jax.ShapeDtypeStruct(shape, kind) for shape, kind in outs],
        in_specs=[any_spec] * count,
        out_specs=[any_spec] * len(outs),
        scratch_shapes=[
            pltpu.SemaphoreType.DMA((remote,)),
            pltpu.SemaphoreType.DMA((remote,)),
            pltpu.SemaphoreType.DMA((len(keeps) + len(scratch) + 1,)),
        ]
        + [pltpu.VMEM(shape, kind) for shape, kind in list(keeps) + list(scratch)],
        compiler_params=pltpu.CompilerParams(
            collective_id=number, has_side_effects=True, vmem_limit_bytes=60 << 20
        ),
        name=name,
    )(*inputs)


def ring_of(at):
    x, z, y_lo, y_hi, core = at
    return [
        device(
            lax.select(core == 0, (x + k) % 4, x), lax.select(core == 0, z, (z + k) % 4), y_lo, y_hi, core
        )
        for k in (1, 2, 3)
    ]


def gather_attention_weights(parts, small, number):
    count = len(parts)

    def body(net, ins, outs):
        at = place()
        x, z, y_lo, y_hi, core = at
        shard = y_hi * 2 + core
        sibling = device(x, z, y_lo, y_hi, 1 - core)
        partner = device(x, z, 1 - y_lo, 1 - y_hi, core)
        crossed = device(x, z, 1 - y_lo, 1 - y_hi, 1 - core)
        here = lax.select(core == 0, x, z)
        ring = ring_of(at)
        net.greet([sibling, partner, crossed] + ring)
        small_spot = outs[count].at[:, pl.ds(pl.multiple_of(shard * SHARD, 128), SHARD)]
        for peer in (partner, crossed, sibling):
            net.send(ins[count], small_spot, peer)

        def block(array, owner, start, size):
            width = ins[array].shape[1]
            return outs[array].at[pl.ds(pl.multiple_of(owner * SHARD + start, 32), size), pl.ds(0, width)]

        quarter = SHARD // 4
        first = []
        for a in range(count):
            rows = pl.ds(pl.multiple_of(here * quarter, 32), quarter)
            first.append(net.send(ins[a].at[rows, :], block(a, shard, here * quarter, quarter), partner))
        for a in range(count):
            net.send(ins[a], block(a, shard, 0, SHARD), sibling)
            net.keep(ins[a], block(a, shard, 0, SHARD))
        net.keep(ins[count], small_spot)
        net.settle()
        far = (1 - y_hi) * 2 + core
        around = []
        for a in range(count):
            net.arrived(first[a])
            mine = block(a, far, here * quarter, quarter)
            around.append([net.send(mine, mine, peer) for peer in ring])
            net.send(mine, mine, sibling)
        for k in (1, 3, 2):
            origin = (here + 4 - k) % 4
            for a in range(count):
                net.arrived(around[a][k - 1])
                piece = block(a, far, origin * quarter, quarter)
                net.send(piece, piece, sibling)

    return exchange(
        body,
        tuple(parts) + (small,),
        [((D, part.shape[1]), BF) for part in parts] + [((16, D), BF)],
        count * 9 + 3,
        [(part.shape, BF) for part in parts] + [((16, SHARD), BF)],
        number,
        "attention_weights",
    )


class ExpertWeights:
    quarter = HALF // 4
    cells = [(h, kind) for h in range(3) for kind in range(3)]

    def source(self, ins, owner, h, kind, start, size):
        index = owner * 3 + h
        expert = index // 2
        offset = pl.multiple_of((index % 2) * HALF, 128)
        if kind < 2:
            return ins[kind].at[expert, pl.ds(start, size), pl.ds(offset, HALF)]
        return ins[2].at[expert, pl.ds(pl.multiple_of(offset + start, 32), size), :]

    def target(self, outs, from_shard, h, kind, start, size):
        if kind < 2:
            rows = pl.multiple_of(from_shard * SHARD + start, 32)
            return outs[0].at[pl.ds(rows, size), pl.ds(kind * SLICE + h * HALF, HALF)]
        columns = pl.multiple_of(from_shard * SHARD, 128)
        return outs[1].at[pl.ds(pl.multiple_of(h * HALF + start, 32), size), pl.ds(columns, SHARD)]

    def cross(self, net, ins, quarters, at):
        x, z, y_lo, y_hi, core = at
        for step in (0, 1):
            far_core = (core + step) % 2
            start = pl.multiple_of(lax.select(far_core == 0, x, z) * self.quarter, 32)
            owner = (1 - y_hi) * 2 + far_core
            peer = device(x, z, 1 - y_lo, 1 - y_hi, far_core)
            for n, (h, kind) in enumerate(self.cells):
                net.send(self.source(ins, owner, h, kind, start, self.quarter), quarters.at[step, n], peer)

    def around(self, net, ins, quarters, outs, at):
        x, z, y_lo, y_hi, core = at
        shard = y_hi * 2 + core
        sibling = device(x, z, y_lo, y_hi, 1 - core)
        here = pl.multiple_of(lax.select(core == 0, x, z) * self.quarter, 32)
        for step in (0, 1):
            from_shard = (1 - y_hi) * 2 + (core + step) % 2
            for n, (h, kind) in enumerate(self.cells):
                spot = self.target(outs, from_shard, h, kind, here, self.quarter)
                for peer in ring_of(at):
                    net.send(quarters.at[step, n], spot, peer)
                net.keep(quarters.at[step, n], spot)
        for h, kind in self.cells:
            other = y_hi * 2 + 1 - core
            net.send(self.source(ins, other, h, kind, 0, HALF), self.target(outs, shard, h, kind, 0, HALF), sibling)
            net.keep(self.source(ins, shard, h, kind, 0, HALF), self.target(outs, shard, h, kind, 0, HALF))


EXPERT = ExpertWeights()


def gather_keys(local, experts, number):
    def body(net, ins, outs):
        mine, whole = ins[0], outs[0]
        at = place()
        x, z, y_lo, y_hi, core = at
        partner = device(x, z, 1 - y_lo, y_hi, core)
        peers = (x_peers(at), z_peers(at))
        across = [device(x, z, 1 - y_lo, 1 - y_hi, c) for c in (0, 1)]
        net.greet([partner] + peers[0] + peers[1] + across)
        spot = whole.at[x, z, y_lo]
        near = net.send(mine, spot, partner)
        net.keep(mine, spot)
        EXPERT.cross(net, ins[1:], outs[1], at)
        net.done(net.settle())
        net.arrived(near)
        half = KV * HD
        order = (1, 0)
        stage = []
        for part in (0, 1):
            block = whole.at[x, z, :, :, pl.ds(part * half, half)]
            stage.append([net.send(block, block, peer) for peer in peers[order[part]]])
        for part in (0, 1):
            for copy in stage[part]:
                net.arrived(copy)
            if part == 0:
                block = whole.at[x, :, :, :, pl.ds(0, half)]
            else:
                block = whole.at[:, z, :, :, pl.ds(half, half)]
            for peer in (peers[part][1], peers[part][0], peers[part][2]):
                net.send(block, block, peer)

    return exchange(
        body,
        (local,) + experts,
        [((4, 4, 2, ROWS, 2 * KV * HD), BF), ((2, 9, EXPERT.quarter, HALF), BF)],
        13 + 18,
        [((ROWS, 2 * KV * HD), BF)],
        number,
        "keys_values",
    )


def group_places(at):
    x, z, y_lo, y_hi, core = at
    sibling = device(x, z, y_lo, y_hi, 1 - core)
    partner = device(x, z, 1 - y_lo, 1 - y_hi, core)
    return sibling, partner


class Spread:
    def start(self, net, mine, whole, at):
        sibling, partner = group_places(at)
        spot = whole.at[at[3] * 2 + at[4]]
        self.copy = net.send(mine, spot, partner)
        net.send(mine, spot, sibling)
        net.keep(mine, spot)

    def forward(self, net, whole, at):
        sibling, partner = group_places(at)
        net.arrived(self.copy)
        far = whole.at[(1 - at[3]) * 2 + at[4]]
        net.send(far, far, sibling)


def group_spread(parts, number, name, weights=None):
    count = len(parts)
    keeps = [(part.shape, part.dtype) for part in parts]
    outs = [((4,) + part.shape, part.dtype) for part in parts]
    inputs = tuple(parts)
    remote = 3 * count
    if weights is not None:
        inputs += weights
        outs += [((D, 2 * SLICE), BF), ((SLICE, D), BF)]
        remote += 7 * 9
        keeps += [((EXPERT.quarter, HALF), BF)] * 18 + [((HALF, HALF), BF)] * 9

    def body(net, ins, outs):
        at = place()
        sibling, partner = group_places(at)
        net.greet([sibling, partner] + (ring_of(at) if weights is not None else []))
        spreads = [Spread() for _ in range(count)]
        for one, mine, whole in zip(spreads, ins, outs):
            one.start(net, mine, whole, at)
        if weights is not None:
            EXPERT.around(net, ins[count:-1], ins[-1], outs[count:], at)
        net.settle()
        for one, whole in zip(spreads, outs):
            one.forward(net, whole, at)

    return exchange(body, inputs, outs, remote, keeps, number, name)


def group_sum(parts, number, name, extra=None):
    count = len(parts)
    spread = () if extra is None else (extra,)
    keeps = [(part.shape[1:], BF) for part in parts] + [(one.shape, one.dtype) for one in spread]
    outs = [((3,) + part.shape[1:], BF) for part in parts] + [((4,) + one.shape, one.dtype) for one in spread]
    scratch = [((2,) + part.shape[1:], BF) for part in parts]

    def body(net, ins, outs):
        at = place()
        x, z, y_lo, y_hi, core = at
        sibling, partner = group_places(at)
        net.greet([sibling, partner])
        sums = net.stage[len(keeps) :]
        far = (1 - y_hi) * 2
        came, own = [], []
        for mine, pair in zip(ins, sums):
            came.append(net.send(mine.at[far + 1 - core], pair.at[1], sibling))
            load = pltpu.make_async_copy(mine.at[far + core], pair.at[0], net.sems[2].at[len(keeps) + len(own)])
            load.start()
            own.append(load)
        for mine, got in zip(ins[:count], outs):
            net.send(mine.at[y_hi * 2 + 1 - core], got.at[1], sibling)
            net.keep(mine.at[y_hi * 2 + core], got.at[0])
        spreads = []
        for mine, whole in zip(ins[count:], outs[count:]):
            spreads.append(Spread())
            spreads[-1].start(net, mine, whole, at)
        for n, pair in enumerate(sums):
            own[n].wait()
            net.arrived(came[n])

            def add(step, carry):
                rows = pl.ds(pl.multiple_of(step * 16, 16), 16)
                pair[0, rows, :] = (pair[0, rows, :].astype(F32) + pair[1, rows, :].astype(F32)).astype(BF)
                return carry

            lax.fori_loop(0, pair.shape[1] // 16, add, 0)
            net.send(pair.at[0], outs[n].at[2], partner)
        net.settle()
        for one, whole in zip(spreads, outs[count:]):
            one.forward(net, whole, at)

    return exchange(
        body, tuple(parts) + spread, outs, 3 * (count + len(spread)), keeps, number, name, scratch
    )


def add_up(pieces, axis):
    return jnp.sum(pieces.astype(F32), axis=axis).astype(BF)


class KeySum:
    half = KV * HD
    shapes = (
        ((2, 4, 4, 2, ROWS, KV * HD), BF),
        ((2, 4, 2, ROWS, KV * HD), BF),
        ((2, 2, ROWS, KV * HD), BF),
    )
    keeps = (
        [((4, 2, ROWS, KV * HD), BF)] * 2,
        [((2, ROWS, KV * HD), BF)] * 2,
        [((2, ROWS, KV * HD), BF)],
    )

    def first(self, net, whole, got, at):
        x, z = at[0], at[1]
        half = self.half
        peers = (x_peers(at), z_peers(at))
        for k in (2, 1, 3):
            net.send(whole.at[(x + k) % 4, :, :, :, pl.ds(0, half)], got.at[0, k], peers[0][k - 1])
            net.send(whole.at[:, (z + k) % 4, :, :, pl.ds(half, half)], got.at[1, k], peers[1][k - 1])
        net.keep(whole.at[x, :, :, :, pl.ds(0, half)], got.at[0, 0])
        net.keep(whole.at[:, z, :, :, pl.ds(half, half)], got.at[1, 0])

    def second(self, net, whole, got, at):
        x, z = at[0], at[1]
        peers = (x_peers(at), z_peers(at))
        for k in (2, 1, 3):
            net.send(whole.at[0, (z + k) % 4], got.at[0, k], peers[1][k - 1])
            net.send(whole.at[1, (x + k) % 4], got.at[1, k], peers[0][k - 1])
        net.keep(whole.at[0, z], got.at[0, 0])
        net.keep(whole.at[1, x], got.at[1, 0])

    def third(self, net, whole, got, at):
        x, z, y_lo, y_hi, core = at
        net.send(whole.at[:, 1 - y_lo], got.at[1], device(x, z, 1 - y_lo, y_hi, core))
        net.keep(whole.at[:, y_lo], got.at[0])


class GradSum:
    def __init__(self, columns):
        self.columns, self.cell = columns, columns // 4
        self.shapes = (
            ((2, 4, 4, STRIP, columns), BF),
            ((2, 4, 4, STRIP, self.cell), BF),
            ((2, 2, 2, STRIP, self.cell), BF),
        )
        self.keeps = (
            [((4, STRIP, columns), BF)] * 2,
            [((4, STRIP, self.cell), BF)] * 2,
            [((2, STRIP, self.cell), BF)],
        )

    def first(self, net, whole, got, at):
        own = (at[0], at[1])
        peers = (x_peers(at), z_peers(at))
        for k in (2, 1, 3, 0):
            for part in (0, 1):
                start = part * PART + ((own[part] + k) % 4) * STRIP
                block = whole.at[:, pl.ds(pl.multiple_of(start, 16), STRIP), :]
                if k == 0:
                    net.keep(block, got.at[part, 0])
                else:
                    net.send(block, got.at[part, k], peers[part][k - 1])

    def second(self, net, whole, got, at):
        own = (at[1], at[0])
        peers = (z_peers(at), x_peers(at))
        for k in (2, 1, 3, 0):
            for part in (0, 1):
                start = ((own[part] + k) % 4) * self.cell
                block = whole.at[part, :, :, pl.ds(pl.multiple_of(start, 128), self.cell)]
                if k == 0:
                    net.keep(block, got.at[part, 0])
                else:
                    net.send(block, got.at[part, k], peers[part][k - 1])

    def third(self, net, whole, got, at):
        x, z, y_lo, y_hi, core = at
        for k in (1, 2, 3):
            hi, low = k // 2, k % 2
            there_hi, there_core = (y_lo + hi) % 2, (core + low) % 2
            shard = there_hi * 2 + there_core
            net.send(whole.at[:, shard], got.at[y_lo, core], device(x, z, y_hi, there_hi, there_core))
        mine = whole.at[:, y_lo * 2 + core]
        spot = got.at[y_lo, core]
        slot, held = net.remote, net.kept
        net.remote += 1
        net.kept += 1
        stage, sem = net.stage[held], net.sems[2].at[held]

        @pl.when(y_lo == y_hi)
        def _():
            load = pltpu.make_async_copy(mine, stage, sem)
            load.start()
            load.wait()
            store = pltpu.make_async_copy(stage, spot, sem)
            store.start()
            store.wait()

        @pl.when(y_lo != y_hi)
        def _():
            copy = pltpu.make_async_remote_copy(
                src_ref=mine,
                dst_ref=spot,
                send_sem=net.sems[0].at[slot],
                recv_sem=net.sems[1].at[slot],
                device_id=device(x, z, y_hi, y_lo, core),
                device_id_type=MESH,
            )
            copy.start()
            copy.wait()


class LossSum:
    shapes = (((4, 8, 128), F32), ((4, 8, 128), F32), ((2, 8, 128), F32))
    keeps = ([((8, 128), F32)],) * 3

    def first(self, net, whole, got, at):
        for peer in x_peers(at):
            net.send(whole, got.at[at[0]], peer)
        net.keep(whole, got.at[at[0]])

    def second(self, net, whole, got, at):
        for peer in z_peers(at):
            net.send(whole, got.at[at[1]], peer)
        net.keep(whole, got.at[at[1]])

    def third(self, net, whole, got, at):
        x, z, y_lo, y_hi, core = at
        net.send(whole, got.at[y_lo], device(x, z, 1 - y_lo, y_hi, core))
        net.keep(whole, got.at[y_lo])


class GroupShare:
    def __init__(self, spread, swapped):
        self.count = len(spread)
        self.inputs = tuple(spread) + tuple(swapped)
        self.outs = [((4,) + one.shape, BF) for one in spread] + [(one.shape, BF) for one in swapped]
        self.keeps = [(one.shape, BF) for one in spread] + [(one.shape[1:], BF) for one in swapped]

    def peers(self, at):
        x, z, y_lo, y_hi, core = at
        return [device(x, z, 1 - y_lo, 1 - y_hi, 1 - core), *group_places(at)]

    def start(self, net, ins, outs, at):
        x, z, y_lo, y_hi, core = at
        crossed, sibling, partner = self.peers(at)
        shard = y_hi * 2 + core
        far = (1 - y_hi) * 2
        for mine, whole in zip(ins[self.count :], outs[self.count :]):
            net.send(mine.at[far + core], whole.at[shard], partner)
            net.send(mine.at[far + 1 - core], whole.at[shard], crossed)
            net.send(mine.at[y_hi * 2 + 1 - core], whole.at[shard], sibling)
        self.spreads = []
        for mine, whole in zip(ins, outs[: self.count]):
            self.spreads.append(Spread())
            self.spreads[-1].start(net, mine, whole, at)
        for mine, whole in zip(ins[self.count :], outs[self.count :]):
            net.keep(mine.at[shard], whole.at[shard])

    def forward(self, net, outs, at):
        for one, whole in zip(self.spreads, outs):
            one.forward(net, whole, at)


def sum_step(sums, arrays, step, number, name, share=None):
    count = len(sums)

    def body(net, ins, outs):
        at = place()
        if step < 2:
            net.greet(x_peers(at) + z_peers(at) + (share.peers(at) if share else []))
        else:
            x, z, y_lo, y_hi, core = at
            net.greet(
                [
                    device(x, z, (y_lo + k // 4) % 2, (y_hi + (k // 2) % 2) % 2, (core + k) % 2)
                    for k in range(1, 8)
                ]
            )
        for one, whole, got in zip(sums, ins, outs):
            (one.first, one.second, one.third)[step](net, whole, got, at)
        if share:
            share.start(net, ins[count:], outs[count:], at)
        net.settle()
        if share:
            share.forward(net, outs[count:], at)

    came = exchange(
        body,
        tuple(arrays) + (share.inputs if share else ()),
        [one.shapes[step] for one in sums] + (share.outs if share else []),
        6 * count + (3 * len(share.inputs) if share else 0),
        [keep for one in sums for keep in one.keeps[step]] + (share.keeps if share else []),
        number,
        name,
    )
    total = []
    for one, got in zip(sums, came):
        if isinstance(one, LossSum):
            total.append(jnp.sum(got, axis=0))
        else:
            total.append(add_up(got, 1 if step < 2 else 0))
    return total + list(came[count:])


def gather_grads(piece, columns, split, number, name, swapped=None):
    cell = columns // 4
    share = GroupShare((), (swapped,)) if swapped is not None else None
    outs = [((4, STRIP, columns), BF)] * 2 if split else [((4, SHARD, columns), BF)]

    def body(net, ins, outs):
        mine = ins[0]
        at = place()
        x, z, y_lo, y_hi, core = at
        partner = device(x, z, 1 - y_lo, y_hi, core)
        peers = (x_peers(at), z_peers(at))
        net.greet([partner] + peers[0] + peers[1] + (share.peers(at) if share else []))
        coordinates = ((x, z), (z, x))

        def strip(part, sets, j):
            cut = slice(None) if j is None else pl.ds(pl.multiple_of(j * cell, 128), cell)
            if split:
                return outs[part].at[sets, :, cut]
            start = pl.multiple_of(part * PART + coordinates[part][0] * STRIP, 16)
            return outs[0].at[sets, pl.ds(start, STRIP), cut]

        near = []
        for part in (0, 1):
            spot = strip(part, pl.ds(2 * y_lo, 2), coordinates[part][1])
            near.append(net.send(mine.at[:, part], spot, partner))
            net.keep(mine.at[:, part], spot)
        net.done(net.settle())
        if share:
            share.start(net, ins[1:], outs[-1:], at)
        stage = []
        for part in (0, 1):
            net.arrived(near[part])
            block = strip(part, slice(None), coordinates[part][1])
            stage.append([net.send(block, block, peer) for peer in peers[1 - part]])
        if split:
            return
        for part in (0, 1):
            for copy in stage[part]:
                net.arrived(copy)
            block = strip(part, slice(None), None)
            for peer in (peers[part][1], peers[part][0], peers[part][2]):
                net.send(block, block, peer)

    return exchange(
        body,
        (piece,) + (share.inputs if share else ()),
        outs + (share.outs if share else []),
        14 + (3 if share else 0),
        [((2, STRIP, cell), BF)] * 2 + (share.keeps if share else []),
        number,
        name,
    )


BLOCK = 4 * SPAN
QUERIES = GROUPS * SPAN
SMEM = pl.BlockSpec(memory_space=pltpu.SMEM)
VMEM = pl.BlockSpec(memory_space=pltpu.VMEM)
LOW = 32
FIRST = 2


def local_call(kernel, args, outs, name, flops, specs=None, out_specs=None, grid=None, scratch=(), limit=60):
    moved = sum(math.prod(arg.shape) * arg.dtype.itemsize for arg in args)
    moved += sum(math.prod(shape) * jnp.dtype(kind).itemsize for shape, kind in outs)
    extra = {} if grid is None else {"grid": grid}
    return pl.pallas_call(
        kernel,
        out_shape=[jax.ShapeDtypeStruct(shape, kind) for shape, kind in outs],
        in_specs=specs or [VMEM] * len(args),
        out_specs=out_specs or [VMEM] * len(outs),
        scratch_shapes=[pltpu.VMEM(shape, kind) for shape, kind in scratch],
        compiler_params=pltpu.CompilerParams(vmem_limit_bytes=limit << 20),
        cost_estimate=pl.CostEstimate(flops=flops // 1000, transcendentals=0, bytes_accessed=moved // 1000),
        name=name,
        **extra,
    )(*args)


def inverse_root(values):
    return lax.rsqrt(jnp.mean(values * values, axis=-1, keepdims=True) + EPS)


def norm_back(values, gain, grad):
    inv = inverse_root(values)
    scaled = gain * grad
    return inv * (scaled - values * (inv * inv) * jnp.mean(scaled * values, axis=-1, keepdims=True))


def turn(values, cosine, sine):
    return values * cosine + pltpu.roll(values, HD // 2, 1) * sine


def head(index):
    return slice(index * HD, (index + 1) * HD)


def stack_heads(ref, span, kv):
    rows = slice(span * SPAN, (span + 1) * SPAN)
    return jnp.concatenate([ref[rows, head(kv * GROUPS + g)] for g in range(GROUPS)], axis=0)


def unstack_heads(ref, span, kv, values):
    rows = slice(span * SPAN, (span + 1) * SPAN)
    for g in range(GROUPS):
        ref[rows, head(kv * GROUPS + g)] = values[g * SPAN : (g + 1) * SPAN, :]


def expert_lanes():
    return lax.broadcasted_iota(jnp.int32, (1, HD), 1)


def wide_router(small_ref):
    rows = small_ref[...]
    number = lax.broadcasted_iota(jnp.int32, rows.shape, 0)
    rows = jnp.where((number >= FIRST) & (number < FIRST + E), rows.astype(F32), 0.0).astype(BF)
    gap = jnp.zeros((16, D), BF)
    return jnp.concatenate([rows, gap, rows, gap, gap, gap, gap, gap], axis=0)


def chosen(routes):
    lanes = expert_lanes()
    number = jnp.where(lanes >= LOW, lanes - LOW, lanes) - FIRST
    total = jnp.zeros((ROWS, HD), F32)
    for slot in range(4):
        total = total + jnp.where(routes[:, slot : slot + 1] == number, 1.0, 0.0)
    return total


def in_two(values):
    high = values.astype(BF).astype(F32)
    return jnp.where(expert_lanes() < LOW, high, values - high).astype(BF)


def project_kernel(tokens, small, cosine, sine, w_query, w_key, w_value, normed, query, keys_values):
    inputs = tokens[...].astype(F32)
    gain = small[...].astype(F32)[0:1, :]
    normed[...] = (inputs * inverse_root(inputs) * gain).astype(BF)
    rows = normed[...]
    cos, sin = cosine[...], sine[...]
    raw = jnp.dot(rows, w_key[...], preferred_element_type=F32)
    for k in range(KV):
        keys_values[:, head(k)] = turn(raw[:, head(k)], cos, sin).astype(BF)
    keys_values[:, KV * HD :] = jnp.dot(rows, w_value[...], preferred_element_type=F32).astype(BF)
    for k in range(0, H, 4):
        raw = jnp.dot(rows, w_query[:, k * HD : (k + 4) * HD], preferred_element_type=F32)
        for j in range(4):
            query[:, head(k + j)] = turn(raw[:, head(j)], cos, sin).astype(BF)


def project(*args):
    outs = [((ROWS, D), BF), ((ROWS, H * HD), BF), ((ROWS, 2 * KV * HD), BF)]
    return local_call(project_kernel, args, outs, "project", 800_000_000)


def nt(a, b):
    return lax.dot_general(a, b, (((1,), (1,)), ((), ())), preferred_element_type=F32)


def tn(a, b):
    return lax.dot_general(a, b, (((0,), (0,)), ((), ())), preferred_element_type=F32)


def block_rows(where, b, ref):
    return jnp.concatenate(
        [ref[pl.ds(pl.multiple_of(where[b * 4 + i] * SPAN, SPAN), SPAN), :] for i in range(4)], axis=0
    )


def lead_of_keys():
    keys = lax.broadcasted_iota(jnp.int32, (BLOCK, QUERIES), 0)
    queries = lax.broadcasted_iota(jnp.int32, (BLOCK, QUERIES), 1)
    return keys - queries % SPAN


def attend_kernel(
    where, spans, q_ref, kv_ref, tokens, w_out, small, routes, o_ref, lse_ref, hidden_ref, normed_ref, gates_ref, probs_ref
):
    lead = lead_of_keys()
    for s in range(2):
        span = spans[s]
        stacked = [stack_heads(q_ref, s, kv) for kv in range(KV)]

        def body(b, carry):
            keys_values = block_rows(where, b, kv_ref)
            allowed = lead <= span * SPAN - b * BLOCK
            out = []
            for kv in range(KV):
                top, total, acc = carry[kv]
                keys = keys_values[:, head(kv)]
                values = keys_values[:, head(KV + kv)]
                logits = jnp.where(allowed, nt(keys, stacked[kv]) * SCALE, NEGATIVE)
                new_top = jnp.maximum(top, jnp.max(logits, axis=0, keepdims=True))
                weights = jnp.exp(logits - new_top)
                shrink = jnp.exp(top - new_top)
                total = total * shrink + jnp.sum(weights, axis=0, keepdims=True)
                acc = acc * shrink + tn(values, weights.astype(BF))
                out.append((new_top, total, acc))
            return tuple(out)

        start = tuple(
            (
                jnp.full((1, QUERIES), NEGATIVE, F32),
                jnp.zeros((1, QUERIES), F32),
                jnp.zeros((HD, QUERIES), F32),
            )
            for _ in range(KV)
        )
        final = lax.fori_loop(0, span // 4 + 1, body, start)
        for kv in range(KV):
            top, total, acc = final[kv]
            unstack_heads(o_ref, s, kv, (acc / total).T)
            lse_ref[2 * s + kv : 2 * s + kv + 1, :] = top + jnp.log(total)
    lse_ref[4:8, :] = jnp.zeros((4, QUERIES), F32)

    for start in range(0, D, 512):
        columns = slice(start, start + 512)
        hidden_ref[:, columns] = tokens[:, columns].astype(F32) + jnp.dot(
            o_ref[...].astype(BF), w_out[:, columns], preferred_element_type=F32
        )
    hidden = hidden_ref[...]
    gain = small[...].astype(F32)[1:2, :]
    normed = (hidden * inverse_root(hidden) * gain).astype(BF)
    normed_ref[...] = normed
    logits = nt(normed, wide_router(small))
    lanes = expert_lanes()
    first = (lanes >= FIRST) & (lanes < FIRST + E)
    second = (lanes >= FIRST + LOW) & (lanes < FIRST + LOW + E)
    top = jnp.max(jnp.where(first, logits, NEGATIVE), axis=1, keepdims=True)
    weights = jnp.where(first | second, jnp.exp(logits - top), 0.0)
    probs = weights / jnp.sum(jnp.where(first, weights, 0.0), axis=1, keepdims=True)
    probs_ref[...] = probs
    gates_ref[...] = in_two(probs * chosen(routes))


def attend(*args):
    outs = [
        ((ROWS, H * HD), F32),
        ((8, QUERIES), F32),
        ((ROWS, D), F32),
        ((ROWS, D), BF),
        ((ROWS, HD), BF),
        ((ROWS, HD), F32),
    ]
    return local_call(attend_kernel, args, outs, "attend", 2_400_000_000, specs=[SMEM, SMEM] + [VMEM] * 6)


GELU = math.sqrt(2.0 / math.pi)


def gate_column(gates, place_ref, h):
    lane = FIRST + (place_ref[0] * 3 + h) // 2
    lanes = expert_lanes()
    here = (lanes == lane) | (lanes == lane + LOW)
    return jnp.sum(jnp.where(here, gates, 0.0), axis=1, keepdims=True)


def experts_kernel(place_ref, rows, gates, w_gate, w_up, w_down, mixed, gate_raw, up_raw, total):
    h = pl.program_id(0)
    gate = jnp.dot(rows[...], w_gate[...], preferred_element_type=F32)
    up = jnp.dot(rows[...], w_up[...], preferred_element_type=F32)
    gate_raw[...] = gate
    up_raw[...] = up
    active = 0.5 * gate * (1.0 + jnp.tanh(GELU * (gate + 0.044715 * gate * gate * gate)))
    weighted = (gate_column(gates[...].astype(F32), place_ref, h) * (active * up)).astype(BF)
    out = jnp.dot(weighted, w_down[...], preferred_element_type=F32)

    @pl.when(h == 0)
    def _():
        total[...] = out

    @pl.when(h == 1)
    def _():
        total[...] += out

    @pl.when(h == 2)
    def _():
        mixed[...] = (total[...] + out).astype(BF)


def whole(shape):
    return pl.BlockSpec(shape, lambda h: (0,) * len(shape))


def experts(place_here, rows, gates, wide, low):
    count = 4 * ROWS
    return local_call(
        experts_kernel,
        (place_here, rows, gates, wide, wide, low),
        [((count, D), BF), ((count, SLICE), F32), ((count, SLICE), F32)],
        "experts",
        5_400_000_000,
        specs=[
            SMEM,
            whole((count, D)),
            whole((count, HD)),
            pl.BlockSpec((D, HALF), lambda h: (0, h)),
            pl.BlockSpec((D, HALF), lambda h: (0, 3 + h)),
            pl.BlockSpec((HALF, D), lambda h: (h, 0)),
        ],
        out_specs=[
            whole((count, D)),
            pl.BlockSpec((count, HALF), lambda h: (0, h)),
            pl.BlockSpec((count, HALF), lambda h: (0, h)),
        ],
        grid=(3,),
        scratch=[((count, D), F32)],
    )


def experts_back_kernel(
    place_ref, rows, d_rows, gates, gate_raw, up_raw, w_gate, w_up, w_down, d_normed, d_gates, *rest
):
    chunks, (total, strip) = rest[:10], rest[10:]
    h = pl.program_id(0)
    gate, up = gate_raw[...], up_raw[...]
    back = nt(d_rows[...], w_down[...])
    inner = jnp.tanh(GELU * (gate + 0.044715 * gate * gate * gate))
    active = 0.5 * gate * (1.0 + inner)
    slope = 0.5 * (1.0 + inner) + 0.5 * gate * (1.0 - inner * inner) * (GELU * (1.0 + 3 * 0.044715 * gate * gate))
    made = active * up
    weight = gate_column(gates[...].astype(F32), place_ref, h)
    lane = FIRST + (place_ref[0] * 3 + h) // 2
    lanes = expert_lanes()
    here = (lanes == lane) | (lanes == lane + LOW)
    d_weight = jnp.where(here, jnp.sum(made * back, axis=1, keepdims=True), 0.0)
    d_made = weight * back
    d_gate = (d_made * up * slope).astype(BF)
    d_up = (d_made * active).astype(BF)
    weighted = (weight * made).astype(BF)
    out = nt(d_gate, w_gate[...]) + nt(d_up, w_up[...])

    @pl.when(h == 0)
    def _():
        total[...] = out
        d_gates[...] = d_weight

    @pl.when(h != 0)
    def _():
        d_gates[...] += d_weight

    @pl.when(h == 1)
    def _():
        total[...] += out

    @pl.when(h == 2)
    def _():
        d_normed[...] = (total[...] + out).astype(BF)

    for shard in range(4):
        columns = slice(shard * SHARD, (shard + 1) * SHARD)
        for kind, (left, right) in enumerate(((rows, d_gate), (rows, d_up), (d_rows, weighted))):
            strip[...] = tn(left[:, columns], right).astype(BF)
            for part in (0, 1):
                for n, k in enumerate((0, 1, 3, 2)):
                    start = part * PART + ((place_ref[1 + part] + k) % 4) * STRIP
                    chunk = chunks[part * 5 + n + (shard // 2 if k == 2 else 0)]
                    chunk[shard % 2 if k == 2 else shard, :, kind * HALF : (kind + 1) * HALF] = strip[
                        pl.ds(pl.multiple_of(start, 16), STRIP), :
                    ]


def experts_back(place_here, rows, d_rows, gates, gate_raw, up_raw, wide, low):
    count = 4 * ROWS
    column = pl.BlockSpec((count, HALF), lambda h: (0, h))
    return local_call(
        experts_back_kernel,
        (place_here, rows, d_rows, gates, gate_raw, up_raw, wide, wide, low),
        [((count, D), BF), ((count, HD), F32)] + ([((4, STRIP, WIDE), BF)] * 3 + [((2, STRIP, WIDE), BF)] * 2) * 2,
        "experts_back",
        10_800_000_000,
        specs=[
            SMEM,
            whole((count, D)),
            whole((count, D)),
            whole((count, HD)),
            column,
            column,
            pl.BlockSpec((D, HALF), lambda h: (0, h)),
            pl.BlockSpec((D, HALF), lambda h: (0, 3 + h)),
            pl.BlockSpec((HALF, D), lambda h: (h, 0)),
        ],
        out_specs=[whole((count, D)), whole((count, HD))]
        + (
            [pl.BlockSpec((4, STRIP, 3 * HALF), lambda h: (0, 0, h))] * 3
            + [pl.BlockSpec((2, STRIP, 3 * HALF), lambda h: (0, 0, h))] * 2
        )
        * 2,
        grid=(3,),
        scratch=[((count, D), F32), ((SHARD, HALF), BF)],
    )


def attend_back_kernel(
    where,
    spans,
    q_ref,
    kv_ref,
    o_ref,
    lse_ref,
    cosine,
    sine,
    w_out,
    small,
    routes,
    probs_ref,
    hidden_ref,
    d_result,
    two_parts,
    gate_parts,
    d_hidden_ref,
    d_attn_ref,
    d_router_ref,
    dq_ref,
    dkv_ref,
    acc_ref,
    do_ref,
    turned_ref,
):
    d_gates = gate_parts[0].astype(F32) + gate_parts[1].astype(F32) + gate_parts[2].astype(F32)
    lanes = expert_lanes()
    first = (lanes >= FIRST) & (lanes < FIRST + E)
    d_select = jnp.where(first, (d_gates + pltpu.roll(d_gates, HD - LOW, 1)) * chosen(routes), 0.0)
    probs = jnp.where(first, probs_ref[...], 0.0)
    d_router = (probs * (d_select - jnp.sum(probs * d_select, axis=1, keepdims=True))).astype(BF)
    d_router_ref[...] = d_router
    d_normed = two_parts[0].astype(F32) + two_parts[1].astype(F32) + two_parts[2].astype(F32)
    d_normed = d_normed + jnp.dot(d_router, wide_router(small), preferred_element_type=F32)
    gain = small[...].astype(F32)[1:2, :]
    d_hidden = d_result[...] + norm_back(hidden_ref[...], gain, d_normed)
    d_hidden_ref[...] = d_hidden
    d_attn = d_hidden.astype(BF)
    d_attn_ref[...] = d_attn
    for start in range(0, H * HD, 512):
        columns = slice(start, start + 512)
        do_ref[:, columns] = nt(d_attn, w_out[columns, :]).astype(BF)

    lead = lead_of_keys()
    acc_ref[...] = jnp.zeros_like(acc_ref)
    for s in range(2):
        span = spans[s]
        stacked = [stack_heads(q_ref, s, kv) for kv in range(KV)]
        d_out = [stack_heads(do_ref, s, kv) for kv in range(KV)]
        delta = [
            jnp.sum((d_out[kv].astype(F32) * stack_heads(o_ref, s, kv)).T, axis=0, keepdims=True) for kv in range(KV)
        ]
        lse = [lse_ref[2 * s + kv : 2 * s + kv + 1, :] for kv in range(KV)]

        def body(b, carry):
            keys_values = block_rows(where, b, kv_ref)
            allowed = lead <= span * SPAN - b * BLOCK
            out, key_grads, value_grads = [], [], []
            for kv in range(KV):
                keys = keys_values[:, head(kv)]
                values = keys_values[:, head(KV + kv)]
                logits = nt(keys, stacked[kv]) * SCALE
                weights = jnp.where(allowed, jnp.exp(logits - lse[kv]), 0.0)
                d_weights = nt(values, d_out[kv])
                d_logits = (weights * (d_weights - delta[kv])).astype(BF)
                out.append(carry[kv] + tn(keys, d_logits))
                key_grads.append(jnp.dot(d_logits, stacked[kv], preferred_element_type=F32) * SCALE)
                value_grads.append(jnp.dot(weights.astype(BF), d_out[kv], preferred_element_type=F32))
            grads = jnp.concatenate(key_grads + value_grads, axis=1)
            for i in range(4):
                rows = pl.ds(pl.multiple_of(where[b * 4 + i] * SPAN, SPAN), SPAN)
                acc_ref[rows, :] += grads[i * SPAN : (i + 1) * SPAN, :]
            return tuple(out)

        start = tuple(jnp.zeros((HD, QUERIES), F32) for _ in range(KV))
        final = lax.fori_loop(0, span // 4 + 1, body, start)
        for kv in range(KV):
            unstack_heads(turned_ref, s, kv, (final[kv] * SCALE).T)
    for k in range(H):
        dq_ref[:, head(k)] = turn(turned_ref[:, head(k)], cosine[...], -sine[...]).astype(BF)

    def put(i, carry):
        rows = pl.ds(pl.multiple_of(i * 256, 256), 256)
        dkv_ref[rows, :] = acc_ref[rows, :].astype(BF)
        return carry

    lax.fori_loop(0, acc_ref.shape[0] // 256, put, 0)


def attend_back(*args):
    length = args[3].shape[0]
    outs = [
        ((ROWS, D), F32),
        ((ROWS, D), BF),
        ((ROWS, HD), BF),
        ((ROWS, H * HD), BF),
        ((length, 2 * KV * HD), BF),
    ]
    return local_call(
        attend_back_kernel,
        args,
        outs,
        "attend_back",
        5_000_000_000,
        specs=[SMEM, SMEM] + [VMEM] * 14,
        scratch=[((length, 2 * KV * HD), F32), ((ROWS, H * HD), BF), ((ROWS, H * HD), F32)],
    )


def blocks_kernel(dq_ref, keys, cosine, sine, blocks):
    for f in range(3):
        blocks[f] = dq_ref[:, f * 512 : (f + 1) * 512]
    for k in range(KV):
        turned = turn(keys[0, :, head(k)].astype(F32), cosine[...], -sine[...])
        blocks[3, :, head(k)] = turned.astype(BF)
    blocks[3, :, KV * HD :] = keys[1]


def query_blocks(*args):
    return local_call(blocks_kernel, args, [((4, ROWS, 512), BF)], "query_blocks", 1_000_000)[0]


def inputs_kernel(blocks, w_query, w_key, w_value, tokens, small, d_hidden, out):
    gain = small[...].astype(F32)[0:1, :]
    d_normed = nt(blocks[3, :, : KV * HD], w_key[...]) + nt(blocks[3, :, KV * HD :], w_value[...])
    for f in range(3):
        d_normed = d_normed + nt(blocks[f], w_query[:, f * 512 : (f + 1) * 512])
    out[...] = d_hidden[...] + norm_back(tokens[...].astype(F32), gain, d_normed)


def input_grads(*args):
    return local_call(inputs_kernel, args, [((ROWS, D), F32)], "input_grads", 800_000_000)[0]


def lay_out_kernel(place_ref, *refs):
    pieces = refs[:10]
    w_gate, w_up, gate_out, up_out, down_out, sum_ref, turned = refs[10:]
    cell = (pl.program_id(0) % 3) * 3
    own_set = pl.program_id(0) // 3
    for part in (0, 1):
        for n, k in enumerate((0, 1, 3, 2)):
            start = part * PART + ((place_ref[1 + part] + 4 - k) % 4) * STRIP
            rows = pl.ds(pl.multiple_of(start, 16), STRIP)
            for kind, out in enumerate((gate_out.at[0], up_out.at[0], turned)):
                columns = pl.ds(pl.multiple_of((cell + kind) * HALF, 128), HALF)
                piece = pieces[part * 5 + n][0, :, columns]
                if k == 2:
                    piece = jnp.where(own_set < 2, piece, pieces[part * 5 + 4][0, :, columns])
                out[rows, :] = piece.astype(F32)
    down_out[0] = turned[...].T
    both = w_gate[0].astype(F32) * gate_out[0] + w_up[0].astype(F32) * up_out[0]
    row_sum = jnp.sum(both, axis=1, keepdims=True)

    @pl.when(pl.program_id(0) == 0)
    def _():
        sum_ref[...] = row_sum

    @pl.when(pl.program_id(0) != 0)
    def _():
        sum_ref[...] += row_sum


def lay_out_experts(place_here, pieces, w_gate, w_up):
    wide = pl.BlockSpec((1, SHARD, HALF), lambda n: (n // 2, 0, n % 2))
    return local_call(
        lay_out_kernel,
        (place_here,) + tuple(pieces) + (w_gate, w_up),
        [((E, SHARD, FF), F32), ((E, SHARD, FF), F32), ((E, FF, SHARD), F32), ((SHARD, 1), F32)],
        "lay_out_experts",
        20_000_000,
        specs=[SMEM]
        + (
            [pl.BlockSpec((1, STRIP, WIDE), lambda n: (n // 3, 0, 0))] * 3
            + [pl.BlockSpec((1, STRIP, WIDE), lambda n: (n // 3 % 2, 0, 0))] * 2
        )
        * 2
        + [wide, wide],
        out_specs=[
            wide,
            wide,
            pl.BlockSpec((1, HALF, SHARD), lambda n: (n // 2, n % 2, 0)),
            pl.BlockSpec((SHARD, 1), lambda n: (0, 0)),
        ],
        grid=(12,),
        scratch=[((SHARD, HALF), F32)],
    )


def attention_kernel(tail, w_query, w_key, w_value, query, key, value, out, router, row_sum):
    total = jnp.zeros((SHARD, 1), F32)
    for f in range(3):
        columns = slice(f * 512, (f + 1) * 512)
        piece = tail[f, :, :512].astype(F32)
        query[:, columns] = piece
        total = total + jnp.sum(w_query[:, columns].astype(F32) * piece, axis=1, keepdims=True)
    for ref, weight, columns in ((key, w_key, slice(0, 256)), (value, w_value, slice(256, 512))):
        piece = tail[3, :, columns].astype(F32)
        ref[...] = piece
        total = total + jnp.sum(weight[...].astype(F32) * piece, axis=1, keepdims=True)
    row_sum[...] = total
    for f in range(4):
        out[:, f * SHARD : (f + 1) * SHARD] = tail[f, :, 512 : 512 + SHARD].astype(F32)
    pieces = [tail[f, :, 512 + SHARD :].astype(F32) for f in range(4)]
    router[...] = (pieces[0] + pieces[1] + pieces[2] + pieces[3])[:, FIRST : FIRST + E]


def lay_out_attention(*args):
    outs = [((SHARD, width), F32) for width in (D, KV * HD, KV * HD, D, E, 1)]
    return local_call(attention_kernel, args, outs, "lay_out_attention", 4_000_000)


def add_two(a, b):
    return (a.astype(F32) + b.astype(F32)).astype(BF)


def shift_pairs(axis, k):
    pairs = []
    for ctx in range(32):
        x, z, y_lo = ctx // 8, (ctx // 2) % 4, ctx % 2
        if axis == 0:
            pairs.append((ctx, (x + k) % 4 * 8 + z * 2 + y_lo))
        else:
            pairs.append((ctx, x * 8 + (z + k) % 4 * 2 + y_lo))
    return pairs


def shift(array, axis, k):
    return lax.ppermute(array, "ctx", shift_pairs(axis, k))


def angle_tables(position):
    half_size = HD // 2
    frequency = jnp.exp(-(jnp.arange(half_size, dtype=F32) * 2.0 / HD) * math.log(BASE))
    angles = position.astype(F32)[:, None] * frequency[None, :]
    cosine, sine = jnp.cos(angles), jnp.sin(angles)
    return (
        jnp.concatenate([cosine, cosine], axis=1),
        jnp.concatenate([-sine, sine], axis=1),
    )


def local(
    tokens,
    teacher,
    valid_mask,
    token_count,
    routes,
    span_order,
    w_query,
    w_key,
    w_value,
    w_out,
    norm_gain,
    w_router,
    moe_gain,
    w_gate,
    w_up,
    w_down,
):
    rows = tokens[0]
    ctx = lax.axis_index("ctx")
    shard = lax.axis_index("fsdp")
    x, z, _, _, _ = place()
    place_here = jnp.stack([shard, x, z])
    spans = lax.dynamic_slice(span_order, (ctx * 2,), (2,))
    numbers = jnp.arange(64, dtype=jnp.int32)
    where = jnp.sum(jnp.where(span_order[None, :] == numbers[:, None], numbers[None, :], 0), axis=1)
    position = (spans[:, None] * SPAN + jnp.arange(SPAN, dtype=jnp.int32)[None, :]).reshape(ROWS)
    cosine, sine = angle_tables(position)

    small = jnp.concatenate(
        [norm_gain[None, :], moe_gain[None, :], w_router.T, jnp.zeros((16 - 2 - E, SHARD), BF)], axis=0
    )
    full_query, full_key, full_value, full_out, small = gather_attention_weights(
        (w_query, w_key, w_value, w_out), small, 1
    )
    input_one, query, keys_values = project(rows, small, cosine, sine, full_query, full_key, full_value)
    keys, quarters = gather_keys(keys_values, (w_gate, w_up, w_down), 2)
    keys = keys.reshape(32 * ROWS, 2 * KV * HD)
    attended, lse, hidden, input_two, gates_sent, probs = attend(
        where, spans, query, keys, rows, full_out, small, routes[0]
    )

    group_two, gates, wide, low = group_spread(
        (input_two, gates_sent), 3, "group_normed", (w_gate, w_up, w_down, quarters)
    )
    group_two, gates = group_two.reshape(4 * ROWS, D), gates.reshape(4 * ROWS, HD)
    mixed, gate_raw, up_raw = experts(place_here, group_two, gates, wide, low)
    (mixed,) = group_sum((mixed.reshape(4, ROWS, D),), 4, "group_mixture")
    result = hidden + jnp.sum(mixed.astype(F32), axis=0)

    valid_rows = valid_mask[0].astype(F32)[:, None]
    error_rows = result - teacher[0].astype(F32)
    squared = jnp.full((8, 128), jnp.sum(valid_rows * error_rows * error_rows), F32)
    norm_factor = token_count[0].astype(F32) * D
    d_result = 2.0 * valid_rows * error_rows / norm_factor
    (group_d,) = group_spread((d_result.astype(BF),), 5, "group_d_result")
    d_two, d_gates, *chunks = experts_back(
        place_here, group_two, group_d.reshape(4 * ROWS, D), gates, gate_raw, up_raw, wide, low
    )
    halfway = [shift(chunks[part * 5 + 3 + n], part, (1, 3)[n]) for n in (0, 1) for part in (0, 1)]
    d_gates_high = d_gates.astype(BF)
    low_lanes = (jnp.arange(HD) >= LOW)[None, :]
    d_gates_sent = jnp.where(low_lanes, (d_gates - d_gates_high.astype(F32)).astype(BF), d_gates_high)
    two_parts, gate_parts, squared = group_sum(
        (d_two.reshape(4, ROWS, D), d_gates_sent.reshape(4, ROWS, HD)), 6, "group_d_normed", squared
    )
    squared = jnp.sum(squared, axis=0)
    halfway, two_parts = lax.optimization_barrier((halfway, two_parts))
    came = []
    for part in (0, 1):
        own, ahead, behind = chunks[part * 5 : part * 5 + 3]
        ahead = jnp.concatenate([add_two(ahead[:2], halfway[part]), ahead[2:]])
        behind = jnp.concatenate([behind[:2], add_two(behind[2:], halfway[2 + part])])
        came.append([own, shift(ahead, part, 1), shift(behind, part, 3)])
    d_hidden, d_attn, d_router, d_query, d_keys = attend_back(
        where,
        spans,
        query,
        keys,
        attended,
        lse,
        cosine,
        sine,
        full_out,
        small,
        routes[0],
        probs,
        hidden,
        d_result,
        two_parts,
        gate_parts,
    )

    expert_sum, tail_sum, key_sum, loss_sum = GradSum(WIDE), GradSum(TAIL), KeySum(), LossSum()
    d_attn_blocks = jnp.stack([d_attn[:, f * SHARD : (f + 1) * SHARD] for f in range(4)])
    share = GroupShare((attended.astype(BF), input_one), (d_attn_blocks,))
    d_keys, squared, group_attended, group_one, group_d_attn = sum_step(
        (key_sum, loss_sum), (d_keys.reshape(4, 4, 2, ROWS, 2 * KV * HD), squared), 0, 7, "sums_first", share
    )
    came, d_keys = lax.optimization_barrier((came, d_keys))
    part = jnp.stack([sum(each.astype(F32) for each in three).astype(BF) for three in came])
    part, d_keys, squared = sum_step(
        (expert_sum, key_sum, loss_sum), (part, d_keys, squared), 1, 8, "sums_second"
    )
    part, d_keys, squared = sum_step((expert_sum, key_sum, loss_sum), (part, d_keys, squared), 2, 9, "sums_third")
    loss_value = (squared[0, 0] / norm_factor).reshape(1)

    blocks = query_blocks(d_query, d_keys, cosine, sine)
    *strips, group_d_qkv = gather_grads(part, WIDE, True, 10, "grads_gather", blocks)
    pieces = [[strips[part], shift(strips[part], part, 1), shift(strips[part], part, 3)] for part in (0, 1)]

    group_one = group_one.reshape(4 * ROWS, D)
    tail = jnp.concatenate(
        [
            tn(group_one, group_d_qkv.reshape(4 * ROWS, 512)).astype(BF),
            tn(group_attended.reshape(4 * ROWS, D), group_d_attn.reshape(4 * ROWS, SHARD)).astype(BF),
            tn(input_two, d_router).astype(BF),
        ],
        axis=1,
    ).reshape(4, SHARD, TAIL)
    for step in range(3):
        (tail,) = sum_step((tail_sum,), (tail,), step, 11 + step, "tail_" + "abc"[step])
        if step == 0:
            pieces, tail = lax.optimization_barrier((pieces, tail))
            for part in (0, 1):
                pieces[part].append(shift(pieces[part][1][:2], part, 1))
                pieces[part].append(shift(pieces[part][2][2:], part, 3))
    (tail,) = gather_grads(tail, TAIL, False, 14, "tail_gather")
    d_inputs = input_grads(blocks, full_query, full_key, full_value, rows, small, d_hidden)
    grad_query, grad_key, grad_value, grad_out, grad_router, gain_one_sum = lay_out_attention(
        tail, w_query, w_key, w_value
    )
    grad_gate, grad_up, grad_down, gain_two_sum = lay_out_experts(place_here, pieces[0] + pieces[1], w_gate, w_up)

    grad_gain_one = gain_one_sum[:, 0] / norm_gain.astype(F32)
    grad_gain_two = (gain_two_sum[:, 0] + jnp.sum(w_router.astype(F32) * grad_router, axis=1)) / moe_gain.astype(
        F32
    )
    return (
        result.astype(BF)[None],
        loss_value,
        d_inputs[None],
        grad_query,
        grad_key,
        grad_value,
        grad_out,
        grad_gain_one,
        grad_router,
        grad_gain_two,
        grad_gate,
        grad_up,
        grad_down,
    )


def solution(mesh):
    in_specs = (
        P("fsdp", "ctx", None),
        P("fsdp", "ctx", None),
        P("fsdp", "ctx"),
        P(),
        P("fsdp", "ctx", None),
        P(),
        P("fsdp", None),
        P("fsdp", None),
        P("fsdp", None),
        P("fsdp", None),
        P("fsdp"),
        P("fsdp", None),
        P("fsdp"),
        P(None, "fsdp", None),
        P(None, "fsdp", None),
        P(None, None, "fsdp"),
    )
    out_specs = (
        P("fsdp", "ctx", None),
        P(),
        P("fsdp", "ctx", None),
        P("fsdp", None),
        P("fsdp", None),
        P("fsdp", None),
        P("fsdp", None),
        P("fsdp"),
        P("fsdp", None),
        P("fsdp"),
        P(None, "fsdp", None),
        P(None, "fsdp", None),
        P(None, None, "fsdp"),
    )
    return jax.shard_map(local, mesh=mesh, in_specs=in_specs, out_specs=out_specs, check_vma=False)
```

```python
import math

import jax
import jax.numpy as jnp
from jax import lax
from jax.experimental import pallas as pl
from jax.experimental.pallas import tpu as pltpu
from jax.sharding import PartitionSpec as P

H = 12
KV = 2
HD = 128
E = 6
D = 1536
FF = 768
GROUPS = H // KV
ROWS = 128
SPAN = 64
HALF = 384
SLICE = 3 * HALF
QKV = 2048
SHARD = 384
WIDE = 3 * SLICE + 128
TAIL = 1024
PART = SHARD // 2
STRIP = PART // 4
EPS = 1e-06
BASE = 1000000.0
NEGATIVE = -1e30
SCALE = HD**-0.5
LOG2_E = math.log2(math.e)
SCALE_2 = SCALE * LOG2_E
MESH = pl.DeviceIdType.MESH
BF = jnp.bfloat16
F32 = jnp.float32


def place():
    ctx = lax.axis_index("ctx")
    shard = lax.axis_index("fsdp")
    return ctx // 8, (ctx // 2) % 4, ctx % 2, shard // 2, shard % 2


def device(x, z, y_lo, y_hi, core):
    return (x * 8 + z * 2 + y_lo, y_hi * 2 + core)


def x_peers(at):
    x, z, y_lo, y_hi, core = at
    return [device((x + k) % 4, z, y_lo, y_hi, core) for k in (1, 2, 3)]


def x_next(at):
    peers = x_peers(at)
    return [peers[0], peers[2]]


def z_next(at):
    peers = z_peers(at)
    return [peers[0], peers[2]]


def z_peers(at):
    x, z, y_lo, y_hi, core = at
    return [device(x, (z + k) % 4, y_lo, y_hi, core) for k in (1, 2, 3)]


def group_member(at, shard_hi, core):
    x, z, y_lo, y_hi, _ = at
    y_lo_there = (y_lo + y_hi + shard_hi) % 2
    return device(x, z, y_lo_there, shard_hi, core)


class Net:
    def __init__(self, send_sem, recv_sem, local_sem, stage):
        self.sems = (send_sem, recv_sem, local_sem)
        self.stage = stage
        self.remote = 0
        self.loads = []
        self.kept = 0
        self.open = {}
        self.copies = []

    def greet(self, peers):
        barrier = pltpu.get_barrier_semaphore()
        for peer in peers:
            pl.semaphore_signal(barrier, inc=1, device_id=peer, device_id_type=MESH)
        pl.semaphore_wait(barrier, len(peers))

    def _open(self, copy):
        copy.start()
        self.open[id(copy)] = copy.wait
        self.copies.append(copy)
        return copy

    def send(self, src, dst, peer):
        slot = self.remote
        self.remote += 1
        return self._open(
            pltpu.make_async_remote_copy(
                src_ref=src,
                dst_ref=dst,
                send_sem=self.sems[0].at[slot],
                recv_sem=self.sems[1].at[slot],
                device_id=peer,
                device_id_type=MESH,
            )
        )

    def keep(self, src, dst):
        slot = self.kept
        self.kept += 1
        load = pltpu.make_async_copy(src, self.stage[slot], self.sems[2].at[slot])
        load.start()
        self.loads.append((load, slot, dst))

    def settle(self):
        stores = []
        for load, slot, dst in self.loads:
            load.wait()
            stores.append(self._open(pltpu.make_async_copy(self.stage[slot], dst, self.sems[2].at[slot])))
        self.loads = []
        return stores

    def done(self, copies):
        for copy in copies:
            copy.wait()
            del self.open[id(copy)]

    def arrived(self, copy):
        copy.wait_recv()
        self.open[id(copy)] = copy.wait_send

    def finish(self):
        self.settle()
        for wait in self.open.values():
            wait()


def exchange(body, inputs, outs, remote, keeps, number, name, scratch=()):
    count = len(inputs)
    total = count + len(outs)

    def kernel(*refs):
        net = Net(*refs[total : total + 3], refs[total + 3 :])
        body(net, refs[:count], refs[count:total])
        net.finish()

    any_spec = pl.BlockSpec(memory_space=pl.ANY)
    return pl.pallas_call(
        kernel,
        out_shape=[jax.ShapeDtypeStruct(shape, kind) for shape, kind in outs],
        in_specs=[any_spec] * count,
        out_specs=[any_spec] * len(outs),
        scratch_shapes=[
            pltpu.SemaphoreType.DMA((remote,)),
            pltpu.SemaphoreType.DMA((remote,)),
            pltpu.SemaphoreType.DMA((len(keeps) + len(scratch) + 1,)),
        ]
        + [pltpu.VMEM(shape, kind) for shape, kind in list(keeps) + list(scratch)],
        compiler_params=pltpu.CompilerParams(
            collective_id=number, has_side_effects=True, vmem_limit_bytes=60 << 20
        ),
        name=name,
    )(*inputs)


def ring_of(at):
    x, z, y_lo, y_hi, core = at
    return [
        device(
            lax.select(core == 0, (x + k) % 4, x), lax.select(core == 0, z, (z + k) % 4), y_lo, y_hi, core
        )
        for k in (1, 3)
    ]


class Ring:
    def __init__(self, net, blocks, own, neighbours):
        self.net, self.blocks, self.own, self.neighbours = net, blocks, own, neighbours
        self.first, self.rest = [], []

    def send(self, origin, half, way):
        return [self.net.send(ref, ref, self.neighbours[way]) for ref in self.blocks(origin, half)]

    def start(self):
        self.start_half(0)
        self.start_half(1)
        return self

    def start_half(self, half):
        self.first.append(self.send(self.own, half, half))
        self.rest.append(self.send(self.own, half, 1 - half))

    def forward(self):
        self.last = []
        for way in (0, 1):
            for copy in self.first[way]:
                self.net.arrived(copy)
            self.last.append(self.send((self.own + (3, 1)[way]) % 4, way, way))
        return self

    def finish(self):
        for copies in self.rest + self.last:
            for copy in copies:
                self.net.arrived(copy)


def gather_attention_weights(parts, small, number):
    count = len(parts)

    def body(net, ins, outs):
        at = place()
        x, z, y_lo, y_hi, core = at
        shard = y_hi * 2 + core
        sibling = device(x, z, y_lo, y_hi, 1 - core)
        partner = device(x, z, 1 - y_lo, 1 - y_hi, core)
        crossed = device(x, z, 1 - y_lo, 1 - y_hi, 1 - core)
        here = lax.select(core == 0, x, z)
        ring = ring_of(at)
        net.greet([sibling, partner, crossed] + ring)
        small_spot = outs[count].at[:, pl.ds(pl.multiple_of(shard * SHARD, 128), SHARD)]
        for peer in (partner, crossed, sibling):
            net.send(ins[count], small_spot, peer)

        def block(array, owner, start, size):
            width = ins[array].shape[1]
            return outs[array].at[pl.ds(pl.multiple_of(owner * SHARD + start, 16), size), pl.ds(0, width)]

        quarter = SHARD // 4
        order = (3, 0, 1, 2)
        part = quarter // 2
        first = {}
        for a in order:
            for half in (0, 1):
                start = here * quarter + half * part
                rows = pl.ds(pl.multiple_of(start, 16), part)
                first[a, half] = net.send(ins[a].at[rows, :], block(a, shard, start, part), partner)
        for a in order:
            net.send(ins[a], block(a, shard, 0, SHARD), sibling)
            net.keep(ins[a], block(a, shard, 0, SHARD))
        net.keep(ins[count], small_spot)
        net.settle()
        far = (1 - y_hi) * 2 + core
        rings = {}
        for a in order:

            def halves(origin, half, a=a):
                return [block(a, far, origin * quarter + half * part, part)]

            rings[a] = Ring(net, halves, here, ring)
            for half in (0, 1):
                net.arrived(first[a, half])
                rings[a].start_half(half)
            mine = block(a, far, here * quarter, quarter)
            net.send(mine, mine, sibling)
        for a in order:
            rings[a].forward()
        for a in order:
            rings[a].finish()
            for k in (1, 2, 3):
                piece = block(a, far, (here + k) % 4 * quarter, quarter)
                net.send(piece, piece, sibling)

    return exchange(
        body,
        tuple(parts) + (small,),
        [((D, part.shape[1]), BF) for part in parts] + [((16, D), BF)],
        count * 13 + 3,
        [(parts[a].shape, BF) for a in (3, 0, 1, 2)] + [((16, SHARD), BF)],
        number,
        "attention_weights",
    )


class ExpertWeights:
    quarter = HALF // 4
    cells = [(h, kind) for h in range(3) for kind in range(3)]

    def source(self, ins, owner, h, kind, start, size):
        index = owner * 3 + h
        expert = index // 2
        offset = pl.multiple_of((index % 2) * HALF, 128)
        if kind < 2:
            return ins[kind].at[expert, pl.ds(start, size), pl.ds(offset, HALF)]
        return ins[2].at[expert, pl.ds(pl.multiple_of(offset + start, 32), size), :]

    def target(self, outs, from_shard, h, kind, start, size):
        if kind < 2:
            rows = pl.multiple_of(from_shard * SHARD + start, 32)
            return outs[0].at[pl.ds(rows, size), pl.ds((2 * h + kind) * HALF, HALF)]
        columns = pl.multiple_of(from_shard * SHARD, 128)
        return outs[1].at[pl.ds(pl.multiple_of(h * HALF + start, 32), size), pl.ds(columns, SHARD)]

    def cross(self, net, ins, quarters, at):
        x, z, y_lo, y_hi, core = at
        for step in (0, 1):
            far_core = (core + step) % 2
            start = pl.multiple_of(lax.select(far_core == 0, x, z) * self.quarter, 32)
            owner = (1 - y_hi) * 2 + far_core
            peer = device(x, z, 1 - y_lo, 1 - y_hi, far_core)
            for n, (h, kind) in enumerate(self.cells):
                net.send(self.source(ins, owner, h, kind, start, self.quarter), quarters.at[step, n], peer)

    def around(self, net, ins, quarters, outs, at):
        x, z, y_lo, y_hi, core = at
        shard = y_hi * 2 + core
        sibling = device(x, z, y_lo, y_hi, 1 - core)
        here = lax.select(core == 0, x, z)

        def spots(origin, step):
            start = pl.multiple_of(origin * self.quarter, 32)
            from_shard = (1 - y_hi) * 2 + (core + step) % 2
            return [self.target(outs, from_shard, h, kind, start, self.quarter) for h, kind in self.cells]

        first, neighbours = [], ring_of(at)
        for turn in (0, 1):
            for way in (0, 1):
                step = way if turn == 0 else 1 - way
                copies = [
                    net.send(quarters.at[step, n], spot, neighbours[way]) for n, spot in enumerate(spots(here, step))
                ]
                if turn == 0:
                    first.append(copies)
        for step in (0, 1):
            for n, spot in enumerate(spots(here, step)):
                net.keep(quarters.at[step, n], spot)
        for h, kind in self.cells:
            other = y_hi * 2 + 1 - core
            net.send(self.source(ins, other, h, kind, 0, HALF), self.target(outs, shard, h, kind, 0, HALF), sibling)
            net.keep(self.source(ins, shard, h, kind, 0, HALF), self.target(outs, shard, h, kind, 0, HALF))
        return first, spots, here, neighbours

    def forward(self, net, state):
        first, spots, here, neighbours = state
        for n in range(len(self.cells)):
            for way in (0, 1):
                net.arrived(first[way][n])
                spot = spots((here + (3, 1)[way]) % 4, way)[n]
                net.send(spot, spot, neighbours[way])


EXPERT = ExpertWeights()


def gather_keys(local, experts, number):
    def body(net, ins, outs):
        mine, whole = ins[0], outs[0]
        at = place()
        x, z, y_lo, y_hi, core = at
        partner = device(x, z, 1 - y_lo, y_hi, core)
        across = [device(x, z, 1 - y_lo, 1 - y_hi, c) for c in (0, 1)]
        net.greet([partner] + x_next(at) + z_next(at) + across)
        spot = whole.at[x, z, y_lo]
        near = net.send(mine, spot, partner)
        net.keep(mine, spot)
        EXPERT.cross(net, ins[1:], outs[1], at)
        net.done(net.settle())
        net.arrived(near)
        half = KV * HD
        cuts = [pl.ds(part * half, half) for part in (0, 1)]
        sides = (x_next(at), z_next(at))
        near_rings = (
            Ring(net, lambda o, h: [whole.at[x, o, h, :, cuts[0]]], z, sides[1]),
            Ring(net, lambda o, h: [whole.at[o, z, h, :, cuts[1]]], x, sides[0]),
        )
        far_rings = (
            Ring(net, lambda o, h: [whole.at[o, :, h, :, cuts[0]]], x, sides[0]),
            Ring(net, lambda o, h: [whole.at[:, o, h, :, cuts[1]]], z, sides[1]),
        )
        for ring in near_rings:
            ring.start()
        for ring in near_rings:
            ring.forward()
        for near_ring, far_ring in zip(near_rings, far_rings):
            near_ring.finish()
            far_ring.start()
        for ring in far_rings:
            ring.forward()

    return exchange(
        body,
        (local,) + experts,
        [((4, 4, 2, ROWS, 2 * KV * HD), BF), ((2, 9, EXPERT.quarter, HALF), BF)],
        25 + 18,
        [((ROWS, 2 * KV * HD), BF)],
        number,
        "keys_values",
    )


def group_places(at):
    x, z, y_lo, y_hi, core = at
    sibling = device(x, z, y_lo, y_hi, 1 - core)
    partner = device(x, z, 1 - y_lo, 1 - y_hi, core)
    return sibling, partner


class Spread:
    def start(self, net, mine, whole, at):
        sibling, partner = group_places(at)
        spot = whole.at[at[3] * 2 + at[4]]
        self.copy = net.send(mine, spot, partner)
        net.send(mine, spot, sibling)
        net.keep(mine, spot)

    def forward(self, net, whole, at):
        sibling, partner = group_places(at)
        net.arrived(self.copy)
        far = whole.at[(1 - at[3]) * 2 + at[4]]
        net.send(far, far, sibling)


def group_spread(parts, number, name, weights=None):
    count = len(parts)
    keeps = [(part.shape, part.dtype) for part in parts]
    outs = [((4,) + part.shape, part.dtype) for part in parts]
    inputs = tuple(parts)
    remote = 3 * count
    if weights is not None:
        inputs += weights
        outs += [((D, 2 * SLICE), BF), ((SLICE, D), BF)]
        remote += 7 * 9
        keeps += [((EXPERT.quarter, HALF), BF)] * 18 + [((HALF, HALF), BF)] * 9

    def body(net, ins, outs):
        at = place()
        sibling, partner = group_places(at)
        net.greet([sibling, partner] + (ring_of(at) if weights is not None else []))
        spreads = [Spread() for _ in range(count)]
        for one, mine, whole in zip(spreads, ins, outs):
            one.start(net, mine, whole, at)
        if weights is not None:
            state = EXPERT.around(net, ins[count:-1], ins[-1], outs[count:], at)
        net.settle()
        for one, whole in zip(spreads, outs):
            one.forward(net, whole, at)
        if weights is not None:
            EXPERT.forward(net, state)

    return exchange(body, inputs, outs, remote, keeps, number, name)


def group_sum(parts, number, name, extra=None):
    count = len(parts)
    spread = () if extra is None else (extra,)
    keeps = [(part.shape[1:], BF) for part in parts] + [(one.shape, one.dtype) for one in spread]
    outs = [((3,) + part.shape[1:], BF) for part in parts] + [((4,) + one.shape, one.dtype) for one in spread]
    scratch = [((2,) + part.shape[1:], BF) for part in parts]

    def body(net, ins, outs):
        at = place()
        x, z, y_lo, y_hi, core = at
        sibling, partner = group_places(at)
        net.greet([sibling, partner])
        sums = net.stage[len(keeps) :]
        far = (1 - y_hi) * 2
        came, own = [], []
        for mine, pair in zip(ins, sums):
            came.append(net.send(mine.at[far + 1 - core], pair.at[1], sibling))
            load = pltpu.make_async_copy(mine.at[far + core], pair.at[0], net.sems[2].at[len(keeps) + len(own)])
            load.start()
            own.append(load)
        for mine, got in zip(ins[:count], outs):
            net.send(mine.at[y_hi * 2 + 1 - core], got.at[1], sibling)
            net.keep(mine.at[y_hi * 2 + core], got.at[0])
        spreads = []
        for mine, whole in zip(ins[count:], outs[count:]):
            spreads.append(Spread())
            spreads[-1].start(net, mine, whole, at)
        for n, pair in enumerate(sums):
            own[n].wait()
            net.arrived(came[n])

            def add(step, carry):
                rows = pl.ds(pl.multiple_of(step * 16, 16), 16)
                pair[0, rows, :] = (pair[0, rows, :].astype(F32) + pair[1, rows, :].astype(F32)).astype(BF)
                return carry

            lax.fori_loop(0, pair.shape[1] // 16, add, 0)
            net.send(pair.at[0], outs[n].at[2], partner)
        net.settle()
        for one, whole in zip(spreads, outs[count:]):
            one.forward(net, whole, at)

    return exchange(
        body, tuple(parts) + spread, outs, 3 * (count + len(spread)), keeps, number, name, scratch
    )


def add_up(pieces, axis):
    return jnp.sum(pieces.astype(F32), axis=axis).astype(BF)


def add_strips_kernel(*refs):
    for part in (0, 1):
        three = [refs[part * 3 + n][...].astype(F32) for n in range(3)]
        refs[6][part] = (three[0] + three[1] + three[2]).astype(BF)


def add_strips(strips):
    cell = WIDE // 4
    return local_call(
        add_strips_kernel,
        tuple(strips),
        [((2, 4, STRIP, WIDE), BF)],
        "add_strips",
        1000,
        specs=[pl.BlockSpec((4, STRIP, cell), lambda n: (0, 0, n))] * 6,
        out_specs=[pl.BlockSpec((2, 4, STRIP, cell), lambda n: (0, 0, 0, n))],
        grid=(4,),
    )[0]


class KeySum:
    half = KV * HD
    shapes = (
        ((2, 4, 4, 2, ROWS, KV * HD), BF),
        ((2, 4, 2, ROWS, KV * HD), BF),
        ((2, 2, ROWS, KV * HD), BF),
    )
    keeps = (
        [((4, 2, ROWS, KV * HD), BF)] * 2,
        [((2, ROWS, KV * HD), BF)] * 2,
        [((2, ROWS, KV * HD), BF)],
    )

    def first(self, net, whole, got, at):
        x, z = at[0], at[1]
        half = self.half
        peers = (x_peers(at), z_peers(at))
        for k in (2, 1, 3):
            net.send(whole.at[(x + k) % 4, :, :, :, pl.ds(0, half)], got.at[0, k], peers[0][k - 1])
            net.send(whole.at[:, (z + k) % 4, :, :, pl.ds(half, half)], got.at[1, k], peers[1][k - 1])
        net.keep(whole.at[x, :, :, :, pl.ds(0, half)], got.at[0, 0])
        net.keep(whole.at[:, z, :, :, pl.ds(half, half)], got.at[1, 0])

    def second(self, net, whole, got, at):
        x, z = at[0], at[1]
        peers = (x_peers(at), z_peers(at))
        for k in (2, 1, 3):
            net.send(whole.at[0, (z + k) % 4], got.at[0, k], peers[1][k - 1])
            net.send(whole.at[1, (x + k) % 4], got.at[1, k], peers[0][k - 1])
        net.keep(whole.at[0, z], got.at[0, 0])
        net.keep(whole.at[1, x], got.at[1, 0])

    def third(self, net, whole, got, at):
        x, z, y_lo, y_hi, core = at
        net.send(whole.at[:, 1 - y_lo], got.at[1], device(x, z, 1 - y_lo, y_hi, core))
        net.keep(whole.at[:, y_lo], got.at[0])


class GradSum:
    def __init__(self, columns):
        self.columns, self.cell = columns, columns // 4
        self.shapes = (
            ((2, 4, 4, STRIP, columns), BF),
            ((2, 4, 4, STRIP, self.cell), BF),
            ((2, 2, 2, STRIP, self.cell), BF),
        )
        self.keeps = (
            [((4, STRIP, columns), BF)] * 2,
            [((4, STRIP, self.cell), BF)] * 2,
            [((2, STRIP, self.cell), BF)],
        )

    def first(self, net, whole, got, at):
        own = (at[0], at[1])
        peers = (x_peers(at), z_peers(at))
        for k in (2, 1, 3, 0):
            for part in (0, 1):
                start = part * PART + ((own[part] + k) % 4) * STRIP
                block = whole.at[:, pl.ds(pl.multiple_of(start, 16), STRIP), :]
                if k == 0:
                    net.keep(block, got.at[part, 0])
                else:
                    net.send(block, got.at[part, k], peers[part][k - 1])

    def second(self, net, whole, got, at):
        own = (at[1], at[0])
        peers = (z_peers(at), x_peers(at))
        for k in (2, 1, 3, 0):
            for part in (0, 1):
                start = ((own[part] + k) % 4) * self.cell
                block = whole.at[part, :, :, pl.ds(pl.multiple_of(start, 128), self.cell)]
                if k == 0:
                    net.keep(block, got.at[part, 0])
                else:
                    net.send(block, got.at[part, k], peers[part][k - 1])

    def third(self, net, whole, got, at):
        x, z, y_lo, y_hi, core = at
        spot = got.at[y_lo, y_hi]
        for k in (2, 3, 1):
            there_hi, there_core = (y_hi + k // 2) % 2, (y_lo + k % 2) % 2
            net.send(whole.at[:, there_hi * 2 + there_core], spot, device(x, z, core, there_hi, there_core))
        mine = whole.at[:, y_hi * 2 + y_lo]
        slot, held = net.remote, net.kept
        net.remote += 1
        net.kept += 1
        stage, sem = net.stage[held], net.sems[2].at[held]

        @pl.when(core == y_lo)
        def _():
            load = pltpu.make_async_copy(mine, stage, sem)
            load.start()
            load.wait()
            store = pltpu.make_async_copy(stage, spot, sem)
            store.start()
            store.wait()

        @pl.when(core != y_lo)
        def _():
            copy = pltpu.make_async_remote_copy(
                src_ref=mine,
                dst_ref=spot,
                send_sem=net.sems[0].at[slot],
                recv_sem=net.sems[1].at[slot],
                device_id=device(x, z, core, y_hi, y_lo),
                device_id_type=MESH,
            )
            copy.start()
            copy.wait()


class LossSum:
    shapes = (((4, 8, 128), F32), ((4, 8, 128), F32), ((2, 8, 128), F32))
    keeps = ([((8, 128), F32)],) * 3

    def first(self, net, whole, got, at):
        for peer in x_peers(at):
            net.send(whole, got.at[at[0]], peer)
        net.keep(whole, got.at[at[0]])

    def second(self, net, whole, got, at):
        for peer in z_peers(at):
            net.send(whole, got.at[at[1]], peer)
        net.keep(whole, got.at[at[1]])

    def third(self, net, whole, got, at):
        x, z, y_lo, y_hi, core = at
        net.send(whole, got.at[y_lo], device(x, z, 1 - y_lo, y_hi, core))
        net.keep(whole, got.at[y_lo])


class GroupShare:
    def __init__(self, spread, swapped):
        self.count = len(spread)
        self.inputs = tuple(spread) + tuple(swapped)
        self.outs = [((4,) + one.shape, BF) for one in spread] + [(one.shape, BF) for one in swapped]
        self.keeps = [(one.shape, BF) for one in spread] + [(one.shape[1:], BF) for one in swapped]

    def peers(self, at):
        x, z, y_lo, y_hi, core = at
        return [device(x, z, 1 - y_lo, 1 - y_hi, 1 - core), *group_places(at)]

    def start(self, net, ins, outs, at):
        x, z, y_lo, y_hi, core = at
        crossed, sibling, partner = self.peers(at)
        shard = y_hi * 2 + core
        far = (1 - y_hi) * 2
        for mine, whole in zip(ins[self.count :], outs[self.count :]):
            net.send(mine.at[far + core], whole.at[shard], partner)
            net.send(mine.at[far + 1 - core], whole.at[shard], crossed)
            net.send(mine.at[y_hi * 2 + 1 - core], whole.at[shard], sibling)
        self.spreads = []
        for mine, whole in zip(ins, outs[: self.count]):
            self.spreads.append(Spread())
            self.spreads[-1].start(net, mine, whole, at)
        for mine, whole in zip(ins[self.count :], outs[self.count :]):
            net.keep(mine.at[shard], whole.at[shard])

    def forward(self, net, outs, at):
        for one, whole in zip(self.spreads, outs):
            one.forward(net, whole, at)


class Forward:
    def __init__(self, behind, ahead):
        self.inputs = tuple(behind) + tuple(ahead)
        self.outs = [(one.shape[1:], BF) for one in self.inputs]
        self.keeps = []

    def peers(self, at):
        return []

    def start(self, net, ins, outs, at):
        for part, (plus, minus) in enumerate((x_next(at), z_next(at))):
            net.send(ins[part].at[0], outs[part], plus)
            net.send(ins[2 + part].at[1], outs[2 + part], minus)

    def forward(self, net, outs, at):
        pass


class Hand:
    def __init__(self, piece, columns, split):
        self.columns, self.cell, self.split = columns, columns // 4, split
        self.inputs = (piece,)
        self.outs = [((2, 2, STRIP, columns), BF)] * 2 if split else [((2, 2, SHARD, columns), BF)]
        self.keeps = [((2, STRIP, columns // 4), BF)] * 2

    def peers(self, at):
        x, z, y_lo, y_hi, core = at
        return [device(x, z, 1 - y_lo, y_hi, core)] + x_next(at) + z_next(at)

    def strip(self, outs, at, part, high, low, j):
        cut = pl.ds(pl.multiple_of(j * self.cell, 128), self.cell)
        if self.split:
            return outs[part].at[high, low, :, cut]
        start = pl.multiple_of(part * PART + at[part] * STRIP, 16)
        return outs[0].at[high, low, pl.ds(start, STRIP), cut]

    def start(self, net, ins, outs, at):
        (mine,) = ins
        self.near = []
        for part in (0, 1):
            spot = self.strip(outs, at, part, slice(None), at[2], at[1 - part])
            self.near.append(net.send(mine.at[:, part], spot, self.peers(at)[0]))
            net.keep(mine.at[:, part], spot)

    def forward(self, net, outs, at):
        sides = (x_next(at), z_next(at))
        rings = []
        for part in (0, 1):
            net.arrived(self.near[part])

            def halves(origin, half, part=part):
                return [self.strip(outs, at, part, half, slice(None), origin)]

            rings.append(Ring(net, halves, at[1 - part], sides[1 - part]).start())
        for ring in rings:
            ring.forward()
        if self.split:
            return
        far_rings = []
        for part in (0, 1):
            rings[part].finish()

            def halves(origin, half, part=part):
                start = pl.multiple_of(part * PART + origin * STRIP, 16)
                return [outs[0].at[half, :, pl.ds(start, STRIP), :]]

            far_rings.append(Ring(net, halves, at[part], sides[part]).start())
        for ring in far_rings:
            ring.forward()


def sum_step(sums, number, name, extras=()):
    count = len(sums)
    steps = [step for _, _, step in sums]

    def body(net, ins, outs):
        at = place()
        x, z, y_lo, y_hi, core = at
        peers = []
        if any(step < 2 for step in steps):
            peers += x_peers(at) + z_peers(at)
        column = any(step == 2 and isinstance(one, GradSum) for one, _, step in sums)
        if column:
            for k in range(1, 8):
                peers.append(device(x, z, (y_lo + k // 4) % 2, (y_hi + (k // 2) % 2) % 2, (core + k) % 2))
        elif any(step == 2 for step in steps) and not extras:
            peers.append(device(x, z, 1 - y_lo, y_hi, core))
        for extra in extras:
            peers += extra.peers(at)
        net.greet(peers)
        at_in = at_out = count
        spans = []
        for extra in extras:
            spans.append((at_in, at_in + len(extra.inputs), at_out, at_out + len(extra.outs)))
            at_in, at_out = spans[-1][1], spans[-1][3]
        for (one, _, step), whole, got in zip(sums, ins, outs):
            (one.first, one.second, one.third)[step](net, whole, got, at)
        for extra, (a, b, c, d) in zip(extras, spans):
            extra.start(net, ins[a:b], outs[c:d], at)
        net.done(net.settle())
        for extra, (a, b, c, d) in zip(extras, spans):
            extra.forward(net, outs[c:d], at)

    came = exchange(
        body,
        tuple(array for _, array, _ in sums) + tuple(one for extra in extras for one in extra.inputs),
        [one.shapes[step] for one, _, step in sums] + [out for extra in extras for out in extra.outs],
        6 * count + 30 * len(extras),
        [keep for one, _, step in sums for keep in one.keeps[step]] + [keep for extra in extras for keep in extra.keeps],
        number,
        name,
    )
    total = []
    for (one, _, step), got in zip(sums, came):
        if isinstance(one, LossSum):
            total.append(jnp.sum(got, axis=0))
        else:
            total.append(add_up(got, 1 if step < 2 else 0))
    return total + list(came[count:])


SPANS = 16
BLOCK = SPANS * SPAN
QUERIES = GROUPS * SPAN
SMEM = pl.BlockSpec(memory_space=pltpu.SMEM)
VMEM = pl.BlockSpec(memory_space=pltpu.VMEM)
LOW = 32
FIRST = 2


def local_call(kernel, args, outs, name, flops, specs=None, out_specs=None, grid=None, scratch=(), limit=60):
    moved = sum(math.prod(arg.shape) * arg.dtype.itemsize for arg in args)
    moved += sum(math.prod(shape) * jnp.dtype(kind).itemsize for shape, kind in outs)
    extra = {} if grid is None else {"grid": grid}
    return pl.pallas_call(
        kernel,
        out_shape=[jax.ShapeDtypeStruct(shape, kind) for shape, kind in outs],
        in_specs=specs or [VMEM] * len(args),
        out_specs=out_specs or [VMEM] * len(outs),
        scratch_shapes=[pltpu.VMEM(shape, kind) for shape, kind in scratch],
        compiler_params=pltpu.CompilerParams(vmem_limit_bytes=limit << 20),
        cost_estimate=pl.CostEstimate(flops=flops // 1000, transcendentals=0, bytes_accessed=moved // 1000),
        name=name,
        **extra,
    )(*args)


def inverse_root(values):
    return lax.rsqrt(jnp.mean(values * values, axis=-1, keepdims=True) + EPS)


def norm_back(values, gain, grad):
    inv = inverse_root(values)
    scaled = gain * grad
    return inv * (scaled - values * (inv * inv) * jnp.mean(scaled * values, axis=-1, keepdims=True))


def turn(values, cosine, sine):
    return values * cosine + pltpu.roll(values, HD // 2, 1) * sine


def head(index):
    return slice(index * HD, (index + 1) * HD)


def stack_heads(ref, span, kv):
    rows = slice(span * SPAN, (span + 1) * SPAN)
    return jnp.concatenate([ref[rows, head(kv * GROUPS + g)] for g in range(GROUPS)], axis=0)


def unstack_heads(ref, span, kv, values):
    rows = slice(span * SPAN, (span + 1) * SPAN)
    for g in range(GROUPS):
        ref[rows, head(kv * GROUPS + g)] = values[g * SPAN : (g + 1) * SPAN, :]


def expert_lanes():
    return lax.broadcasted_iota(jnp.int32, (1, HD), 1)


def wide_router(small_ref):
    rows = small_ref[...]
    number = lax.broadcasted_iota(jnp.int32, rows.shape, 0)
    rows = jnp.where((number >= FIRST) & (number < FIRST + E), rows.astype(F32), 0.0).astype(BF)
    gap = jnp.zeros((16, D), BF)
    return jnp.concatenate([rows, gap, rows, gap, gap, gap, gap, gap], axis=0)


def chosen(routes):
    lanes = expert_lanes()
    number = jnp.where(lanes >= LOW, lanes - LOW, lanes) - FIRST
    total = jnp.zeros((ROWS, HD), F32)
    for slot in range(4):
        total = total + jnp.where(routes[:, slot : slot + 1] == number, 1.0, 0.0)
    return total


def in_two(values):
    high = values.astype(BF).astype(F32)
    return jnp.where(expert_lanes() < LOW, high, values - high).astype(BF)


def project_kernel(
    spans, tokens, small, w_query, w_key, w_value, normed, query, keys_values, cosine, sine
):
    lanes = lax.broadcasted_iota(jnp.int32, (SPAN, HD), 1)
    offsets = lax.broadcasted_iota(jnp.int32, (SPAN, HD), 0)
    half_size = HD // 2
    steps = jnp.where(lanes >= half_size, lanes - half_size, lanes).astype(F32)
    frequency = jnp.exp(-(steps * 2.0 / HD) * math.log(BASE))
    for s in range(2):
        rows = slice(s * SPAN, (s + 1) * SPAN)
        angles = (spans[s] * SPAN + offsets).astype(F32) * frequency
        cosine[rows, :] = jnp.cos(angles)
        turned = jnp.sin(angles)
        sine[rows, :] = jnp.where(lanes >= half_size, turned, -turned)
    inputs = tokens[...].astype(F32)
    gain = small[...].astype(F32)[0:1, :]
    normed[...] = (inputs * inverse_root(inputs) * gain).astype(BF)
    rows = normed[...]
    cos, sin = cosine[...], sine[...]
    raw = jnp.dot(rows, w_key[...], preferred_element_type=F32)
    for k in range(KV):
        keys_values[:, head(k)] = turn(raw[:, head(k)], cos, sin).astype(BF)
    keys_values[:, KV * HD :] = jnp.dot(rows, w_value[...], preferred_element_type=F32).astype(BF)
    for k in range(0, H, 4):
        raw = jnp.dot(rows, w_query[:, k * HD : (k + 4) * HD], preferred_element_type=F32)
        for j in range(4):
            query[:, head(k + j)] = turn(raw[:, head(j)], cos, sin).astype(BF)


def project(*args):
    outs = [((ROWS, D), BF), ((ROWS, H * HD), BF), ((ROWS, 2 * KV * HD), BF), ((ROWS, HD), F32), ((ROWS, HD), F32)]
    return local_call(project_kernel, args, outs, "project", 800_000_000, specs=[SMEM] + [VMEM] * 5)


def combine_kernel(mixed, hidden, teacher, valid, count, result, d_result, d_low, squared):
    total = hidden[...] + (mixed[0].astype(F32) + mixed[1].astype(F32) + mixed[2].astype(F32))
    result[...] = total.astype(BF)
    error = total - teacher[...].astype(F32)
    valid_rows = valid[...].astype(F32).T
    squared[...] = jnp.full((8, 128), jnp.sum(valid_rows * error * error), F32)
    norm_factor = jnp.full((1, 1), count[0], jnp.int32).astype(F32) * D
    grad = 2.0 * valid_rows * error / norm_factor
    d_result[...] = grad
    d_low[...] = grad.astype(BF)


def combine(*args):
    outs = [((ROWS, D), BF), ((ROWS, D), F32), ((ROWS, D), BF), ((8, 128), F32)]
    return local_call(combine_kernel, args, outs, "combine", 1000, specs=[VMEM] * 4 + [SMEM])


def tail_kernel(normed, d_qkv, attended, d_attn, normed_two, d_router, out):
    for shard in range(4):
        columns = slice(shard * SHARD, (shard + 1) * SHARD)
        out[shard, :, :512] = tn(normed[:, columns], d_qkv[...]).astype(BF)
        out[shard, :, 512 : 512 + SHARD] = tn(attended[:, columns], d_attn[...]).astype(BF)
        out[shard, :, 512 + SHARD :] = tn(normed_two[:, columns], d_router[...]).astype(BF)


def tail_grads(*args):
    return local_call(tail_kernel, args, [((4, SHARD, TAIL), BF)], "tail_grads", 1000)[0]


def nt(a, b):
    return lax.dot_general(a, b, (((1,), (1,)), ((), ())), preferred_element_type=F32)


def tn(a, b):
    return lax.dot_general(a, b, (((0,), (0,)), ((), ())), preferred_element_type=F32)


def block_rows(where, b, ref):
    return jnp.concatenate(
        [ref[pl.ds(pl.multiple_of(where[b * SPANS + i] * SPAN, SPAN), SPAN), :] for i in range(SPANS)], axis=0
    )


def lead_of_keys():
    keys = lax.broadcasted_iota(jnp.int32, (BLOCK, QUERIES), 0)
    queries = lax.broadcasted_iota(jnp.int32, (BLOCK, QUERIES), 1)
    return keys - queries % SPAN


def attend_kernel(
    where, spans, q_ref, kv_ref, tokens, w_out, small, routes, o_ref, low_ref, lse_ref, hidden_ref, normed_ref, gates_ref, probs_ref
):
    lead = lead_of_keys()
    for s in range(2):
        span = spans[s]
        stacked = [stack_heads(q_ref, s, kv) for kv in range(KV)]

        def body(b, carry, last=False):
            keys_values = block_rows(where, b, kv_ref)
            out = []
            for kv in range(KV):
                top, total, acc = carry[kv]
                keys = keys_values[:, head(kv)]
                values = keys_values[:, head(KV + kv)]
                logits = nt(keys, stacked[kv])
                if last:
                    logits = jnp.where(lead <= span * SPAN - b * BLOCK, logits, NEGATIVE)
                new_top = jnp.maximum(top, jnp.max(logits, axis=0, keepdims=True))
                weights = jnp.exp2((logits - new_top) * SCALE_2)
                shrink = jnp.exp2((top - new_top) * SCALE_2)
                total = total * shrink + jnp.sum(weights, axis=0, keepdims=True)
                acc = acc * shrink + tn(values, weights.astype(BF))
                out.append((new_top, total, acc))
            return tuple(out)

        start = tuple(
            (
                jnp.full((1, QUERIES), NEGATIVE, F32),
                jnp.zeros((1, QUERIES), F32),
                jnp.zeros((HD, QUERIES), F32),
            )
            for _ in range(KV)
        )
        final = body(span // SPANS, lax.fori_loop(0, span // SPANS, body, start), last=True)
        for kv in range(KV):
            top, total, acc = final[kv]
            unstack_heads(o_ref, s, kv, (acc / total).T)
            lse_ref[2 * s + kv : 2 * s + kv + 1, :] = top * SCALE_2 + jnp.log(total) * LOG2_E
    lse_ref[4:8, :] = jnp.zeros((4, QUERIES), F32)

    low_ref[...] = o_ref[...].astype(BF)
    for start in range(0, D, 512):
        columns = slice(start, start + 512)
        hidden_ref[:, columns] = tokens[:, columns].astype(F32) + jnp.dot(
            low_ref[...], w_out[:, columns], preferred_element_type=F32
        )
    hidden = hidden_ref[...]
    gain = small[...].astype(F32)[1:2, :]
    normed = (hidden * inverse_root(hidden) * gain).astype(BF)
    normed_ref[...] = normed
    logits = nt(normed, wide_router(small))
    lanes = expert_lanes()
    first = (lanes >= FIRST) & (lanes < FIRST + E)
    second = (lanes >= FIRST + LOW) & (lanes < FIRST + LOW + E)
    top = jnp.max(jnp.where(first, logits, NEGATIVE), axis=1, keepdims=True)
    weights = jnp.where(first | second, jnp.exp(logits - top), 0.0)
    probs = weights / jnp.sum(jnp.where(first, weights, 0.0), axis=1, keepdims=True)
    probs_ref[...] = probs
    gates_ref[...] = in_two(probs * chosen(routes))


def attend(*args):
    outs = [
        ((ROWS, H * HD), F32),
        ((ROWS, H * HD), BF),
        ((8, QUERIES), F32),
        ((ROWS, D), F32),
        ((ROWS, D), BF),
        ((ROWS, HD), BF),
        ((ROWS, HD), F32),
    ]
    return local_call(attend_kernel, args, outs, "attend", 2_400_000_000, specs=[SMEM, SMEM] + [VMEM] * 6)


GELU = math.sqrt(2.0 / math.pi)


def gate_column(gates, place_ref, h):
    lane = FIRST + (place_ref[0] * 3 + h) // 2
    lanes = expert_lanes()
    here = (lanes == lane) | (lanes == lane + LOW)
    return jnp.sum(jnp.where(here, gates, 0.0), axis=1, keepdims=True)


def experts_kernel(place_ref, rows, gates, w_both, w_down, mixed, made_ref, active_ref, steep_ref, total):
    h = pl.program_id(0)
    raw = jnp.dot(rows[...], w_both[...], preferred_element_type=F32)
    gate, up = raw[:, :HALF], raw[:, HALF:]
    squared = gate * gate
    inner = jnp.tanh(GELU * gate * (1.0 + 0.044715 * squared))
    active = 0.5 * gate * (1.0 + inner)
    slope = 0.5 * (1.0 + inner) + 0.5 * gate * (1.0 - inner * inner) * (GELU + 3 * 0.044715 * GELU * squared)
    made = active * up
    made_ref[...] = made.astype(BF)
    active_ref[...] = active.astype(BF)
    steep_ref[...] = (slope * up).astype(BF)
    weighted = (gate_column(gates[...].astype(F32), place_ref, h) * made).astype(BF)
    out = jnp.dot(weighted, w_down[...], preferred_element_type=F32)

    @pl.when(h == 0)
    def _():
        total[...] = out

    @pl.when(h == 1)
    def _():
        total[...] += out

    @pl.when(h == 2)
    def _():
        mixed[...] = (total[...] + out).astype(BF)


def whole(shape):
    return pl.BlockSpec(shape, lambda h: (0,) * len(shape))


def experts(place_here, rows, gates, wide, low):
    count = 4 * ROWS
    return local_call(
        experts_kernel,
        (place_here, rows, gates, wide, low),
        [((count, D), BF)] + [((count, SLICE), BF)] * 3,
        "experts",
        5_400_000_000,
        specs=[
            SMEM,
            whole((count, D)),
            whole((count, HD)),
            pl.BlockSpec((D, 2 * HALF), lambda h: (0, h)),
            pl.BlockSpec((HALF, D), lambda h: (h, 0)),
        ],
        out_specs=[whole((count, D))] + [pl.BlockSpec((count, HALF), lambda h: (0, h))] * 3,
        grid=(3,),
        scratch=[((count, D), F32)],
    )


def experts_back_kernel(
    place_ref, rows, d_rows, gates, made_ref, active_ref, steep_ref, w_both, w_down, d_normed, gates_sent, *rest
):
    chunks, (total, strip, rows_t, d_rows_t, d_gates) = rest[:10], rest[10:]
    h = pl.program_id(0)

    @pl.when(h == 0)
    def _():
        rows_t[...] = rows[...].T
        d_rows_t[...] = d_rows[...].T

    back = nt(d_rows[...], w_down[...])
    made = made_ref[...].astype(F32)
    weight = gate_column(gates[...].astype(F32), place_ref, h)
    lane = FIRST + (place_ref[0] * 3 + h) // 2
    lanes = expert_lanes()
    here = (lanes == lane) | (lanes == lane + LOW)
    d_weight = jnp.where(here, jnp.sum(made * back, axis=1, keepdims=True), 0.0)
    d_made = weight * back
    d_gate = (d_made * steep_ref[...].astype(F32)).astype(BF)
    d_up = (d_made * active_ref[...].astype(F32)).astype(BF)
    weighted = (weight * made).astype(BF)
    d_raw = jnp.concatenate([d_gate, d_up], axis=1)
    out = nt(d_raw, w_both[...])

    @pl.when(h == 0)
    def _():
        total[...] = out
        d_gates[...] = d_weight

    @pl.when(h != 0)
    def _():
        d_gates[...] += d_weight

    @pl.when(h == 1)
    def _():
        total[...] += out

    @pl.when(h == 2)
    def _():
        d_normed[...] = (total[...] + out).astype(BF)
        gates_sent[...] = in_two(d_gates[...])

    for shard in range(4):
        columns = slice(shard * SHARD, (shard + 1) * SHARD)
        strip[:, : 2 * HALF] = jnp.dot(rows_t[columns, :], d_raw, preferred_element_type=F32).astype(BF)
        strip[:, 2 * HALF :] = jnp.dot(d_rows_t[columns, :], weighted, preferred_element_type=F32).astype(BF)
        for part in (0, 1):
            for n, k in enumerate((0, 1, 3, 2)):
                start = part * PART + ((place_ref[1 + part] + k) % 4) * STRIP
                chunk = chunks[part * 5 + n + (shard // 2 if k == 2 else 0)]
                chunk[shard % 2 if k == 2 else shard] = strip[pl.ds(pl.multiple_of(start, 16), STRIP), :]


def experts_back(place_here, rows, d_rows, gates, made, active, steep, wide, low):
    count = 4 * ROWS
    column = pl.BlockSpec((count, HALF), lambda h: (0, h))
    return local_call(
        experts_back_kernel,
        (place_here, rows, d_rows, gates, made, active, steep, wide, low),
        [((count, D), BF), ((count, HD), BF)] + ([((4, STRIP, WIDE), BF)] * 3 + [((2, STRIP, WIDE), BF)] * 2) * 2,
        "experts_back",
        10_800_000_000,
        specs=[
            SMEM,
            whole((count, D)),
            whole((count, D)),
            whole((count, HD)),
            column,
            column,
            column,
            pl.BlockSpec((D, 2 * HALF), lambda h: (0, h)),
            pl.BlockSpec((HALF, D), lambda h: (h, 0)),
        ],
        out_specs=[whole((count, D)), whole((count, HD))]
        + (
            [pl.BlockSpec((4, STRIP, 3 * HALF), lambda h: (0, 0, h))] * 3
            + [pl.BlockSpec((2, STRIP, 3 * HALF), lambda h: (0, 0, h))] * 2
        )
        * 2,
        grid=(3,),
        scratch=[((count, D), F32), ((SHARD, SLICE), BF), ((D, count), BF), ((D, count), BF), ((count, HD), F32)],
    )


def attend_back_kernel(
    where,
    spans,
    q_ref,
    kv_ref,
    o_ref,
    lse_ref,
    cosine,
    sine,
    w_out,
    small,
    routes,
    probs_ref,
    hidden_ref,
    d_result,
    two_parts,
    gate_parts,
    d_hidden_ref,
    d_attn_ref,
    d_router_ref,
    dq_ref,
    dkv_ref,
    acc_ref,
    do_ref,
    turned_ref,
):
    d_gates = gate_parts[0].astype(F32) + gate_parts[1].astype(F32) + gate_parts[2].astype(F32)
    lanes = expert_lanes()
    first = (lanes >= FIRST) & (lanes < FIRST + E)
    d_select = jnp.where(first, (d_gates + pltpu.roll(d_gates, HD - LOW, 1)) * chosen(routes), 0.0)
    probs = jnp.where(first, probs_ref[...], 0.0)
    d_router = (probs * (d_select - jnp.sum(probs * d_select, axis=1, keepdims=True))).astype(BF)
    d_router_ref[...] = d_router
    d_normed = two_parts[0].astype(F32) + two_parts[1].astype(F32) + two_parts[2].astype(F32)
    d_normed = d_normed + jnp.dot(d_router, wide_router(small), preferred_element_type=F32)
    gain = small[...].astype(F32)[1:2, :]
    d_hidden = d_result[...] + norm_back(hidden_ref[...], gain, d_normed)
    d_hidden_ref[...] = d_hidden
    d_attn = d_hidden.astype(BF)
    for f in range(4):
        d_attn_ref[f] = d_attn[:, f * SHARD : (f + 1) * SHARD]
    for start in range(0, H * HD, 512):
        columns = slice(start, start + 512)
        do_ref[:, columns] = nt(d_attn, w_out[columns, :]).astype(BF)

    lead = lead_of_keys()
    acc_ref[...] = jnp.zeros_like(acc_ref)
    for s in range(2):
        span = spans[s]
        stacked = [stack_heads(q_ref, s, kv) for kv in range(KV)]
        d_out = [stack_heads(do_ref, s, kv) for kv in range(KV)]
        delta = [
            jnp.sum((d_out[kv].astype(F32) * stack_heads(o_ref, s, kv)).T, axis=0, keepdims=True) for kv in range(KV)
        ]
        lse = [lse_ref[2 * s + kv : 2 * s + kv + 1, :] for kv in range(KV)]

        def body(b, carry, last=False):
            keys_values = block_rows(where, b, kv_ref)
            out, key_grads, value_grads = [], [], []
            for kv in range(KV):
                keys = keys_values[:, head(kv)]
                values = keys_values[:, head(KV + kv)]
                weights = jnp.exp2(nt(keys, stacked[kv]) * SCALE_2 - lse[kv])
                if last:
                    weights = jnp.where(lead <= span * SPAN - b * BLOCK, weights, 0.0)
                d_weights = nt(values, d_out[kv])
                d_logits = (weights * (d_weights - delta[kv])).astype(BF)
                out.append(carry[kv] + tn(keys, d_logits))
                key_grads.append(jnp.dot(d_logits, stacked[kv], preferred_element_type=F32) * SCALE)
                value_grads.append(jnp.dot(weights.astype(BF), d_out[kv], preferred_element_type=F32))
            grads = jnp.concatenate(key_grads + value_grads, axis=1)
            for i in range(SPANS):
                rows = pl.ds(pl.multiple_of(where[b * SPANS + i] * SPAN, SPAN), SPAN)
                acc_ref[rows, :] += grads[i * SPAN : (i + 1) * SPAN, :]
            return tuple(out)

        start = tuple(jnp.zeros((HD, QUERIES), F32) for _ in range(KV))
        final = body(span // SPANS, lax.fori_loop(0, span // SPANS, body, start), last=True)
        for kv in range(KV):
            unstack_heads(turned_ref, s, kv, (final[kv] * SCALE).T)
    for k in range(H):
        dq_ref[:, head(k)] = turn(turned_ref[:, head(k)], cosine[...], -sine[...]).astype(BF)

    def put(i, carry):
        rows = pl.ds(pl.multiple_of(i * 256, 256), 256)
        dkv_ref[rows, :] = acc_ref[rows, :].astype(BF)
        return carry

    lax.fori_loop(0, acc_ref.shape[0] // 256, put, 0)


def attend_back(*args):
    length = args[3].shape[0]
    outs = [
        ((ROWS, D), F32),
        ((4, ROWS, SHARD), BF),
        ((ROWS, HD), BF),
        ((ROWS, H * HD), BF),
        ((length, 2 * KV * HD), BF),
    ]
    return local_call(
        attend_back_kernel,
        args,
        outs,
        "attend_back",
        5_000_000_000,
        specs=[SMEM, SMEM] + [VMEM] * 14,
        scratch=[((length, 2 * KV * HD), F32), ((ROWS, H * HD), BF), ((ROWS, H * HD), F32)],
    )


def blocks_kernel(dq_ref, keys, cosine, sine, blocks):
    for f in range(3):
        blocks[f] = dq_ref[:, f * 512 : (f + 1) * 512]
    for k in range(KV):
        turned = turn(keys[0, :, head(k)].astype(F32), cosine[...], -sine[...])
        blocks[3, :, head(k)] = turned.astype(BF)
    blocks[3, :, KV * HD :] = keys[1]


def query_blocks(*args):
    return local_call(blocks_kernel, args, [((4, ROWS, 512), BF)], "query_blocks", 1_000_000)[0]


def inputs_kernel(blocks, w_query, w_key, w_value, tokens, small, d_hidden, out):
    gain = small[...].astype(F32)[0:1, :]
    d_normed = nt(blocks[3, :, : KV * HD], w_key[...]) + nt(blocks[3, :, KV * HD :], w_value[...])
    for f in range(3):
        d_normed = d_normed + nt(blocks[f], w_query[:, f * 512 : (f + 1) * 512])
    out[...] = d_hidden[...] + norm_back(tokens[...].astype(F32), gain, d_normed)


def input_grads(*args):
    return local_call(inputs_kernel, args, [((ROWS, D), F32)], "input_grads", 800_000_000)[0]


def lay_out_kernel(place_ref, *refs):
    pieces = refs[:10]
    w_gate, w_up, w_router, router, gain, gate_out, up_out, down_out, gain_out, turned, sum_ref = refs[10:]
    own_set = pl.program_id(0) // 3
    for part in (0, 1):
        for n, k in enumerate((0, 1, 3, 2)):
            start = part * PART + ((place_ref[1 + part] + 4 - k) % 4) * STRIP
            rows = pl.ds(pl.multiple_of(start, 16), STRIP)
            for kind, out in enumerate((gate_out.at[0], up_out.at[0], turned)):
                columns = slice(kind * HALF, (kind + 1) * HALF)
                piece = pieces[part * 5 + n][0, :, columns]
                if k == 2:
                    piece = jnp.where(own_set < 2, piece, pieces[part * 5 + 4][0, :, columns])
                out[rows, :] = piece.astype(F32)
    down_out[0] = turned[...].T
    both = w_gate[0].astype(F32) * gate_out[0] + w_up[0].astype(F32) * up_out[0]
    row_sum = jnp.sum(both, axis=1, keepdims=True)

    @pl.when(pl.program_id(0) == 0)
    def _():
        sum_ref[...] = row_sum

    @pl.when(pl.program_id(0) != 0)
    def _():
        sum_ref[...] += row_sum

    @pl.when(pl.program_id(0) == 11)
    def _():
        total = sum_ref[...] + jnp.sum(w_router[...].astype(F32) * router[...], axis=1, keepdims=True)
        gain_out[...] = total.T / gain[...].astype(F32)


def lay_out_experts(place_here, pieces, w_gate, w_up, w_router, router, gain):
    wide = pl.BlockSpec((1, SHARD, HALF), lambda n: (n // 2, 0, n % 2))
    return local_call(
        lay_out_kernel,
        (place_here,) + tuple(pieces) + (w_gate, w_up, w_router, router, gain),
        [((E, SHARD, FF), F32), ((E, SHARD, FF), F32), ((E, FF, SHARD), F32), ((1, SHARD), F32)],
        "lay_out_experts",
        20_000_000,
        specs=[SMEM]
        + (
            [pl.BlockSpec((1, STRIP, SLICE), lambda n: (n // 3, 0, n % 3))] * 3
            + [pl.BlockSpec((1, STRIP, SLICE), lambda n: (n // 3 % 2, 0, n % 3))] * 2
        )
        * 2
        + [wide, wide, whole((SHARD, E)), whole((SHARD, E)), whole((1, SHARD))],
        out_specs=[
            wide,
            wide,
            pl.BlockSpec((1, HALF, SHARD), lambda n: (n // 2, n % 2, 0)),
            whole((1, SHARD)),
        ],
        grid=(12,),
        scratch=[((SHARD, HALF), F32), ((SHARD, 1), F32)],
    )


def attention_kernel(tail, w_query, w_key, w_value, gain, query, key, value, out, router, gain_out):
    total = jnp.zeros((SHARD, 1), F32)
    for f in range(3):
        columns = slice(f * 512, (f + 1) * 512)
        piece = tail[f, :, :512].astype(F32)
        query[:, columns] = piece
        total = total + jnp.sum(w_query[:, columns].astype(F32) * piece, axis=1, keepdims=True)
    for ref, weight, columns in ((key, w_key, slice(0, 256)), (value, w_value, slice(256, 512))):
        piece = tail[3, :, columns].astype(F32)
        ref[...] = piece
        total = total + jnp.sum(weight[...].astype(F32) * piece, axis=1, keepdims=True)
    gain_out[...] = total.T / gain[...].astype(F32)
    for f in range(4):
        out[:, f * SHARD : (f + 1) * SHARD] = tail[f, :, 512 : 512 + SHARD].astype(F32)
    pieces = [tail[f, :, 512 + SHARD :].astype(F32) for f in range(4)]
    router[...] = (pieces[0] + pieces[1] + pieces[2] + pieces[3])[:, FIRST : FIRST + E]


def lay_out_attention(*args):
    outs = [((SHARD, width), F32) for width in (D, KV * HD, KV * HD, D, E)] + [((1, SHARD), F32)]
    return local_call(attention_kernel, args, outs, "lay_out_attention", 4_000_000)


def add_halves_kernel(*refs):
    for n in range(4):
        refs[8 + n][...] = (refs[n][...].astype(F32) + refs[4 + n][...].astype(F32)).astype(BF)


def add_halves(blocks, halves):
    cell = WIDE // 4
    specs = [pl.BlockSpec((2, STRIP, cell), lambda n, side=side: (side, 0, n)) for side in (0, 1, 0, 1)]
    half_spec = pl.BlockSpec((2, STRIP, cell), lambda n: (0, 0, n))
    return pl.pallas_call(
        add_halves_kernel,
        out_shape=[jax.ShapeDtypeStruct(block.shape, BF) for block in blocks],
        grid=(4,),
        in_specs=specs + [half_spec] * 4,
        out_specs=specs,
        input_output_aliases={n: n for n in range(4)},
        compiler_params=pltpu.CompilerParams(vmem_limit_bytes=32 << 20),
        cost_estimate=pl.CostEstimate(flops=1000, transcendentals=0, bytes_accessed=1000),
        name="add_halves",
    )(*blocks, *halves)


def shift_pairs(axis, k):
    pairs = []
    for ctx in range(32):
        x, z, y_lo = ctx // 8, (ctx // 2) % 4, ctx % 2
        if axis == 0:
            pairs.append((ctx, (x + k) % 4 * 8 + z * 2 + y_lo))
        else:
            pairs.append((ctx, x * 8 + (z + k) % 4 * 2 + y_lo))
    return pairs


def shift(array, axis, k):
    return lax.ppermute(array, "ctx", shift_pairs(axis, k))


def local(
    tokens,
    teacher,
    valid_mask,
    token_count,
    routes,
    span_order,
    w_query,
    w_key,
    w_value,
    w_out,
    norm_gain,
    w_router,
    moe_gain,
    w_gate,
    w_up,
    w_down,
):
    rows = tokens[0]
    ctx = lax.axis_index("ctx")
    shard = lax.axis_index("fsdp")
    x, z, _, _, _ = place()
    place_here = jnp.stack([shard, x, z])
    spans = lax.dynamic_slice(span_order, (ctx * 2,), (2,))
    numbers = jnp.arange(64, dtype=jnp.int32)
    where = jnp.sum(jnp.where(span_order[None, :] == numbers[:, None], numbers[None, :], 0), axis=1)

    small = jnp.concatenate(
        [norm_gain[None, :], moe_gain[None, :], w_router.T, jnp.zeros((16 - 2 - E, SHARD), BF)], axis=0
    )
    full_query, full_key, full_value, full_out, small = gather_attention_weights(
        (w_query, w_key, w_value, w_out), small, 1
    )
    input_one, query, keys_values, cosine, sine = project(spans, rows, small, full_query, full_key, full_value)
    keys, quarters = gather_keys(keys_values, (w_gate, w_up, w_down), 2)
    keys = keys.reshape(32 * ROWS, 2 * KV * HD)
    attended, attended_low, lse, hidden, input_two, gates_sent, probs = attend(
        where, spans, query, keys, rows, full_out, small, routes[0]
    )

    group_two, gates, wide, low = group_spread(
        (input_two, gates_sent), 3, "group_normed", (w_gate, w_up, w_down, quarters)
    )
    group_two, gates = group_two.reshape(4 * ROWS, D), gates.reshape(4 * ROWS, HD)
    mixed, *kept = experts(place_here, group_two, gates, wide, low)
    (mixed,) = group_sum((mixed.reshape(4, ROWS, D),), 4, "group_mixture")
    result, d_result, d_low, squared = combine(mixed, hidden, teacher[0], valid_mask, token_count)
    (group_d,) = group_spread((d_low,), 5, "group_d_result")
    d_two, d_gates_sent, *chunks = experts_back(
        place_here, group_two, group_d.reshape(4 * ROWS, D), gates, *kept, wide, low
    )
    halfway = [shift(chunks[part * 5 + 3 + n], part, (1, 3)[n]) for n in (0, 1) for part in (0, 1)]
    two_parts, gate_parts, squared = group_sum(
        (d_two.reshape(4, ROWS, D), d_gates_sent.reshape(4, ROWS, HD)), 6, "group_d_normed", squared
    )
    squared = jnp.sum(squared, axis=0)
    halfway, two_parts = lax.optimization_barrier((halfway, two_parts))
    sums = add_halves(
        (chunks[1], chunks[2], chunks[6], chunks[7]), (halfway[0], halfway[2], halfway[1], halfway[3])
    )
    came = [[chunks[part * 5], shift(sums[part * 2], part, 1), shift(sums[part * 2 + 1], part, 3)] for part in (0, 1)]
    d_hidden, d_attn_blocks, d_router, d_query, d_keys = attend_back(
        where,
        spans,
        query,
        keys,
        attended,
        lse,
        cosine,
        sine,
        full_out,
        small,
        routes[0],
        probs,
        hidden,
        d_result,
        two_parts,
        gate_parts,
    )

    expert_sum, tail_sum, key_sum, loss_sum = GradSum(WIDE), GradSum(TAIL), KeySum(), LossSum()
    came, d_keys = lax.optimization_barrier((came, d_keys))
    part = add_strips(came[0] + came[1])
    share = GroupShare((attended_low, input_one), (d_attn_blocks,))
    part, d_keys, squared, group_attended, group_one, group_d_attn = sum_step(
        (
            (expert_sum, part, 1),
            (key_sum, d_keys.reshape(4, 4, 2, ROWS, 2 * KV * HD), 0),
            (loss_sum, squared, 0),
        ),
        7,
        "sums_first",
        (share,),
    )
    part, d_keys, squared = sum_step(
        ((expert_sum, part, 2), (key_sum, d_keys, 1), (loss_sum, squared, 1)), 8, "sums_second"
    )
    d_keys, squared, *strips = sum_step(
        ((key_sum, d_keys, 2), (loss_sum, squared, 2)), 9, "sums_third", (Hand(part, WIDE, True),)
    )
    pieces = [[strips[part], shift(strips[part], part, 1), shift(strips[part], part, 3)] for part in (0, 1)]
    norm_factor = token_count[0].astype(F32) * D
    loss_value = (squared[0, 0] / norm_factor).reshape(1)

    blocks = query_blocks(d_query, d_keys, cosine, sine)
    (group_d_qkv,) = sum_step((), 10, "group_d_qkv", (GroupShare((), (blocks,)),))
    tail = tail_grads(
        group_one.reshape(4 * ROWS, D),
        group_d_qkv.reshape(4 * ROWS, 512),
        group_attended.reshape(4 * ROWS, D),
        group_d_attn.reshape(4 * ROWS, SHARD),
        input_two,
        d_router,
    )
    d_inputs = input_grads(blocks, full_query, full_key, full_value, rows, small, d_hidden)
    pieces, tail, d_inputs = lax.optimization_barrier((pieces, tail, d_inputs))
    tail, *halves = sum_step(
        ((tail_sum, tail, 0),), 11, "tail_a", (Forward([pieces[0][1], pieces[1][1]], [pieces[0][2], pieces[1][2]]),)
    )
    for part in (0, 1):
        pieces[part] += [halves[part], halves[2 + part]]
    (tail,) = sum_step(((tail_sum, tail, 1),), 12, "tail_b")
    (tail,) = sum_step(((tail_sum, tail, 2),), 13, "tail_c")
    (tail,) = sum_step((), 14, "tail_gather", (Hand(tail, TAIL, False),))
    grad_query, grad_key, grad_value, grad_out, grad_router, grad_gain_one = lay_out_attention(
        tail.reshape(4, SHARD, TAIL), w_query, w_key, w_value, norm_gain[None]
    )
    grad_gate, grad_up, grad_down, grad_gain_two = lay_out_experts(
        place_here, [one.reshape((-1,) + one.shape[-2:]) for one in pieces[0] + pieces[1]], w_gate, w_up, w_router, grad_router, moe_gain[None]
    )
    return (
        result[None],
        loss_value,
        d_inputs[None],
        grad_query,
        grad_key,
        grad_value,
        grad_out,
        grad_gain_one[0],
        grad_router,
        grad_gain_two[0],
        grad_gate,
        grad_up,
        grad_down,
    )


def solution(mesh):
    in_specs = (
        P("fsdp", "ctx", None),
        P("fsdp", "ctx", None),
        P("fsdp", "ctx"),
        P(),
        P("fsdp", "ctx", None),
        P(),
        P("fsdp", None),
        P("fsdp", None),
        P("fsdp", None),
        P("fsdp", None),
        P("fsdp"),
        P("fsdp", None),
        P("fsdp"),
        P(None, "fsdp", None),
        P(None, "fsdp", None),
        P(None, None, "fsdp"),
    )
    out_specs = (
        P("fsdp", "ctx", None),
        P(),
        P("fsdp", "ctx", None),
        P("fsdp", None),
        P("fsdp", None),
        P("fsdp", None),
        P("fsdp", None),
        P("fsdp"),
        P("fsdp", None),
        P("fsdp"),
        P(None, "fsdp", None),
        P(None, "fsdp", None),
        P(None, None, "fsdp"),
    )
    return jax.shard_map(local, mesh=mesh, in_specs=in_specs, out_specs=out_specs, check_vma=False)
```

```python
import itertools
import math

import jax
import jax.numpy as jnp
from jax import lax
from jax.experimental import pallas as pl
from jax.experimental.pallas import tpu as pltpu
from jax.sharding import PartitionSpec as P

H = 12
KV = 2
HD = 128
E = 6
D = 1536
FF = 768
GROUPS = H // KV
ROWS = 128
SPAN = 64
HALF = 384
SLICE = 3 * HALF
QKV = 2048
SHARD = 384
WIDE = 3 * SLICE + 128
TAIL = 1024
PART = SHARD // 2
STRIP = PART // 4
EPS = 1e-06
BASE = 1000000.0
NEGATIVE = -1e30
SCALE = HD**-0.5
LOG2_E = math.log2(math.e)
SCALE_2 = SCALE * LOG2_E
MESH = pl.DeviceIdType.MESH
BF = jnp.bfloat16
F32 = jnp.float32


def place():
    ctx = lax.axis_index("ctx")
    shard = lax.axis_index("fsdp")
    return ctx // 8, (ctx // 2) % 4, ctx % 2, shard // 2, shard % 2


def device(x, z, y_lo, y_hi, core):
    return (x * 8 + z * 2 + y_lo, y_hi * 2 + core)


def x_peers(at):
    x, z, y_lo, y_hi, core = at
    return [device((x + k) % 4, z, y_lo, y_hi, core) for k in (1, 2, 3)]


def x_next(at):
    peers = x_peers(at)
    return [peers[0], peers[2]]


def z_next(at):
    peers = z_peers(at)
    return [peers[0], peers[2]]


def z_peers(at):
    x, z, y_lo, y_hi, core = at
    return [device(x, (z + k) % 4, y_lo, y_hi, core) for k in (1, 2, 3)]


def group_member(at, shard_hi, core):
    x, z, y_lo, y_hi, _ = at
    y_lo_there = (y_lo + y_hi + shard_hi) % 2
    return device(x, z, y_lo_there, shard_hi, core)


class Net:
    def __init__(self, send_sem, recv_sem, local_sem, extra_sem, stage):
        self.sems = (send_sem, recv_sem, local_sem, extra_sem)
        self.extra = 0
        self.stage = stage
        self.remote = 0
        self.loads = []
        self.kept = 0
        self.open = {}
        self.copies = []

    def greet(self, peers):
        barrier = pltpu.get_barrier_semaphore()
        for peer in peers:
            pl.semaphore_signal(barrier, inc=1, device_id=peer, device_id_type=MESH)
        pl.semaphore_wait(barrier, len(peers))

    def _open(self, copy):
        copy.start()
        self.open[id(copy)] = copy.wait
        self.copies.append(copy)
        return copy

    def send(self, src, dst, peer):
        slot = self.remote
        self.remote += 1
        return self._open(
            pltpu.make_async_remote_copy(
                src_ref=src,
                dst_ref=dst,
                send_sem=self.sems[0].at[slot],
                recv_sem=self.sems[1].at[slot],
                device_id=peer,
                device_id_type=MESH,
            )
        )

    def keep(self, src, dst):
        slot = self.kept
        self.kept += 1
        load = pltpu.make_async_copy(src, self.stage[slot], self.sems[2].at[slot])
        load.start()
        self.loads.append((load, slot, dst))

    def settle(self):
        stores = []
        for load, slot, dst in self.loads:
            load.wait()
            stores.append(self._open(pltpu.make_async_copy(self.stage[slot], dst, self.sems[2].at[slot])))
        self.loads = []
        return stores

    def done(self, copies):
        for copy in copies:
            copy.wait()
            del self.open[id(copy)]

    def arrived(self, copy):
        copy.wait_recv()
        self.open[id(copy)] = copy.wait_send

    def finish(self):
        self.settle()
        for wait in self.open.values():
            wait()


def exchange(body, inputs, outs, remote, keeps, number, name, scratch=()):
    count = len(inputs)
    total = count + len(outs)

    def kernel(*refs):
        net = Net(*refs[total : total + 4], refs[total + 4 :])
        body(net, refs[:count], refs[count:total])
        net.finish()

    any_spec = pl.BlockSpec(memory_space=pl.ANY)
    return pl.pallas_call(
        kernel,
        out_shape=[jax.ShapeDtypeStruct(shape, kind) for shape, kind in outs],
        in_specs=[any_spec] * count,
        out_specs=[any_spec] * len(outs),
        scratch_shapes=[
            pltpu.SemaphoreType.DMA((remote,)),
            pltpu.SemaphoreType.DMA((remote,)),
            pltpu.SemaphoreType.DMA((len(keeps) + len(scratch) + 1,)),
            pltpu.SemaphoreType.DMA((2 * len(scratch) + 1,)),
        ]
        + [pltpu.VMEM(shape, kind) for shape, kind in list(keeps) + list(scratch)],
        compiler_params=pltpu.CompilerParams(
            collective_id=number, has_side_effects=True, vmem_limit_bytes=60 << 20
        ),
        name=name,
    )(*inputs)


def ring_of(at):
    x, z, y_lo, y_hi, core = at
    return [
        device(
            lax.select(core == 0, (x + k) % 4, x), lax.select(core == 0, z, (z + k) % 4), y_lo, y_hi, core
        )
        for k in (1, 3)
    ]


class Ring:
    def __init__(self, net, blocks, own, neighbours):
        self.net, self.blocks, self.own, self.neighbours = net, blocks, own, neighbours
        self.first, self.rest = [], []

    def send(self, origin, half, way):
        return [self.net.send(ref, ref, self.neighbours[way]) for ref in self.blocks(origin, half)]

    def start(self):
        self.start_half(0)
        self.start_half(1)
        return self

    def start_half(self, half):
        self.first.append(self.send(self.own, half, half))
        self.rest.append(self.send(self.own, half, 1 - half))

    def forward(self):
        self.last = []
        for way in (0, 1):
            for copy in self.first[way]:
                self.net.arrived(copy)
            self.last.append(self.send((self.own + (3, 1)[way]) % 4, way, way))
        return self

    def finish(self):
        for copies in self.rest + self.last:
            for copy in copies:
                self.net.arrived(copy)


def gather_attention_weights(parts, small, number):
    count = len(parts)

    def body(net, ins, outs):
        at = place()
        x, z, y_lo, y_hi, core = at
        shard = y_hi * 2 + core
        sibling = device(x, z, y_lo, y_hi, 1 - core)
        partner = device(x, z, 1 - y_lo, 1 - y_hi, core)
        crossed = device(x, z, 1 - y_lo, 1 - y_hi, 1 - core)
        here = lax.select(core == 0, x, z)
        ring = ring_of(at)
        net.greet([sibling, partner, crossed] + ring)
        small_spot = outs[count].at[:, pl.ds(pl.multiple_of(shard * SHARD, 128), SHARD)]
        for peer in (partner, crossed, sibling):
            net.send(ins[count], small_spot, peer)

        def block(array, owner, start, size):
            width = ins[array].shape[1]
            return outs[array].at[pl.ds(pl.multiple_of(owner * SHARD + start, 16), size), pl.ds(0, width)]

        quarter = SHARD // 4
        order = (3, 0, 1, 2)
        part = quarter // 2
        first = {}
        for a in order:
            for half in (0, 1):
                start = here * quarter + half * part
                rows = pl.ds(pl.multiple_of(start, 16), part)
                first[a, half] = net.send(ins[a].at[rows, :], block(a, shard, start, part), partner)
        for a in order:
            net.send(ins[a], block(a, shard, 0, SHARD), sibling)
            net.keep(ins[a], block(a, shard, 0, SHARD))
        net.keep(ins[count], small_spot)
        net.settle()
        far = (1 - y_hi) * 2 + core
        rings = {}
        for a in order:

            def halves(origin, half, a=a):
                return [block(a, far, origin * quarter + half * part, part)]

            rings[a] = Ring(net, halves, here, ring)
            for half in (0, 1):
                net.arrived(first[a, half])
                rings[a].start_half(half)
            mine = block(a, far, here * quarter, quarter)
            net.send(mine, mine, sibling)
        for a in order:
            rings[a].forward()
        for a in order:
            rings[a].finish()
            for k in (1, 2, 3):
                piece = block(a, far, (here + k) % 4 * quarter, quarter)
                net.send(piece, piece, sibling)

    return exchange(
        body,
        tuple(parts) + (small,),
        [((D, part.shape[1]), BF) for part in parts] + [((16, D), BF)],
        count * 13 + 3,
        [(parts[a].shape, BF) for a in (3, 0, 1, 2)] + [((16, SHARD), BF)],
        number,
        "attention_weights",
    )


class ExpertWeights:
    quarter = HALF // 4
    cells = [(h, kind) for h in range(3) for kind in range(3)]

    def source(self, ins, owner, h, kind, start, size):
        index = owner * 3 + h
        expert = index // 2
        offset = pl.multiple_of((index % 2) * HALF, 128)
        if kind < 2:
            return ins[kind].at[expert, pl.ds(start, size), pl.ds(offset, HALF)]
        return ins[2].at[expert, pl.ds(pl.multiple_of(offset + start, 32), size), :]

    def target(self, outs, from_shard, h, kind, start, size):
        if kind < 2:
            rows = pl.multiple_of(from_shard * SHARD + start, 32)
            return outs[0].at[pl.ds(rows, size), pl.ds((2 * h + kind) * HALF, HALF)]
        columns = pl.multiple_of(from_shard * SHARD, 128)
        return outs[1].at[pl.ds(pl.multiple_of(h * HALF + start, 32), size), pl.ds(columns, SHARD)]

    def cross(self, net, ins, quarters, at):
        x, z, y_lo, y_hi, core = at
        for step in (0, 1):
            far_core = (core + step) % 2
            start = pl.multiple_of(lax.select(far_core == 0, x, z) * self.quarter, 32)
            owner = (1 - y_hi) * 2 + far_core
            peer = device(x, z, 1 - y_lo, 1 - y_hi, far_core)
            for n, (h, kind) in enumerate(self.cells):
                net.send(self.source(ins, owner, h, kind, start, self.quarter), quarters.at[step, n], peer)

    def around(self, net, ins, quarters, outs, at):
        x, z, y_lo, y_hi, core = at
        shard = y_hi * 2 + core
        sibling = device(x, z, y_lo, y_hi, 1 - core)
        here = lax.select(core == 0, x, z)

        def spots(origin, step):
            start = pl.multiple_of(origin * self.quarter, 32)
            from_shard = (1 - y_hi) * 2 + (core + step) % 2
            return [self.target(outs, from_shard, h, kind, start, self.quarter) for h, kind in self.cells]

        first, neighbours = [], ring_of(at)
        for turn in (0, 1):
            for way in (0, 1):
                step = way if turn == 0 else 1 - way
                copies = [
                    net.send(quarters.at[step, n], spot, neighbours[way]) for n, spot in enumerate(spots(here, step))
                ]
                if turn == 0:
                    first.append(copies)
        for step in (0, 1):
            for n, spot in enumerate(spots(here, step)):
                net.keep(quarters.at[step, n], spot)
        for h, kind in self.cells:
            other = y_hi * 2 + 1 - core
            net.send(self.source(ins, other, h, kind, 0, HALF), self.target(outs, shard, h, kind, 0, HALF), sibling)
            net.keep(self.source(ins, shard, h, kind, 0, HALF), self.target(outs, shard, h, kind, 0, HALF))
        return first, spots, here, neighbours

    def forward(self, net, state):
        first, spots, here, neighbours = state
        for n in range(len(self.cells)):
            for way in (0, 1):
                net.arrived(first[way][n])
                spot = spots((here + (3, 1)[way]) % 4, way)[n]
                net.send(spot, spot, neighbours[way])


EXPERT = ExpertWeights()


def gather_keys(local, experts, number):
    def body(net, ins, outs):
        mine, whole = ins[0], outs[0]
        at = place()
        x, z, y_lo, y_hi, core = at
        partner = device(x, z, 1 - y_lo, y_hi, core)
        across = [device(x, z, 1 - y_lo, 1 - y_hi, c) for c in (0, 1)]
        net.greet([partner] + x_next(at) + z_next(at) + across)
        spot = whole.at[x, z, y_lo]
        near = net.send(mine, spot, partner)
        net.keep(mine, spot)
        EXPERT.cross(net, ins[1:], outs[1], at)
        net.done(net.settle())
        net.arrived(near)
        half = KV * HD
        cuts = [pl.ds(part * half, half) for part in (0, 1)]
        sides = (x_next(at), z_next(at))
        near_rings = (
            Ring(net, lambda o, h: [whole.at[x, o, h, :, cuts[0]]], z, sides[1]),
            Ring(net, lambda o, h: [whole.at[o, z, h, :, cuts[1]]], x, sides[0]),
        )
        far_rings = (
            Ring(net, lambda o, h: [whole.at[o, :, h, :, cuts[0]]], x, sides[0]),
            Ring(net, lambda o, h: [whole.at[:, o, h, :, cuts[1]]], z, sides[1]),
        )
        for ring in near_rings:
            ring.start()
        for ring in near_rings:
            ring.forward()
        for near_ring, far_ring in zip(near_rings, far_rings):
            near_ring.finish()
            far_ring.start()
        for ring in far_rings:
            ring.forward()

    return exchange(
        body,
        (local,) + experts,
        [((4, 4, 2, ROWS, 2 * KV * HD), BF), ((2, 9, EXPERT.quarter, HALF), BF)],
        25 + 18,
        [((ROWS, 2 * KV * HD), BF)],
        number,
        "keys_values",
    )


def group_places(at):
    x, z, y_lo, y_hi, core = at
    sibling = device(x, z, y_lo, y_hi, 1 - core)
    partner = device(x, z, 1 - y_lo, 1 - y_hi, core)
    return sibling, partner


class Spread:
    def start(self, net, mine, whole, at):
        sibling, partner = group_places(at)
        spot = whole.at[at[3] * 2 + at[4]]
        self.copy = net.send(mine, spot, partner)
        net.send(mine, spot, sibling)
        net.keep(mine, spot)

    def forward(self, net, whole, at):
        sibling, partner = group_places(at)
        net.arrived(self.copy)
        far = whole.at[(1 - at[3]) * 2 + at[4]]
        net.send(far, far, sibling)


def group_spread(parts, number, name, weights=None):
    count = len(parts)
    keeps = [(part.shape, part.dtype) for part in parts]
    outs = [((4,) + part.shape, part.dtype) for part in parts]
    inputs = tuple(parts)
    remote = 3 * count
    if weights is not None:
        inputs += weights
        outs += [((D, 2 * SLICE), BF), ((SLICE, D), BF)]
        remote += 7 * 9
        keeps += [((EXPERT.quarter, HALF), BF)] * 18 + [((HALF, HALF), BF)] * 9

    def body(net, ins, outs):
        at = place()
        sibling, partner = group_places(at)
        net.greet([sibling, partner] + (ring_of(at) if weights is not None else []))
        spreads = [Spread() for _ in range(count)]
        for one, mine, whole in zip(spreads, ins, outs):
            one.start(net, mine, whole, at)
        if weights is not None:
            state = EXPERT.around(net, ins[count:-1], ins[-1], outs[count:], at)
        net.settle()
        for one, whole in zip(spreads, outs):
            one.forward(net, whole, at)
        if weights is not None:
            EXPERT.forward(net, state)

    return exchange(body, inputs, outs, remote, keeps, number, name)


def group_sum(parts, number, name, extra=None):
    count = len(parts)
    spread = () if extra is None else (extra,)
    keeps = [(part.shape[1:], BF) for part in parts] + [(one.shape, one.dtype) for one in spread]
    outs = [((3,) + part.shape[1:], BF) for part in parts] + [((4,) + one.shape, one.dtype) for one in spread]
    scratch = [((2,) + part.shape[1:], BF) for part in parts]

    def body(net, ins, outs):
        at = place()
        x, z, y_lo, y_hi, core = at
        sibling, partner = group_places(at)
        net.greet([sibling, partner])
        sums = net.stage[len(keeps) :]
        far = (1 - y_hi) * 2
        came, own = [], []
        for mine, pair in zip(ins, sums):
            came.append(net.send(mine.at[far + 1 - core], pair.at[1], sibling))
            load = pltpu.make_async_copy(mine.at[far + core], pair.at[0], net.sems[2].at[len(keeps) + len(own)])
            load.start()
            own.append(load)
        for mine, got in zip(ins[:count], outs):
            net.send(mine.at[y_hi * 2 + 1 - core], got.at[1], sibling)
            net.keep(mine.at[y_hi * 2 + core], got.at[0])
        spreads = []
        for mine, whole in zip(ins[count:], outs[count:]):
            spreads.append(Spread())
            spreads[-1].start(net, mine, whole, at)
        for n, pair in enumerate(sums):
            own[n].wait()
            net.arrived(came[n])

            def add(step, carry):
                rows = pl.ds(pl.multiple_of(step * 16, 16), 16)
                pair[0, rows, :] = (pair[0, rows, :].astype(F32) + pair[1, rows, :].astype(F32)).astype(BF)
                return carry

            lax.fori_loop(0, pair.shape[1] // 16, add, 0)
            net.send(pair.at[0], outs[n].at[2], partner)
        net.settle()
        for one, whole in zip(spreads, outs[count:]):
            one.forward(net, whole, at)

    return exchange(
        body, tuple(parts) + spread, outs, 3 * (count + len(spread)), keeps, number, name, scratch
    )


def add_up(pieces, axis):
    return jnp.sum(pieces.astype(F32), axis=axis).astype(BF)


def add_strips_kernel(*refs):
    for part in (0, 1):
        three = [refs[part * 3 + n][...].astype(F32) for n in range(3)]
        refs[6][part] = (three[0] + three[1] + three[2]).astype(BF)


def add_strips(strips):
    cell = WIDE // 4
    return local_call(
        add_strips_kernel,
        tuple(strips),
        [((2, 4, STRIP, WIDE), BF)],
        "add_strips",
        1000,
        specs=[pl.BlockSpec((4, STRIP, cell), lambda n: (0, 0, n))] * 6,
        out_specs=[pl.BlockSpec((2, 4, STRIP, cell), lambda n: (0, 0, 0, n))],
        grid=(4,),
    )[0]


class RingSum:
    def __init__(self, net, block, place_of, own, neighbours, pair):
        self.net, self.block, self.place_of, self.own = net, block, place_of, own
        self.neighbours, self.pair = neighbours, pair

    def start(self):
        net = self.net
        self.came = [
            net.send(self.block((self.own + 2) % 4, way), self.pair.at[way, 1], self.neighbours[way]) for way in (0, 1)
        ]
        self.loads = []
        for way in (0, 1):
            target = (self.own + (1, 3)[way]) % 4
            load = pltpu.make_async_copy(self.block(target, way), self.pair.at[way, 0], net.sems[3].at[net.extra])
            net.extra += 1
            load.start()
            self.loads.append(load)
            net.send(self.block(target, 1 - way), self.place_of(1 + way, 1 - way), self.neighbours[way])
        for half in (0, 1):
            net.keep(self.block(self.own, half), self.place_of(0, half))

    def forward(self):
        net, pair = self.net, self.pair
        *lead, rows, _ = pair.shape[2:]
        for way in (0, 1):
            self.loads[way].wait()
            net.arrived(self.came[way])
            for spot in itertools.product(*(range(size) for size in lead)):

                def add(step, carry):
                    cut = pl.ds(pl.multiple_of(step * 16, 16), 16)
                    own, came = pair[(way, 0) + spot + (cut,)], pair[(way, 1) + spot + (cut,)]
                    pair[(way, 0) + spot + (cut,)] = (own.astype(F32) + came.astype(F32)).astype(BF)
                    return carry

                lax.fori_loop(0, rows // 16, add, 0)
            net.send(pair.at[way, 0], self.place_of(1 + way, way), self.neighbours[way])


class KeySum:
    half = KV * HD
    shapes = (
        ((2, 3, 4, 2, ROWS, KV * HD), BF),
        ((2, 4, 2, ROWS, KV * HD), BF),
        ((2, 2, ROWS, KV * HD), BF),
    )
    pairs = ([((2, 2, 2, 2, ROWS, KV * HD), BF)] * 2, [], [])
    keeps = (
        [((2, 2, ROWS, KV * HD), BF)] * 4,
        [((2, ROWS, KV * HD), BF)] * 2,
        [((2, ROWS, KV * HD), BF)],
    )

    def first(self, net, whole, got, at, pairs):
        cuts = [pl.ds(part * self.half, self.half) for part in (0, 1)]
        blocks = (
            lambda target, half: whole.at[target, pl.ds(2 * half, 2), :, :, cuts[0]],
            lambda target, half: whole.at[pl.ds(2 * half, 2), target, :, :, cuts[1]],
        )
        sides = (x_next(at), z_next(at))
        return [
            RingSum(
                net,
                blocks[part],
                lambda n, half, part=part: got.at[part, n, pl.ds(2 * half, 2)],
                at[part],
                sides[part],
                pairs[part],
            )
            for part in (0, 1)
        ]

    def second(self, net, whole, got, at, pairs):
        x, z = at[0], at[1]
        peers = (x_peers(at), z_peers(at))
        for k in (2, 1, 3):
            net.send(whole.at[0, (z + k) % 4], got.at[0, k], peers[1][k - 1])
            net.send(whole.at[1, (x + k) % 4], got.at[1, k], peers[0][k - 1])
        net.keep(whole.at[0, z], got.at[0, 0])
        net.keep(whole.at[1, x], got.at[1, 0])

    def third(self, net, whole, got, at, pairs):
        x, z, y_lo, y_hi, core = at
        net.send(whole.at[:, 1 - y_lo], got.at[1], device(x, z, 1 - y_lo, y_hi, core))
        net.keep(whole.at[:, y_lo], got.at[0])


class GradSum:
    def __init__(self, columns, ring_step):
        self.columns, self.cell, self.ring_step = columns, columns // 4, ring_step
        widths = (columns, self.cell)
        came = [3 if ring_step == step else 4 for step in (0, 1)]
        self.shapes = tuple(((2, came[step], 4, STRIP, widths[step]), BF) for step in (0, 1))
        self.shapes += (((2, 2, 2, STRIP, self.cell), BF),)
        self.keeps = tuple(
            [((2, STRIP, widths[step]), BF)] * 4 if ring_step == step else [((4, STRIP, widths[step]), BF)] * 2
            for step in (0, 1)
        )
        self.keeps += ([((2, STRIP, self.cell), BF)],)
        self.pairs = tuple(
            [((2, 2, 2, STRIP, widths[step]), BF)] * 2 if ring_step == step else [] for step in (0, 1)
        ) + ([],)

    def rings(self, net, block, got, own, sides, pairs):
        return [
            RingSum(
                net,
                lambda target, half, part=part: block(part, target, pl.ds(2 * half, 2)),
                lambda n, half, part=part: got.at[part, n, pl.ds(2 * half, 2)],
                own[part],
                sides[part],
                pairs[part],
            )
            for part in (0, 1)
        ]

    def direct(self, net, block, got, own, peers):
        for k in (2, 1, 3, 0):
            for part in (0, 1):
                piece = block(part, (own[part] + k) % 4, slice(None))
                if k == 0:
                    net.keep(piece, got.at[part, 0])
                else:
                    net.send(piece, got.at[part, k], peers[part][k - 1])

    def first(self, net, whole, got, at, pairs):
        def block(part, target, sets):
            return whole.at[sets, pl.ds(pl.multiple_of(part * PART + target * STRIP, 16), STRIP), :]

        if self.ring_step == 0:
            return self.rings(net, block, got, (at[0], at[1]), (x_next(at), z_next(at)), pairs)
        return self.direct(net, block, got, (at[0], at[1]), (x_peers(at), z_peers(at)))

    def second(self, net, whole, got, at, pairs):
        def block(part, target, sets):
            return whole.at[part, sets, :, pl.ds(pl.multiple_of(target * self.cell, 128), self.cell)]

        if self.ring_step == 1:
            return self.rings(net, block, got, (at[1], at[0]), (z_next(at), x_next(at)), pairs)
        return self.direct(net, block, got, (at[1], at[0]), (z_peers(at), x_peers(at)))

    def third(self, net, whole, got, at, pairs):
        x, z, y_lo, y_hi, core = at
        spot = got.at[y_lo, y_hi]
        for k in (2, 3, 1):
            there_hi, there_core = (y_hi + k // 2) % 2, (y_lo + k % 2) % 2
            net.send(whole.at[:, there_hi * 2 + there_core], spot, device(x, z, core, there_hi, there_core))
        mine = whole.at[:, y_hi * 2 + y_lo]
        slot, held = net.remote, net.kept
        net.remote += 1
        net.kept += 1
        stage, sem = net.stage[held], net.sems[2].at[held]

        @pl.when(core == y_lo)
        def _():
            load = pltpu.make_async_copy(mine, stage, sem)
            load.start()
            load.wait()
            store = pltpu.make_async_copy(stage, spot, sem)
            store.start()
            store.wait()

        @pl.when(core != y_lo)
        def _():
            copy = pltpu.make_async_remote_copy(
                src_ref=mine,
                dst_ref=spot,
                send_sem=net.sems[0].at[slot],
                recv_sem=net.sems[1].at[slot],
                device_id=device(x, z, core, y_hi, y_lo),
                device_id_type=MESH,
            )
            copy.start()
            copy.wait()


class LossSum:
    shapes = (((4, 8, 128), F32), ((4, 8, 128), F32), ((2, 8, 128), F32))
    keeps = ([((8, 128), F32)],) * 3
    pairs = ([],) * 3

    def first(self, net, whole, got, at, pairs):
        for peer in x_peers(at):
            net.send(whole, got.at[at[0]], peer)
        net.keep(whole, got.at[at[0]])

    def second(self, net, whole, got, at, pairs):
        for peer in z_peers(at):
            net.send(whole, got.at[at[1]], peer)
        net.keep(whole, got.at[at[1]])

    def third(self, net, whole, got, at, pairs):
        x, z, y_lo, y_hi, core = at
        net.send(whole, got.at[y_lo], device(x, z, 1 - y_lo, y_hi, core))
        net.keep(whole, got.at[y_lo])


class GroupShare:
    def __init__(self, spread, swapped):
        self.count = len(spread)
        self.inputs = tuple(spread) + tuple(swapped)
        self.outs = [((4,) + one.shape, BF) for one in spread] + [(one.shape, BF) for one in swapped]
        self.keeps = [(one.shape, BF) for one in spread] + [(one.shape[1:], BF) for one in swapped]

    def peers(self, at):
        x, z, y_lo, y_hi, core = at
        return [device(x, z, 1 - y_lo, 1 - y_hi, 1 - core), *group_places(at)]

    def start(self, net, ins, outs, at):
        x, z, y_lo, y_hi, core = at
        crossed, sibling, partner = self.peers(at)
        shard = y_hi * 2 + core
        far = (1 - y_hi) * 2
        for mine, whole in zip(ins[self.count :], outs[self.count :]):
            net.send(mine.at[far + core], whole.at[shard], partner)
            net.send(mine.at[far + 1 - core], whole.at[shard], crossed)
            net.send(mine.at[y_hi * 2 + 1 - core], whole.at[shard], sibling)
        self.spreads = []
        for mine, whole in zip(ins, outs[: self.count]):
            self.spreads.append(Spread())
            self.spreads[-1].start(net, mine, whole, at)
        for mine, whole in zip(ins[self.count :], outs[self.count :]):
            net.keep(mine.at[shard], whole.at[shard])

    def forward(self, net, outs, at):
        for one, whole in zip(self.spreads, outs):
            one.forward(net, whole, at)


class Forward:
    def __init__(self, behind, ahead):
        self.inputs = tuple(behind) + tuple(ahead)
        self.outs = [(one.shape, BF) for one in behind]
        self.keeps = []

    def peers(self, at):
        return []

    def start(self, net, ins, outs, at):
        for part, (plus, minus) in enumerate((x_next(at), z_next(at))):
            net.send(ins[part].at[0], outs[part].at[0], plus)
            net.send(ins[2 + part].at[1], outs[part].at[1], minus)

    def forward(self, net, outs, at):
        pass


class Hand:
    def __init__(self, piece, columns, split):
        self.columns, self.cell, self.split = columns, columns // 4, split
        self.inputs = (piece,)
        self.outs = [((2, 2, STRIP, columns), BF)] * 2 if split else [((2, 2, SHARD, columns), BF)]
        self.keeps = [((2, STRIP, columns // 4), BF)] * 2

    def peers(self, at):
        x, z, y_lo, y_hi, core = at
        return [device(x, z, 1 - y_lo, y_hi, core)] + x_next(at) + z_next(at)

    def strip(self, outs, at, part, high, low, j):
        cut = pl.ds(pl.multiple_of(j * self.cell, 128), self.cell)
        if self.split:
            return outs[part].at[high, low, :, cut]
        start = pl.multiple_of(part * PART + at[part] * STRIP, 16)
        return outs[0].at[high, low, pl.ds(start, STRIP), cut]

    def start(self, net, ins, outs, at):
        (mine,) = ins
        self.near = []
        for part in (0, 1):
            spot = self.strip(outs, at, part, slice(None), at[2], at[1 - part])
            self.near.append(net.send(mine.at[:, part], spot, self.peers(at)[0]))
            net.keep(mine.at[:, part], spot)

    def forward(self, net, outs, at):
        sides = (x_next(at), z_next(at))
        rings = []
        for part in (0, 1):
            net.arrived(self.near[part])

            def halves(origin, half, part=part):
                return [self.strip(outs, at, part, half, slice(None), origin)]

            rings.append(Ring(net, halves, at[1 - part], sides[1 - part]).start())
        for ring in rings:
            ring.forward()
        if self.split:
            return
        far_rings = []
        for part in (0, 1):
            rings[part].finish()

            def halves(origin, half, part=part):
                start = pl.multiple_of(part * PART + origin * STRIP, 16)
                return [outs[0].at[half, :, pl.ds(start, STRIP), :]]

            far_rings.append(Ring(net, halves, at[part], sides[part]).start())
        for ring in far_rings:
            ring.forward()


def sum_step(sums, number, name, extras=()):
    count = len(sums)
    steps = [step for _, _, step in sums]
    ringed = [one.pairs[step] != [] for one, _, step in sums]
    keeps = [keep for (one, _, step), late in zip(sums, ringed) if not late for keep in one.keeps[step]]
    keeps += [keep for (one, _, step), late in zip(sums, ringed) if late for keep in one.keeps[step]]
    keeps += [keep for extra in extras for keep in extra.keeps]

    def body(net, ins, outs):
        at = place()
        x, z, y_lo, y_hi, core = at
        peers = []
        if any(step < 2 for step in steps):
            peers += x_peers(at) + z_peers(at)
        column = any(step == 2 and isinstance(one, GradSum) for one, _, step in sums)
        if column:
            for k in range(1, 8):
                peers.append(device(x, z, (y_lo + k // 4) % 2, (y_hi + (k // 2) % 2) % 2, (core + k) % 2))
        elif any(step == 2 for step in steps) and not extras:
            peers.append(device(x, z, 1 - y_lo, y_hi, core))
        for extra in extras:
            peers += extra.peers(at)
        net.greet(peers)
        at_in = at_out = count
        spans = []
        for extra in extras:
            spans.append((at_in, at_in + len(extra.inputs), at_out, at_out + len(extra.outs)))
            at_in, at_out = spans[-1][1], spans[-1][3]
        rings, at_pair = [], len(keeps)
        for (one, _, step), whole, got in zip(sums, ins, outs):
            pairs = net.stage[at_pair : at_pair + len(one.pairs[step])]
            at_pair += len(pairs)
            rings += (one.first, one.second, one.third)[step](net, whole, got, at, pairs) or []
        for ring in rings:
            ring.start()
        for extra, (a, b, c, d) in zip(extras, spans):
            extra.start(net, ins[a:b], outs[c:d], at)
        stores = net.settle()
        for ring in rings:
            ring.forward()
        net.done(stores)
        for extra, (a, b, c, d) in zip(extras, spans):
            extra.forward(net, outs[c:d], at)

    came = exchange(
        body,
        tuple(array for _, array, _ in sums) + tuple(one for extra in extras for one in extra.inputs),
        [one.shapes[step] for one, _, step in sums] + [out for extra in extras for out in extra.outs],
        12 * count + 30 * len(extras),
        keeps,
        number,
        name,
        [pair for one, _, step in sums for pair in one.pairs[step]],
    )
    total = []
    for (one, _, step), got in zip(sums, came):
        if isinstance(one, LossSum):
            total.append(jnp.sum(got, axis=0))
        else:
            total.append(add_up(got, 1 if step < 2 else 0))
    return total + list(came[count:])


SPANS = 16
BLOCK = SPANS * SPAN
QUERIES = GROUPS * SPAN
SMEM = pl.BlockSpec(memory_space=pltpu.SMEM)
VMEM = pl.BlockSpec(memory_space=pltpu.VMEM)
LOW = 32
FIRST = 2


def local_call(kernel, args, outs, name, flops, specs=None, out_specs=None, grid=None, scratch=(), limit=60):
    moved = sum(math.prod(arg.shape) * arg.dtype.itemsize for arg in args)
    moved += sum(math.prod(shape) * jnp.dtype(kind).itemsize for shape, kind in outs)
    extra = {} if grid is None else {"grid": grid}
    return pl.pallas_call(
        kernel,
        out_shape=[jax.ShapeDtypeStruct(shape, kind) for shape, kind in outs],
        in_specs=specs or [VMEM] * len(args),
        out_specs=out_specs or [VMEM] * len(outs),
        scratch_shapes=[pltpu.VMEM(shape, kind) for shape, kind in scratch],
        compiler_params=pltpu.CompilerParams(vmem_limit_bytes=limit << 20),
        cost_estimate=pl.CostEstimate(flops=flops // 1000, transcendentals=0, bytes_accessed=moved // 1000),
        name=name,
        **extra,
    )(*args)


def inverse_root(values):
    return lax.rsqrt(jnp.mean(values * values, axis=-1, keepdims=True) + EPS)


def norm_back(values, gain, grad):
    inv = inverse_root(values)
    scaled = gain * grad
    return inv * (scaled - values * (inv * inv) * jnp.mean(scaled * values, axis=-1, keepdims=True))


def turn(values, cosine, sine):
    return values * cosine + pltpu.roll(values, HD // 2, 1) * sine


def head(index):
    return slice(index * HD, (index + 1) * HD)


def stack_heads(ref, span, kv):
    rows = slice(span * SPAN, (span + 1) * SPAN)
    return jnp.concatenate([ref[rows, head(kv * GROUPS + g)] for g in range(GROUPS)], axis=0)


def unstack_heads(ref, span, kv, values):
    rows = slice(span * SPAN, (span + 1) * SPAN)
    for g in range(GROUPS):
        ref[rows, head(kv * GROUPS + g)] = values[g * SPAN : (g + 1) * SPAN, :]


def expert_lanes():
    return lax.broadcasted_iota(jnp.int32, (1, HD), 1)


def wide_router(small_ref):
    rows = small_ref[...]
    number = lax.broadcasted_iota(jnp.int32, rows.shape, 0)
    rows = jnp.where((number >= FIRST) & (number < FIRST + E), rows.astype(F32), 0.0).astype(BF)
    gap = jnp.zeros((16, D), BF)
    return jnp.concatenate([rows, gap, rows, gap, gap, gap, gap, gap], axis=0)


def chosen(routes):
    lanes = expert_lanes()
    number = jnp.where(lanes >= LOW, lanes - LOW, lanes) - FIRST
    total = jnp.zeros((ROWS, HD), F32)
    for slot in range(4):
        total = total + jnp.where(routes[:, slot : slot + 1] == number, 1.0, 0.0)
    return total


def in_two(values):
    high = values.astype(BF).astype(F32)
    return jnp.where(expert_lanes() < LOW, high, values - high).astype(BF)


def project_kernel(
    spans, tokens, small, w_query, w_key, w_value, normed, query, keys_values, cosine, sine
):
    lanes = lax.broadcasted_iota(jnp.int32, (SPAN, HD), 1)
    offsets = lax.broadcasted_iota(jnp.int32, (SPAN, HD), 0)
    half_size = HD // 2
    steps = jnp.where(lanes >= half_size, lanes - half_size, lanes).astype(F32)
    frequency = jnp.exp(-(steps * 2.0 / HD) * math.log(BASE))
    for s in range(2):
        rows = slice(s * SPAN, (s + 1) * SPAN)
        angles = (spans[s] * SPAN + offsets).astype(F32) * frequency
        cosine[rows, :] = jnp.cos(angles)
        turned = jnp.sin(angles)
        sine[rows, :] = jnp.where(lanes >= half_size, turned, -turned)
    inputs = tokens[...].astype(F32)
    gain = small[...].astype(F32)[0:1, :]
    normed[...] = (inputs * inverse_root(inputs) * gain).astype(BF)
    rows = normed[...]
    cos, sin = cosine[...], sine[...]
    raw = jnp.dot(rows, w_key[...], preferred_element_type=F32)
    for k in range(KV):
        keys_values[:, head(k)] = turn(raw[:, head(k)], cos, sin).astype(BF)
    keys_values[:, KV * HD :] = jnp.dot(rows, w_value[...], preferred_element_type=F32).astype(BF)
    for k in range(0, H, 4):
        raw = jnp.dot(rows, w_query[:, k * HD : (k + 4) * HD], preferred_element_type=F32)
        for j in range(4):
            query[:, head(k + j)] = turn(raw[:, head(j)], cos, sin).astype(BF)


def project(*args):
    outs = [((ROWS, D), BF), ((ROWS, H * HD), BF), ((ROWS, 2 * KV * HD), BF), ((ROWS, HD), F32), ((ROWS, HD), F32)]
    return local_call(project_kernel, args, outs, "project", 800_000_000, specs=[SMEM] + [VMEM] * 5)


def combine_kernel(mixed, hidden, teacher, valid, count, result, d_result, d_low, squared):
    total = hidden[...] + (mixed[0].astype(F32) + mixed[1].astype(F32) + mixed[2].astype(F32))
    result[...] = total.astype(BF)
    error = total - teacher[...].astype(F32)
    valid_rows = valid[...].astype(F32).T
    squared[...] = jnp.full((8, 128), jnp.sum(valid_rows * error * error), F32)
    norm_factor = jnp.full((1, 1), count[0], jnp.int32).astype(F32) * D
    grad = 2.0 * valid_rows * error / norm_factor
    d_result[...] = grad
    d_low[...] = grad.astype(BF)


def combine(*args):
    outs = [((ROWS, D), BF), ((ROWS, D), F32), ((ROWS, D), BF), ((8, 128), F32)]
    return local_call(combine_kernel, args, outs, "combine", 1000, specs=[VMEM] * 4 + [SMEM])


def tail_kernel(normed, d_qkv, attended, d_attn, normed_two, d_router, out):
    for shard in range(4):
        columns = slice(shard * SHARD, (shard + 1) * SHARD)
        out[shard, :, :512] = tn(normed[:, columns], d_qkv[...]).astype(BF)
        out[shard, :, 512 : 512 + SHARD] = tn(attended[:, columns], d_attn[...]).astype(BF)
        out[shard, :, 512 + SHARD :] = tn(normed_two[:, columns], d_router[...]).astype(BF)


def tail_grads(*args):
    return local_call(tail_kernel, args, [((4, SHARD, TAIL), BF)], "tail_grads", 1000)[0]


def nt(a, b):
    return lax.dot_general(a, b, (((1,), (1,)), ((), ())), preferred_element_type=F32)


def tn(a, b):
    return lax.dot_general(a, b, (((0,), (0,)), ((), ())), preferred_element_type=F32)


def block_rows(where, b, ref):
    return jnp.concatenate(
        [ref[pl.ds(pl.multiple_of(where[b * SPANS + i] * SPAN, SPAN), SPAN), :] for i in range(SPANS)], axis=0
    )


def lead_of_keys():
    keys = lax.broadcasted_iota(jnp.int32, (BLOCK, QUERIES), 0)
    queries = lax.broadcasted_iota(jnp.int32, (BLOCK, QUERIES), 1)
    return keys - queries % SPAN


def attend_kernel(
    where, spans, q_ref, kv_ref, tokens, w_out, small, routes, o_ref, low_ref, lse_ref, hidden_ref, normed_ref, gates_ref, probs_ref
):
    lead = lead_of_keys()
    for s in range(2):
        span = spans[s]
        stacked = [stack_heads(q_ref, s, kv) for kv in range(KV)]

        def body(b, carry, last=False):
            keys_values = block_rows(where, b, kv_ref)
            out = []
            for kv in range(KV):
                top, total, acc = carry[kv]
                keys = keys_values[:, head(kv)]
                values = keys_values[:, head(KV + kv)]
                logits = nt(keys, stacked[kv])
                if last:
                    logits = jnp.where(lead <= span * SPAN - b * BLOCK, logits, NEGATIVE)
                new_top = jnp.maximum(top, jnp.max(logits, axis=0, keepdims=True))
                weights = jnp.exp2((logits - new_top) * SCALE_2)
                shrink = jnp.exp2((top - new_top) * SCALE_2)
                total = total * shrink + jnp.sum(weights, axis=0, keepdims=True)
                acc = acc * shrink + tn(values, weights.astype(BF))
                out.append((new_top, total, acc))
            return tuple(out)

        start = tuple(
            (
                jnp.full((1, QUERIES), NEGATIVE, F32),
                jnp.zeros((1, QUERIES), F32),
                jnp.zeros((HD, QUERIES), F32),
            )
            for _ in range(KV)
        )
        final = body(span // SPANS, lax.fori_loop(0, span // SPANS, body, start), last=True)
        for kv in range(KV):
            top, total, acc = final[kv]
            unstack_heads(o_ref, s, kv, (acc / total).T)
            lse_ref[2 * s + kv : 2 * s + kv + 1, :] = top * SCALE_2 + jnp.log(total) * LOG2_E
    lse_ref[4:8, :] = jnp.zeros((4, QUERIES), F32)

    low_ref[...] = o_ref[...].astype(BF)
    for start in range(0, D, 512):
        columns = slice(start, start + 512)
        hidden_ref[:, columns] = tokens[:, columns].astype(F32) + jnp.dot(
            low_ref[...], w_out[:, columns], preferred_element_type=F32
        )
    hidden = hidden_ref[...]
    gain = small[...].astype(F32)[1:2, :]
    normed = (hidden * inverse_root(hidden) * gain).astype(BF)
    normed_ref[...] = normed
    logits = nt(normed, wide_router(small))
    lanes = expert_lanes()
    first = (lanes >= FIRST) & (lanes < FIRST + E)
    second = (lanes >= FIRST + LOW) & (lanes < FIRST + LOW + E)
    top = jnp.max(jnp.where(first, logits, NEGATIVE), axis=1, keepdims=True)
    weights = jnp.where(first | second, jnp.exp(logits - top), 0.0)
    probs = weights / jnp.sum(jnp.where(first, weights, 0.0), axis=1, keepdims=True)
    probs_ref[...] = probs
    gates_ref[...] = in_two(probs * chosen(routes))


def attend(*args):
    outs = [
        ((ROWS, H * HD), F32),
        ((ROWS, H * HD), BF),
        ((8, QUERIES), F32),
        ((ROWS, D), F32),
        ((ROWS, D), BF),
        ((ROWS, HD), BF),
        ((ROWS, HD), F32),
    ]
    return local_call(attend_kernel, args, outs, "attend", 2_400_000_000, specs=[SMEM, SMEM] + [VMEM] * 6)


GELU = math.sqrt(2.0 / math.pi)


def gate_column(gates, place_ref, h):
    lane = FIRST + (place_ref[0] * 3 + h) // 2
    lanes = expert_lanes()
    here = (lanes == lane) | (lanes == lane + LOW)
    return jnp.sum(jnp.where(here, gates, 0.0), axis=1, keepdims=True)


def experts_kernel(place_ref, rows, gates, w_both, w_down, mixed, made_ref, active_ref, steep_ref, total):
    h = pl.program_id(0)
    raw = jnp.dot(rows[...], w_both[...], preferred_element_type=F32)
    gate, up = raw[:, :HALF], raw[:, HALF:]
    squared = gate * gate
    inner = jnp.tanh(GELU * gate * (1.0 + 0.044715 * squared))
    active = 0.5 * gate * (1.0 + inner)
    slope = 0.5 * (1.0 + inner) + 0.5 * gate * (1.0 - inner * inner) * (GELU + 3 * 0.044715 * GELU * squared)
    made = active * up
    made_ref[...] = made.astype(BF)
    active_ref[...] = active.astype(BF)
    steep_ref[...] = (slope * up).astype(BF)
    weighted = (gate_column(gates[...].astype(F32), place_ref, h) * made).astype(BF)
    out = jnp.dot(weighted, w_down[...], preferred_element_type=F32)

    @pl.when(h == 0)
    def _():
        total[...] = out

    @pl.when(h == 1)
    def _():
        total[...] += out

    @pl.when(h == 2)
    def _():
        mixed[...] = (total[...] + out).astype(BF)


def whole(shape):
    return pl.BlockSpec(shape, lambda h: (0,) * len(shape))


def experts(place_here, rows, gates, wide, low):
    count = 4 * ROWS
    return local_call(
        experts_kernel,
        (place_here, rows, gates, wide, low),
        [((count, D), BF)] + [((count, SLICE), BF)] * 3,
        "experts",
        5_400_000_000,
        specs=[
            SMEM,
            whole((count, D)),
            whole((count, HD)),
            pl.BlockSpec((D, 2 * HALF), lambda h: (0, h)),
            pl.BlockSpec((HALF, D), lambda h: (h, 0)),
        ],
        out_specs=[whole((count, D))] + [pl.BlockSpec((count, HALF), lambda h: (0, h))] * 3,
        grid=(3,),
        scratch=[((count, D), F32)],
    )


def experts_back_kernel(
    place_ref, rows, d_rows, gates, made_ref, active_ref, steep_ref, w_both, w_down, d_normed, gates_sent, *rest
):
    chunks, (total, strip, rows_t, d_rows_t, d_gates) = rest[:10], rest[10:]
    h = pl.program_id(0)

    @pl.when(h == 0)
    def _():
        rows_t[...] = rows[...].T
        d_rows_t[...] = d_rows[...].T

    back = nt(d_rows[...], w_down[...])
    made = made_ref[...].astype(F32)
    weight = gate_column(gates[...].astype(F32), place_ref, h)
    lane = FIRST + (place_ref[0] * 3 + h) // 2
    lanes = expert_lanes()
    here = (lanes == lane) | (lanes == lane + LOW)
    d_weight = jnp.where(here, jnp.sum(made * back, axis=1, keepdims=True), 0.0)
    d_made = weight * back
    d_gate = (d_made * steep_ref[...].astype(F32)).astype(BF)
    d_up = (d_made * active_ref[...].astype(F32)).astype(BF)
    weighted = (weight * made).astype(BF)
    d_raw = jnp.concatenate([d_gate, d_up], axis=1)
    out = nt(d_raw, w_both[...])

    @pl.when(h == 0)
    def _():
        total[...] = out
        d_gates[...] = d_weight

    @pl.when(h != 0)
    def _():
        d_gates[...] += d_weight

    @pl.when(h == 1)
    def _():
        total[...] += out

    @pl.when(h == 2)
    def _():
        d_normed[...] = (total[...] + out).astype(BF)
        gates_sent[...] = in_two(d_gates[...])

    for shard in range(4):
        columns = slice(shard * SHARD, (shard + 1) * SHARD)
        strip[:, : 2 * HALF] = jnp.dot(rows_t[columns, :], d_raw, preferred_element_type=F32).astype(BF)
        strip[:, 2 * HALF :] = jnp.dot(d_rows_t[columns, :], weighted, preferred_element_type=F32).astype(BF)
        for part in (0, 1):
            for n, k in enumerate((0, 1, 3, 2)):
                start = part * PART + ((place_ref[1 + part] + k) % 4) * STRIP
                chunk = chunks[part * 5 + n + (shard // 2 if k == 2 else 0)]
                chunk[shard % 2 if k == 2 else shard] = strip[pl.ds(pl.multiple_of(start, 16), STRIP), :]


def experts_back(place_here, rows, d_rows, gates, made, active, steep, wide, low):
    count = 4 * ROWS
    column = pl.BlockSpec((count, HALF), lambda h: (0, h))
    return local_call(
        experts_back_kernel,
        (place_here, rows, d_rows, gates, made, active, steep, wide, low),
        [((count, D), BF), ((count, HD), BF)] + ([((4, STRIP, WIDE), BF)] * 3 + [((2, STRIP, WIDE), BF)] * 2) * 2,
        "experts_back",
        10_800_000_000,
        specs=[
            SMEM,
            whole((count, D)),
            whole((count, D)),
            whole((count, HD)),
            column,
            column,
            column,
            pl.BlockSpec((D, 2 * HALF), lambda h: (0, h)),
            pl.BlockSpec((HALF, D), lambda h: (h, 0)),
        ],
        out_specs=[whole((count, D)), whole((count, HD))]
        + (
            [pl.BlockSpec((4, STRIP, 3 * HALF), lambda h: (0, 0, h))] * 3
            + [pl.BlockSpec((2, STRIP, 3 * HALF), lambda h: (0, 0, h))] * 2
        )
        * 2,
        grid=(3,),
        scratch=[((count, D), F32), ((SHARD, SLICE), BF), ((D, count), BF), ((D, count), BF), ((count, HD), F32)],
    )


def attend_back_kernel(
    where,
    spans,
    q_ref,
    kv_ref,
    o_ref,
    lse_ref,
    cosine,
    sine,
    w_out,
    small,
    routes,
    probs_ref,
    hidden_ref,
    d_result,
    two_parts,
    gate_parts,
    d_hidden_ref,
    d_attn_ref,
    d_router_ref,
    dq_ref,
    dkv_ref,
    acc_ref,
    do_ref,
    turned_ref,
):
    d_gates = gate_parts[0].astype(F32) + gate_parts[1].astype(F32) + gate_parts[2].astype(F32)
    lanes = expert_lanes()
    first = (lanes >= FIRST) & (lanes < FIRST + E)
    d_select = jnp.where(first, (d_gates + pltpu.roll(d_gates, HD - LOW, 1)) * chosen(routes), 0.0)
    probs = jnp.where(first, probs_ref[...], 0.0)
    d_router = (probs * (d_select - jnp.sum(probs * d_select, axis=1, keepdims=True))).astype(BF)
    d_router_ref[...] = d_router
    d_normed = two_parts[0].astype(F32) + two_parts[1].astype(F32) + two_parts[2].astype(F32)
    d_normed = d_normed + jnp.dot(d_router, wide_router(small), preferred_element_type=F32)
    gain = small[...].astype(F32)[1:2, :]
    d_hidden = d_result[...] + norm_back(hidden_ref[...], gain, d_normed)
    d_hidden_ref[...] = d_hidden
    d_attn = d_hidden.astype(BF)
    for f in range(4):
        d_attn_ref[f] = d_attn[:, f * SHARD : (f + 1) * SHARD]
    for start in range(0, H * HD, 512):
        columns = slice(start, start + 512)
        do_ref[:, columns] = nt(d_attn, w_out[columns, :]).astype(BF)

    lead = lead_of_keys()
    acc_ref[...] = jnp.zeros_like(acc_ref)
    for s in range(2):
        span = spans[s]
        stacked = [stack_heads(q_ref, s, kv) for kv in range(KV)]
        d_out = [stack_heads(do_ref, s, kv) for kv in range(KV)]
        delta = [
            jnp.sum((d_out[kv].astype(F32) * stack_heads(o_ref, s, kv)).T, axis=0, keepdims=True) for kv in range(KV)
        ]
        lse = [lse_ref[2 * s + kv : 2 * s + kv + 1, :] for kv in range(KV)]

        def body(b, carry, last=False):
            keys_values = block_rows(where, b, kv_ref)
            out, key_grads, value_grads = [], [], []
            for kv in range(KV):
                keys = keys_values[:, head(kv)]
                values = keys_values[:, head(KV + kv)]
                weights = jnp.exp2(nt(keys, stacked[kv]) * SCALE_2 - lse[kv])
                if last:
                    weights = jnp.where(lead <= span * SPAN - b * BLOCK, weights, 0.0)
                d_weights = nt(values, d_out[kv])
                d_logits = (weights * (d_weights - delta[kv])).astype(BF)
                out.append(carry[kv] + tn(keys, d_logits))
                key_grads.append(jnp.dot(d_logits, stacked[kv], preferred_element_type=F32) * SCALE)
                value_grads.append(jnp.dot(weights.astype(BF), d_out[kv], preferred_element_type=F32))
            grads = jnp.concatenate(key_grads + value_grads, axis=1)
            for i in range(SPANS):
                rows = pl.ds(pl.multiple_of(where[b * SPANS + i] * SPAN, SPAN), SPAN)
                acc_ref[rows, :] += grads[i * SPAN : (i + 1) * SPAN, :]
            return tuple(out)

        start = tuple(jnp.zeros((HD, QUERIES), F32) for _ in range(KV))
        final = body(span // SPANS, lax.fori_loop(0, span // SPANS, body, start), last=True)
        for kv in range(KV):
            unstack_heads(turned_ref, s, kv, (final[kv] * SCALE).T)
    for k in range(H):
        dq_ref[:, head(k)] = turn(turned_ref[:, head(k)], cosine[...], -sine[...]).astype(BF)

    def put(i, carry):
        rows = pl.ds(pl.multiple_of(i * 256, 256), 256)
        dkv_ref[rows, :] = acc_ref[rows, :].astype(BF)
        return carry

    lax.fori_loop(0, acc_ref.shape[0] // 256, put, 0)


def attend_back(*args):
    length = args[3].shape[0]
    outs = [
        ((ROWS, D), F32),
        ((4, ROWS, SHARD), BF),
        ((ROWS, HD), BF),
        ((ROWS, H * HD), BF),
        ((length, 2 * KV * HD), BF),
    ]
    return local_call(
        attend_back_kernel,
        args,
        outs,
        "attend_back",
        5_000_000_000,
        specs=[SMEM, SMEM] + [VMEM] * 14,
        scratch=[((length, 2 * KV * HD), F32), ((ROWS, H * HD), BF), ((ROWS, H * HD), F32)],
    )


def blocks_kernel(dq_ref, keys, cosine, sine, blocks):
    for f in range(3):
        blocks[f] = dq_ref[:, f * 512 : (f + 1) * 512]
    for k in range(KV):
        turned = turn(keys[0, :, head(k)].astype(F32), cosine[...], -sine[...])
        blocks[3, :, head(k)] = turned.astype(BF)
    blocks[3, :, KV * HD :] = keys[1]


def query_blocks(*args):
    return local_call(blocks_kernel, args, [((4, ROWS, 512), BF)], "query_blocks", 1_000_000)[0]


def inputs_kernel(blocks, w_query, w_key, w_value, tokens, small, d_hidden, out):
    gain = small[...].astype(F32)[0:1, :]
    d_normed = nt(blocks[3, :, : KV * HD], w_key[...]) + nt(blocks[3, :, KV * HD :], w_value[...])
    for f in range(3):
        d_normed = d_normed + nt(blocks[f], w_query[:, f * 512 : (f + 1) * 512])
    out[...] = d_hidden[...] + norm_back(tokens[...].astype(F32), gain, d_normed)


def input_grads(*args):
    return local_call(inputs_kernel, args, [((ROWS, D), F32)], "input_grads", 800_000_000)[0]


def lay_out_kernel(place_ref, *refs):
    w_gate, w_up, w_router, router, gain, gate_out, up_out, down_out, gain_out, turned, sum_ref = refs[16:]
    part_sum = jnp.zeros((SHARD, HD), F32)
    for side in (0, 1):
        columns = slice(side * HALF, (side + 1) * HALF)
        for part in (0, 1):
            for n, k in enumerate((0, 1, 3, 2)):
                start = part * PART + ((place_ref[1 + part] + 4 - k) % 4) * STRIP
                rows = pl.ds(pl.multiple_of(start, 16), STRIP)
                piece = refs[side * 8 + part * 4 + n]
                gate_out[0, rows, columns] = piece[0, :, :HALF].astype(F32)
                up_out[0, rows, columns] = piece[0, :, HALF : 2 * HALF].astype(F32)
                turned[rows, :] = piece[0, :, 2 * HALF :].astype(F32)
        down_out[0, columns, :] = turned[...].T
        both = w_gate[0, :, columns].astype(F32) * gate_out[0, :, columns]
        both = both + w_up[0, :, columns].astype(F32) * up_out[0, :, columns]
        part_sum = part_sum + (both[:, :HD] + both[:, HD : 2 * HD] + both[:, 2 * HD :])

    @pl.when(pl.program_id(0) == 0)
    def _():
        sum_ref[...] = part_sum

    @pl.when(pl.program_id(0) != 0)
    def _():
        sum_ref[...] += part_sum

    @pl.when(pl.program_id(0) == E - 1)
    def _():
        total = jnp.sum(sum_ref[...], axis=1, keepdims=True)
        total = total + jnp.sum(w_router[...].astype(F32) * router[...], axis=1, keepdims=True)
        gain_out[...] = total.T / gain[...].astype(F32)


def lay_out_experts(place_here, pieces, w_gate, w_up, w_router, router, gain):
    def strips(side):
        return [pl.BlockSpec((1, STRIP, SLICE), lambda e: ((2 * e + side) // 3, 0, (2 * e + side) % 3))] * 8

    wide = pl.BlockSpec((1, SHARD, FF), lambda e: (e, 0, 0))
    return local_call(
        lay_out_kernel,
        (place_here,) + tuple(pieces) * 2 + (w_gate, w_up, w_router, router, gain),
        [((E, SHARD, FF), F32), ((E, SHARD, FF), F32), ((E, FF, SHARD), F32), ((1, SHARD), F32)],
        "lay_out_experts",
        20_000_000,
        specs=[SMEM] + strips(0) + strips(1) + [wide, wide, whole((SHARD, E)), whole((SHARD, E)), whole((1, SHARD))],
        out_specs=[wide, wide, pl.BlockSpec((1, FF, SHARD), lambda e: (e, 0, 0)), whole((1, SHARD))],
        grid=(E,),
        scratch=[((SHARD, HALF), F32), ((SHARD, HD), F32)],
    )


def attention_kernel(tail, w_query, w_key, w_value, gain, query, key, value, out, router, gain_out):
    total = jnp.zeros((SHARD, 1), F32)
    for f in range(3):
        columns = slice(f * 512, (f + 1) * 512)
        piece = tail[f, :, :512].astype(F32)
        query[:, columns] = piece
        total = total + jnp.sum(w_query[:, columns].astype(F32) * piece, axis=1, keepdims=True)
    for ref, weight, columns in ((key, w_key, slice(0, 256)), (value, w_value, slice(256, 512))):
        piece = tail[3, :, columns].astype(F32)
        ref[...] = piece
        total = total + jnp.sum(weight[...].astype(F32) * piece, axis=1, keepdims=True)
    gain_out[...] = total.T / gain[...].astype(F32)
    for f in range(4):
        out[:, f * SHARD : (f + 1) * SHARD] = tail[f, :, 512 : 512 + SHARD].astype(F32)
    pieces = [tail[f, :, 512 + SHARD :].astype(F32) for f in range(4)]
    router[...] = (pieces[0] + pieces[1] + pieces[2] + pieces[3])[:, FIRST : FIRST + E]


def lay_out_attention(*args):
    outs = [((SHARD, width), F32) for width in (D, KV * HD, KV * HD, D, E)] + [((1, SHARD), F32)]
    return local_call(attention_kernel, args, outs, "lay_out_attention", 4_000_000)


def add_halves_kernel(*refs):
    for n in range(4):
        refs[8 + n][...] = (refs[n][...].astype(F32) + refs[4 + n][...].astype(F32)).astype(BF)


def add_halves(blocks, halves):
    cell = WIDE // 4
    specs = [pl.BlockSpec((2, STRIP, cell), lambda n, side=side: (side, 0, n)) for side in (0, 1, 0, 1)]
    half_spec = pl.BlockSpec((2, STRIP, cell), lambda n: (0, 0, n))
    return pl.pallas_call(
        add_halves_kernel,
        out_shape=[jax.ShapeDtypeStruct(block.shape, BF) for block in blocks],
        grid=(4,),
        in_specs=specs + [half_spec] * 4,
        out_specs=specs,
        input_output_aliases={n: n for n in range(4)},
        compiler_params=pltpu.CompilerParams(vmem_limit_bytes=32 << 20),
        cost_estimate=pl.CostEstimate(flops=1000, transcendentals=0, bytes_accessed=1000),
        name="add_halves",
    )(*blocks, *halves)


def shift_pairs(axis, k):
    pairs = []
    for ctx in range(32):
        x, z, y_lo = ctx // 8, (ctx // 2) % 4, ctx % 2
        if axis == 0:
            pairs.append((ctx, (x + k) % 4 * 8 + z * 2 + y_lo))
        else:
            pairs.append((ctx, x * 8 + (z + k) % 4 * 2 + y_lo))
    return pairs


def shift(array, axis, k):
    return lax.ppermute(array, "ctx", shift_pairs(axis, k))


def local(
    tokens,
    teacher,
    valid_mask,
    token_count,
    routes,
    span_order,
    w_query,
    w_key,
    w_value,
    w_out,
    norm_gain,
    w_router,
    moe_gain,
    w_gate,
    w_up,
    w_down,
):
    rows = tokens[0]
    ctx = lax.axis_index("ctx")
    shard = lax.axis_index("fsdp")
    x, z, _, _, _ = place()
    place_here = jnp.stack([shard, x, z])
    spans = lax.dynamic_slice(span_order, (ctx * 2,), (2,))
    numbers = jnp.arange(64, dtype=jnp.int32)
    where = jnp.sum(jnp.where(span_order[None, :] == numbers[:, None], numbers[None, :], 0), axis=1)

    small = jnp.concatenate(
        [norm_gain[None, :], moe_gain[None, :], w_router.T, jnp.zeros((16 - 2 - E, SHARD), BF)], axis=0
    )
    full_query, full_key, full_value, full_out, small = gather_attention_weights(
        (w_query, w_key, w_value, w_out), small, 1
    )
    input_one, query, keys_values, cosine, sine = project(spans, rows, small, full_query, full_key, full_value)
    keys, quarters = gather_keys(keys_values, (w_gate, w_up, w_down), 2)
    keys = keys.reshape(32 * ROWS, 2 * KV * HD)
    attended, attended_low, lse, hidden, input_two, gates_sent, probs = attend(
        where, spans, query, keys, rows, full_out, small, routes[0]
    )

    group_two, gates, wide, low = group_spread(
        (input_two, gates_sent), 3, "group_normed", (w_gate, w_up, w_down, quarters)
    )
    group_two, gates = group_two.reshape(4 * ROWS, D), gates.reshape(4 * ROWS, HD)
    mixed, *kept = experts(place_here, group_two, gates, wide, low)
    (mixed,) = group_sum((mixed.reshape(4, ROWS, D),), 4, "group_mixture")
    result, d_result, d_low, squared = combine(mixed, hidden, teacher[0], valid_mask, token_count)
    (group_d,) = group_spread((d_low,), 5, "group_d_result")
    d_two, d_gates_sent, *chunks = experts_back(
        place_here, group_two, group_d.reshape(4 * ROWS, D), gates, *kept, wide, low
    )
    halfway = [shift(chunks[part * 5 + 3 + n], part, (1, 3)[n]) for n in (0, 1) for part in (0, 1)]
    two_parts, gate_parts, squared = group_sum(
        (d_two.reshape(4, ROWS, D), d_gates_sent.reshape(4, ROWS, HD)), 6, "group_d_normed", squared
    )
    squared = jnp.sum(squared, axis=0)
    halfway, two_parts = lax.optimization_barrier((halfway, two_parts))
    sums = add_halves(
        (chunks[1], chunks[2], chunks[6], chunks[7]), (halfway[0], halfway[2], halfway[1], halfway[3])
    )
    came = [[chunks[part * 5], shift(sums[part * 2], part, 1), shift(sums[part * 2 + 1], part, 3)] for part in (0, 1)]
    d_hidden, d_attn_blocks, d_router, d_query, d_keys = attend_back(
        where,
        spans,
        query,
        keys,
        attended,
        lse,
        cosine,
        sine,
        full_out,
        small,
        routes[0],
        probs,
        hidden,
        d_result,
        two_parts,
        gate_parts,
    )

    expert_sum, tail_sum, key_sum, loss_sum = GradSum(WIDE, 1), GradSum(TAIL, 0), KeySum(), LossSum()
    came, d_keys = lax.optimization_barrier((came, d_keys))
    part = add_strips(came[0] + came[1])
    share = GroupShare((attended_low, input_one), (d_attn_blocks,))
    part, d_keys, squared, group_attended, group_one, group_d_attn = sum_step(
        (
            (expert_sum, part, 1),
            (key_sum, d_keys.reshape(4, 4, 2, ROWS, 2 * KV * HD), 0),
            (loss_sum, squared, 0),
        ),
        7,
        "sums_first",
        (share,),
    )
    d_keys, squared, part = sum_step(
        ((key_sum, d_keys, 1), (loss_sum, squared, 1), (expert_sum, part, 2)), 8, "sums_second"
    )
    d_keys, squared, *strips = sum_step(
        ((key_sum, d_keys, 2), (loss_sum, squared, 2)), 9, "sums_third", (Hand(part, WIDE, True),)
    )
    pieces = [[strips[part], shift(strips[part], part, 1), shift(strips[part], part, 3)] for part in (0, 1)]
    norm_factor = token_count[0].astype(F32) * D
    loss_value = (squared[0, 0] / norm_factor).reshape(1)

    blocks = query_blocks(d_query, d_keys, cosine, sine)
    (group_d_qkv,) = sum_step((), 10, "group_d_qkv", (GroupShare((), (blocks,)),))
    tail = tail_grads(
        group_one.reshape(4 * ROWS, D),
        group_d_qkv.reshape(4 * ROWS, 512),
        group_attended.reshape(4 * ROWS, D),
        group_d_attn.reshape(4 * ROWS, SHARD),
        input_two,
        d_router,
    )
    d_inputs = input_grads(blocks, full_query, full_key, full_value, rows, small, d_hidden)
    pieces, tail, d_inputs = lax.optimization_barrier((pieces, tail, d_inputs))
    tail, *halves = sum_step(
        ((tail_sum, tail, 0),), 11, "tail_a", (Forward([pieces[0][1], pieces[1][1]], [pieces[0][2], pieces[1][2]]),)
    )
    for part in (0, 1):
        pieces[part].append(halves[part])
    (tail,) = sum_step(((tail_sum, tail, 1),), 12, "tail_b")
    (tail,) = sum_step(((tail_sum, tail, 2),), 13, "tail_c")
    (tail,) = sum_step((), 14, "tail_gather", (Hand(tail, TAIL, False),))
    grad_query, grad_key, grad_value, grad_out, grad_router, grad_gain_one = lay_out_attention(
        tail.reshape(4, SHARD, TAIL), w_query, w_key, w_value, norm_gain[None]
    )
    grad_gate, grad_up, grad_down, grad_gain_two = lay_out_experts(
        place_here, [one.reshape((-1,) + one.shape[-2:]) for one in pieces[0] + pieces[1]], w_gate, w_up, w_router, grad_router, moe_gain[None]
    )
    return (
        result[None],
        loss_value,
        d_inputs[None],
        grad_query,
        grad_key,
        grad_value,
        grad_out,
        grad_gain_one[0],
        grad_router,
        grad_gain_two[0],
        grad_gate,
        grad_up,
        grad_down,
    )


def solution(mesh):
    in_specs = (
        P("fsdp", "ctx", None),
        P("fsdp", "ctx", None),
        P("fsdp", "ctx"),
        P(),
        P("fsdp", "ctx", None),
        P(),
        P("fsdp", None),
        P("fsdp", None),
        P("fsdp", None),
        P("fsdp", None),
        P("fsdp"),
        P("fsdp", None),
        P("fsdp"),
        P(None, "fsdp", None),
        P(None, "fsdp", None),
        P(None, None, "fsdp"),
    )
    out_specs = (
        P("fsdp", "ctx", None),
        P(),
        P("fsdp", "ctx", None),
        P("fsdp", None),
        P("fsdp", None),
        P("fsdp", None),
        P("fsdp", None),
        P("fsdp"),
        P("fsdp", None),
        P("fsdp"),
        P(None, "fsdp", None),
        P(None, "fsdp", None),
        P(None, None, "fsdp"),
    )
    return jax.shard_map(local, mesh=mesh, in_specs=in_specs, out_specs=out_specs, check_vma=False)
```

```python
import itertools
import math

import jax
import jax.numpy as jnp
from jax import lax
from jax.experimental import pallas as pl
from jax.experimental.pallas import tpu as pltpu
from jax.sharding import PartitionSpec as P

H = 12
KV = 2
HD = 128
E = 6
D = 1536
FF = 768
GROUPS = H // KV
ROWS = 128
SPAN = 64
HALF = 384
SLICE = 3 * HALF
QKV = 2048
SHARD = 384
WIDE = 3 * SLICE + 128
TAIL = 1024
PART = SHARD // 2
STRIP = PART // 4
EPS = 1e-06
BASE = 1000000.0
NEGATIVE = -1e30
SCALE = HD**-0.5
LOG2_E = math.log2(math.e)
SCALE_2 = SCALE * LOG2_E
MESH = pl.DeviceIdType.MESH
BF = jnp.bfloat16
F32 = jnp.float32


def place():
    ctx = lax.axis_index("ctx")
    shard = lax.axis_index("fsdp")
    return ctx // 8, (ctx // 2) % 4, ctx % 2, shard // 2, shard % 2


def device(x, z, y_lo, y_hi, core):
    return (x * 8 + z * 2 + y_lo, y_hi * 2 + core)


def x_peers(at):
    x, z, y_lo, y_hi, core = at
    return [device((x + k) % 4, z, y_lo, y_hi, core) for k in (1, 2, 3)]


def x_next(at):
    peers = x_peers(at)
    return [peers[0], peers[2]]


def z_next(at):
    peers = z_peers(at)
    return [peers[0], peers[2]]


def z_peers(at):
    x, z, y_lo, y_hi, core = at
    return [device(x, (z + k) % 4, y_lo, y_hi, core) for k in (1, 2, 3)]


def group_member(at, shard_hi, core):
    x, z, y_lo, y_hi, _ = at
    y_lo_there = (y_lo + y_hi + shard_hi) % 2
    return device(x, z, y_lo_there, shard_hi, core)


class Net:
    def __init__(self, send_sem, recv_sem, local_sem, extra_sem, stage):
        self.sems = (send_sem, recv_sem, local_sem, extra_sem)
        self.extra = 0
        self.stage = stage
        self.remote = 0
        self.loads = []
        self.kept = 0
        self.open = {}
        self.copies = []

    def greet(self, peers):
        barrier = pltpu.get_barrier_semaphore()
        for peer in peers:
            pl.semaphore_signal(barrier, inc=1, device_id=peer, device_id_type=MESH)
        pl.semaphore_wait(barrier, len(peers))

    def _open(self, copy):
        copy.start()
        self.open[id(copy)] = copy.wait
        self.copies.append(copy)
        return copy

    def send(self, src, dst, peer):
        slot = self.remote
        self.remote += 1
        return self._open(
            pltpu.make_async_remote_copy(
                src_ref=src,
                dst_ref=dst,
                send_sem=self.sems[0].at[slot],
                recv_sem=self.sems[1].at[slot],
                device_id=peer,
                device_id_type=MESH,
            )
        )

    def keep(self, src, dst):
        slot = self.kept
        self.kept += 1
        load = pltpu.make_async_copy(src, self.stage[slot], self.sems[2].at[slot])
        load.start()
        self.loads.append((load, slot, dst))

    def settle(self):
        stores = []
        for load, slot, dst in self.loads:
            load.wait()
            stores.append(self._open(pltpu.make_async_copy(self.stage[slot], dst, self.sems[2].at[slot])))
        self.loads = []
        return stores

    def done(self, copies):
        for copy in copies:
            copy.wait()
            del self.open[id(copy)]

    def arrived(self, copy):
        copy.wait_recv()
        self.open[id(copy)] = copy.wait_send

    def finish(self):
        self.settle()
        for wait in self.open.values():
            wait()


def exchange(body, inputs, outs, remote, keeps, number, name, scratch=()):
    count = len(inputs)
    total = count + len(outs)

    def kernel(*refs):
        net = Net(*refs[total : total + 4], refs[total + 4 :])
        body(net, refs[:count], refs[count:total])
        net.finish()

    any_spec = pl.BlockSpec(memory_space=pl.ANY)
    return pl.pallas_call(
        kernel,
        out_shape=[jax.ShapeDtypeStruct(shape, kind) for shape, kind in outs],
        in_specs=[any_spec] * count,
        out_specs=[any_spec] * len(outs),
        scratch_shapes=[
            pltpu.SemaphoreType.DMA((remote,)),
            pltpu.SemaphoreType.DMA((remote,)),
            pltpu.SemaphoreType.DMA((len(keeps) + len(scratch) + 1,)),
            pltpu.SemaphoreType.DMA((2 * len(scratch) + 1,)),
        ]
        + [pltpu.VMEM(shape, kind) for shape, kind in list(keeps) + list(scratch)],
        compiler_params=pltpu.CompilerParams(
            collective_id=number, has_side_effects=True, vmem_limit_bytes=60 << 20
        ),
        name=name,
    )(*inputs)


def ring_of(at):
    x, z, y_lo, y_hi, core = at
    return [
        device(
            lax.select(core == 0, (x + k) % 4, x), lax.select(core == 0, z, (z + k) % 4), y_lo, y_hi, core
        )
        for k in (1, 3)
    ]


class Ring:
    def __init__(self, net, blocks, own, neighbours):
        self.net, self.blocks, self.own, self.neighbours = net, blocks, own, neighbours
        self.first, self.rest = [], []

    def send(self, origin, half, way):
        return [self.net.send(ref, ref, self.neighbours[way]) for ref in self.blocks(origin, half)]

    def start(self):
        self.start_half(0)
        self.start_half(1)
        return self

    def start_half(self, half):
        self.first.append(self.send(self.own, half, half))
        self.rest.append(self.send(self.own, half, 1 - half))

    def forward(self):
        self.last = []
        for way in (0, 1):
            for copy in self.first[way]:
                self.net.arrived(copy)
            self.last.append(self.send((self.own + (3, 1)[way]) % 4, way, way))
        return self

    def finish(self):
        for copies in self.rest + self.last:
            for copy in copies:
                self.net.arrived(copy)


def gather_attention_weights(parts, small, number):
    count = len(parts)

    def body(net, ins, outs):
        at = place()
        x, z, y_lo, y_hi, core = at
        shard = y_hi * 2 + core
        sibling = device(x, z, y_lo, y_hi, 1 - core)
        partner = device(x, z, 1 - y_lo, 1 - y_hi, core)
        crossed = device(x, z, 1 - y_lo, 1 - y_hi, 1 - core)
        here = lax.select(core == 0, x, z)
        ring = ring_of(at)
        net.greet([sibling, partner, crossed] + ring)
        small_spot = outs[count].at[:, pl.ds(pl.multiple_of(shard * SHARD, 128), SHARD)]
        for peer in (partner, crossed, sibling):
            net.send(ins[count], small_spot, peer)

        def block(array, owner, start, size):
            width = ins[array].shape[1]
            return outs[array].at[pl.ds(pl.multiple_of(owner * SHARD + start, 16), size), pl.ds(0, width)]

        quarter = SHARD // 4
        order = (3, 0, 1, 2)
        part = quarter // 2
        first = {}
        for a in order:
            for half in (0, 1):
                start = here * quarter + half * part
                rows = pl.ds(pl.multiple_of(start, 16), part)
                first[a, half] = net.send(ins[a].at[rows, :], block(a, shard, start, part), partner)
        for a in order:
            net.send(ins[a], block(a, shard, 0, SHARD), sibling)
            net.keep(ins[a], block(a, shard, 0, SHARD))
        net.keep(ins[count], small_spot)
        net.settle()
        far = (1 - y_hi) * 2 + core
        rings = {}
        for a in order:

            def halves(origin, half, a=a):
                return [block(a, far, origin * quarter + half * part, part)]

            rings[a] = Ring(net, halves, here, ring)
            for half in (0, 1):
                net.arrived(first[a, half])
                rings[a].start_half(half)
            mine = block(a, far, here * quarter, quarter)
            net.send(mine, mine, sibling)
        for a in order:
            rings[a].forward()
        for a in order:
            rings[a].finish()
            for k in (1, 2, 3):
                piece = block(a, far, (here + k) % 4 * quarter, quarter)
                net.send(piece, piece, sibling)

    return exchange(
        body,
        tuple(parts) + (small,),
        [((D, part.shape[1]), BF) for part in parts] + [((16, D), BF)],
        count * 13 + 3,
        [(parts[a].shape, BF) for a in (3, 0, 1, 2)] + [((16, SHARD), BF)],
        number,
        "attention_weights",
    )


class ExpertWeights:
    quarter = HALF // 4
    cells = [(h, kind) for h in range(3) for kind in range(3)]

    def source(self, ins, owner, h, kind, start, size):
        index = owner * 3 + h
        expert = index // 2
        offset = pl.multiple_of((index % 2) * HALF, 128)
        if kind < 2:
            return ins[kind].at[expert, pl.ds(start, size), pl.ds(offset, HALF)]
        return ins[2].at[expert, pl.ds(pl.multiple_of(offset + start, 32), size), :]

    def target(self, outs, from_shard, h, kind, start, size):
        if kind < 2:
            rows = pl.multiple_of(from_shard * SHARD + start, 32)
            return outs[0].at[pl.ds(rows, size), pl.ds((2 * h + kind) * HALF, HALF)]
        columns = pl.multiple_of(from_shard * SHARD, 128)
        return outs[1].at[pl.ds(pl.multiple_of(h * HALF + start, 32), size), pl.ds(columns, SHARD)]

    def cross(self, net, ins, quarters, at):
        x, z, y_lo, y_hi, core = at
        for step in (0, 1):
            far_core = (core + step) % 2
            start = pl.multiple_of(lax.select(far_core == 0, x, z) * self.quarter, 32)
            owner = (1 - y_hi) * 2 + far_core
            peer = device(x, z, 1 - y_lo, 1 - y_hi, far_core)
            for n, (h, kind) in enumerate(self.cells):
                net.send(self.source(ins, owner, h, kind, start, self.quarter), quarters.at[step, n], peer)

    def around(self, net, ins, quarters, outs, at):
        x, z, y_lo, y_hi, core = at
        shard = y_hi * 2 + core
        sibling = device(x, z, y_lo, y_hi, 1 - core)
        here = lax.select(core == 0, x, z)

        def spots(origin, step):
            start = pl.multiple_of(origin * self.quarter, 32)
            from_shard = (1 - y_hi) * 2 + (core + step) % 2
            return [self.target(outs, from_shard, h, kind, start, self.quarter) for h, kind in self.cells]

        first, neighbours = [], ring_of(at)
        for turn in (0, 1):
            for way in (0, 1):
                step = way if turn == 0 else 1 - way
                copies = [
                    net.send(quarters.at[step, n], spot, neighbours[way]) for n, spot in enumerate(spots(here, step))
                ]
                if turn == 0:
                    first.append(copies)
        for step in (0, 1):
            for n, spot in enumerate(spots(here, step)):
                net.keep(quarters.at[step, n], spot)
        for h, kind in self.cells:
            other = y_hi * 2 + 1 - core
            net.send(self.source(ins, other, h, kind, 0, HALF), self.target(outs, shard, h, kind, 0, HALF), sibling)
            net.keep(self.source(ins, shard, h, kind, 0, HALF), self.target(outs, shard, h, kind, 0, HALF))
        return first, spots, here, neighbours

    def forward(self, net, state):
        first, spots, here, neighbours = state
        for n in range(len(self.cells)):
            for way in (0, 1):
                net.arrived(first[way][n])
                spot = spots((here + (3, 1)[way]) % 4, way)[n]
                net.send(spot, spot, neighbours[way])


EXPERT = ExpertWeights()


def gather_keys(local, experts, number):
    def body(net, ins, outs):
        mine, whole = ins[0], outs[0]
        at = place()
        x, z, y_lo, y_hi, core = at
        partner = device(x, z, 1 - y_lo, y_hi, core)
        across = [device(x, z, 1 - y_lo, 1 - y_hi, c) for c in (0, 1)]
        net.greet([partner] + x_next(at) + z_next(at) + across)
        spot = whole.at[x, z, y_lo]
        near = net.send(mine, spot, partner)
        net.keep(mine, spot)
        EXPERT.cross(net, ins[1:], outs[1], at)
        net.done(net.settle())
        net.arrived(near)
        half = KV * HD
        cuts = [pl.ds(part * half, half) for part in (0, 1)]
        sides = (x_next(at), z_next(at))
        near_rings = (
            Ring(net, lambda o, h: [whole.at[x, o, h, :, cuts[0]]], z, sides[1]),
            Ring(net, lambda o, h: [whole.at[o, z, h, :, cuts[1]]], x, sides[0]),
        )
        own = ((x, z), (z, x))

        def far_ring(part, other):
            if part == 0:
                return Ring(net, lambda o, h: [whole.at[o, other, h, :, cuts[0]]], x, sides[0])
            return Ring(net, lambda o, h: [whole.at[other, o, h, :, cuts[1]]], z, sides[1])

        for ring in near_rings:
            ring.start()
        far_rings = [far_ring(part, own[part][1]).start() for part in (0, 1)]
        for ring in near_rings:
            ring.forward()
        for way, step in ((1, 3), (0, 1)):
            for part in (0, 1):
                for copy in near_rings[part].rest[way]:
                    net.arrived(copy)
                far_rings.append(far_ring(part, (own[part][1] + step) % 4).start())
        for part in (0, 1):
            for copies in near_rings[part].last:
                for copy in copies:
                    net.arrived(copy)
            far_rings.append(far_ring(part, (own[part][1] + 2) % 4).start())
        for ring in far_rings:
            ring.forward()

    return exchange(
        body,
        (local,) + experts,
        [((4, 4, 2, ROWS, 2 * KV * HD), BF), ((2, 9, EXPERT.quarter, HALF), BF)],
        61 + 18,
        [((ROWS, 2 * KV * HD), BF)],
        number,
        "keys_values",
    )


def group_places(at):
    x, z, y_lo, y_hi, core = at
    sibling = device(x, z, y_lo, y_hi, 1 - core)
    partner = device(x, z, 1 - y_lo, 1 - y_hi, core)
    return sibling, partner


class Spread:
    def start(self, net, mine, whole, at):
        sibling, partner = group_places(at)
        spot = whole.at[at[3] * 2 + at[4]]
        self.copy = net.send(mine, spot, partner)
        net.send(mine, spot, sibling)
        net.keep(mine, spot)

    def forward(self, net, whole, at):
        sibling, partner = group_places(at)
        net.arrived(self.copy)
        far = whole.at[(1 - at[3]) * 2 + at[4]]
        net.send(far, far, sibling)


def group_spread(parts, number, name, weights=None):
    count = len(parts)
    keeps = [(part.shape, part.dtype) for part in parts]
    outs = [((4,) + part.shape, part.dtype) for part in parts]
    inputs = tuple(parts)
    remote = 3 * count
    if weights is not None:
        inputs += weights
        outs += [((D, 2 * SLICE), BF), ((SLICE, D), BF)]
        remote += 7 * 9
        keeps += [((EXPERT.quarter, HALF), BF)] * 18 + [((HALF, HALF), BF)] * 9

    def body(net, ins, outs):
        at = place()
        sibling, partner = group_places(at)
        net.greet([sibling, partner] + (ring_of(at) if weights is not None else []))
        spreads = [Spread() for _ in range(count)]
        for one, mine, whole in zip(spreads, ins, outs):
            one.start(net, mine, whole, at)
        if weights is not None:
            state = EXPERT.around(net, ins[count:-1], ins[-1], outs[count:], at)
        net.settle()
        for one, whole in zip(spreads, outs):
            one.forward(net, whole, at)
        if weights is not None:
            EXPERT.forward(net, state)

    return exchange(body, inputs, outs, remote, keeps, number, name)


def group_sum(parts, number, name, extra=None):
    count = len(parts)
    spread = () if extra is None else (extra,)
    keeps = [(part.shape[1:], BF) for part in parts] + [(one.shape, one.dtype) for one in spread]
    outs = [((3,) + part.shape[1:], BF) for part in parts] + [((4,) + one.shape, one.dtype) for one in spread]
    scratch = [((2,) + part.shape[1:], BF) for part in parts]

    def body(net, ins, outs):
        at = place()
        x, z, y_lo, y_hi, core = at
        sibling, partner = group_places(at)
        net.greet([sibling, partner])
        sums = net.stage[len(keeps) :]
        far = (1 - y_hi) * 2
        came, own = [], []
        for mine, pair in zip(ins, sums):
            came.append(net.send(mine.at[far + 1 - core], pair.at[1], sibling))
            load = pltpu.make_async_copy(mine.at[far + core], pair.at[0], net.sems[2].at[len(keeps) + len(own)])
            load.start()
            own.append(load)
        for mine, got in zip(ins[:count], outs):
            net.send(mine.at[y_hi * 2 + 1 - core], got.at[1], sibling)
            net.keep(mine.at[y_hi * 2 + core], got.at[0])
        spreads = []
        for mine, whole in zip(ins[count:], outs[count:]):
            spreads.append(Spread())
            spreads[-1].start(net, mine, whole, at)
        for n, pair in enumerate(sums):
            own[n].wait()
            net.arrived(came[n])

            def add(step, carry):
                rows = pl.ds(pl.multiple_of(step * 16, 16), 16)
                pair[0, rows, :] = (pair[0, rows, :].astype(F32) + pair[1, rows, :].astype(F32)).astype(BF)
                return carry

            lax.fori_loop(0, pair.shape[1] // 16, add, 0)
            net.send(pair.at[0], outs[n].at[2], partner)
        net.settle()
        for one, whole in zip(spreads, outs[count:]):
            one.forward(net, whole, at)

    return exchange(
        body, tuple(parts) + spread, outs, 3 * (count + len(spread)), keeps, number, name, scratch
    )


def add_up(pieces, axis):
    return jnp.sum(pieces.astype(F32), axis=axis).astype(BF)


def add_strips_kernel(*refs):
    for part in (0, 1):
        three = [refs[part * 3 + n][...].astype(F32) for n in range(3)]
        refs[6][part] = (three[0] + three[1] + three[2]).astype(BF)


def add_strips(strips):
    cell = SLICE
    return local_call(
        add_strips_kernel,
        tuple(strips),
        [((2, 4, STRIP, WIDE), BF)],
        "add_strips",
        1000,
        specs=[pl.BlockSpec((4, STRIP, cell), lambda n: (0, 0, n))] * 6,
        out_specs=[pl.BlockSpec((2, 4, STRIP, cell), lambda n: (0, 0, 0, n))],
        grid=(3,),
    )[0]


class RingSum:
    def __init__(self, net, block, place_of, own, neighbours, pair):
        self.net, self.block, self.place_of, self.own = net, block, place_of, own
        self.neighbours, self.pair = neighbours, pair

    def start(self):
        net = self.net
        self.came = [
            net.send(self.block((self.own + 2) % 4, way), self.pair.at[way, 1], self.neighbours[way]) for way in (0, 1)
        ]
        self.loads = []
        for way in (0, 1):
            target = (self.own + (1, 3)[way]) % 4
            load = pltpu.make_async_copy(self.block(target, way), self.pair.at[way, 0], net.sems[3].at[net.extra])
            net.extra += 1
            load.start()
            self.loads.append(load)
            net.send(self.block(target, 1 - way), self.place_of(1 + way, 1 - way), self.neighbours[way])
        for half in (0, 1):
            net.keep(self.block(self.own, half), self.place_of(0, half))

    def forward(self):
        net, pair = self.net, self.pair
        *lead, rows, _ = pair.shape[2:]
        for way in (0, 1):
            self.loads[way].wait()
            net.arrived(self.came[way])
            for spot in itertools.product(*(range(size) for size in lead)):

                def add(step, carry):
                    cut = pl.ds(pl.multiple_of(step * 16, 16), 16)
                    own, came = pair[(way, 0) + spot + (cut,)], pair[(way, 1) + spot + (cut,)]
                    pair[(way, 0) + spot + (cut,)] = (own.astype(F32) + came.astype(F32)).astype(BF)
                    return carry

                lax.fori_loop(0, rows // 16, add, 0)
            net.send(pair.at[way, 0], self.place_of(1 + way, way), self.neighbours[way])


class KeySum:
    half = KV * HD
    shapes = (
        ((2, 3, 4, 2, ROWS, KV * HD), BF),
        ((2, 4, 2, ROWS, KV * HD), BF),
        ((2, 2, ROWS, KV * HD), BF),
    )
    pairs = ([((2, 2, 2, 2, ROWS, KV * HD), BF)] * 2, [], [])
    keeps = (
        [((2, 2, ROWS, KV * HD), BF)] * 4,
        [((2, ROWS, KV * HD), BF)] * 2,
        [((2, ROWS, KV * HD), BF)],
    )

    def first(self, net, whole, got, at, pairs):
        cuts = [pl.ds(part * self.half, self.half) for part in (0, 1)]
        blocks = (
            lambda target, half: whole.at[target, pl.ds(2 * half, 2), :, :, cuts[0]],
            lambda target, half: whole.at[pl.ds(2 * half, 2), target, :, :, cuts[1]],
        )
        sides = (x_next(at), z_next(at))
        return [
            RingSum(
                net,
                blocks[part],
                lambda n, half, part=part: got.at[part, n, pl.ds(2 * half, 2)],
                at[part],
                sides[part],
                pairs[part],
            )
            for part in (0, 1)
        ]

    def second(self, net, whole, got, at, pairs):
        x, z = at[0], at[1]
        peers = (x_peers(at), z_peers(at))
        for k in (2, 1, 3):
            net.send(whole.at[0, (z + k) % 4], got.at[0, k], peers[1][k - 1])
            net.send(whole.at[1, (x + k) % 4], got.at[1, k], peers[0][k - 1])
        net.keep(whole.at[0, z], got.at[0, 0])
        net.keep(whole.at[1, x], got.at[1, 0])

    def third(self, net, whole, got, at, pairs):
        x, z, y_lo, y_hi, core = at
        net.send(whole.at[:, 1 - y_lo], got.at[1], device(x, z, 1 - y_lo, y_hi, core))
        net.keep(whole.at[:, y_lo], got.at[0])


class GradSum:
    def __init__(self, columns, ring_step):
        self.columns, self.cell, self.ring_step = columns, columns // 4, ring_step
        widths = (columns, self.cell)
        came = [3 if ring_step == step else 4 for step in (0, 1)]
        self.shapes = tuple(((2, came[step], 4, STRIP, widths[step]), BF) for step in (0, 1))
        self.shapes += (((2, 2, 2, STRIP, self.cell), BF),)
        self.keeps = tuple(
            [((2, STRIP, widths[step]), BF)] * 4 if ring_step == step else [((4, STRIP, widths[step]), BF)] * 2
            for step in (0, 1)
        )
        self.keeps += ([((2, STRIP, self.cell), BF)],)
        self.pairs = tuple(
            [((2, 2, 2, STRIP, widths[step]), BF)] * 2 if ring_step == step else [] for step in (0, 1)
        ) + ([],)

    def rings(self, net, block, got, own, sides, pairs):
        return [
            RingSum(
                net,
                lambda target, half, part=part: block(part, target, pl.ds(2 * half, 2)),
                lambda n, half, part=part: got.at[part, n, pl.ds(2 * half, 2)],
                own[part],
                sides[part],
                pairs[part],
            )
            for part in (0, 1)
        ]

    def direct(self, net, block, got, own, peers):
        for k in (2, 1, 3, 0):
            for part in (0, 1):
                piece = block(part, (own[part] + k) % 4, slice(None))
                if k == 0:
                    net.keep(piece, got.at[part, 0])
                else:
                    net.send(piece, got.at[part, k], peers[part][k - 1])

    def first(self, net, whole, got, at, pairs):
        def block(part, target, sets):
            return whole.at[sets, pl.ds(pl.multiple_of(part * PART + target * STRIP, 16), STRIP), :]

        if self.ring_step == 0:
            return self.rings(net, block, got, (at[0], at[1]), (x_next(at), z_next(at)), pairs)
        return self.direct(net, block, got, (at[0], at[1]), (x_peers(at), z_peers(at)))

    def second(self, net, whole, got, at, pairs):
        def block(part, target, sets):
            return whole.at[part, sets, :, pl.ds(pl.multiple_of(target * self.cell, 128), self.cell)]

        if self.ring_step == 1:
            return self.rings(net, block, got, (at[1], at[0]), (z_next(at), x_next(at)), pairs)
        return self.direct(net, block, got, (at[1], at[0]), (z_peers(at), x_peers(at)))

    def third(self, net, whole, got, at, pairs):
        x, z, y_lo, y_hi, core = at
        spot = got.at[y_lo, y_hi]
        for k in (2, 3, 1):
            there_hi, there_core = (y_hi + k // 2) % 2, (y_lo + k % 2) % 2
            net.send(whole.at[:, there_hi * 2 + there_core], spot, device(x, z, core, there_hi, there_core))
        mine = whole.at[:, y_hi * 2 + y_lo]
        slot, held = net.remote, net.kept
        net.remote += 1
        net.kept += 1
        stage, sem = net.stage[held], net.sems[2].at[held]

        @pl.when(core == y_lo)
        def _():
            load = pltpu.make_async_copy(mine, stage, sem)
            load.start()
            load.wait()
            store = pltpu.make_async_copy(stage, spot, sem)
            store.start()
            store.wait()

        @pl.when(core != y_lo)
        def _():
            copy = pltpu.make_async_remote_copy(
                src_ref=mine,
                dst_ref=spot,
                send_sem=net.sems[0].at[slot],
                recv_sem=net.sems[1].at[slot],
                device_id=device(x, z, core, y_hi, y_lo),
                device_id_type=MESH,
            )
            copy.start()
            copy.wait()


class LossSum:
    shapes = (((4, 8, 128), F32), ((4, 8, 128), F32), ((2, 8, 128), F32))
    keeps = ([((8, 128), F32)],) * 3
    pairs = ([],) * 3

    def first(self, net, whole, got, at, pairs):
        for peer in x_peers(at):
            net.send(whole, got.at[at[0]], peer)
        net.keep(whole, got.at[at[0]])

    def second(self, net, whole, got, at, pairs):
        for peer in z_peers(at):
            net.send(whole, got.at[at[1]], peer)
        net.keep(whole, got.at[at[1]])

    def third(self, net, whole, got, at, pairs):
        x, z, y_lo, y_hi, core = at
        net.send(whole, got.at[y_lo], device(x, z, 1 - y_lo, y_hi, core))
        net.keep(whole, got.at[y_lo])


class GroupShare:
    def __init__(self, spread, swapped):
        self.count = len(spread)
        self.inputs = tuple(spread) + tuple(swapped)
        self.outs = [((4,) + one.shape, BF) for one in spread] + [(one.shape, BF) for one in swapped]
        self.keeps = [(one.shape, BF) for one in spread] + [(one.shape[1:], BF) for one in swapped]

    def peers(self, at):
        x, z, y_lo, y_hi, core = at
        return [device(x, z, 1 - y_lo, 1 - y_hi, 1 - core), *group_places(at)]

    def start(self, net, ins, outs, at):
        x, z, y_lo, y_hi, core = at
        crossed, sibling, partner = self.peers(at)
        shard = y_hi * 2 + core
        far = (1 - y_hi) * 2
        for mine, whole in zip(ins[self.count :], outs[self.count :]):
            net.send(mine.at[far + core], whole.at[shard], partner)
            net.send(mine.at[far + 1 - core], whole.at[shard], crossed)
            net.send(mine.at[y_hi * 2 + 1 - core], whole.at[shard], sibling)
        self.spreads = []
        for mine, whole in zip(ins, outs[: self.count]):
            self.spreads.append(Spread())
            self.spreads[-1].start(net, mine, whole, at)
        for mine, whole in zip(ins[self.count :], outs[self.count :]):
            net.keep(mine.at[shard], whole.at[shard])

    def forward(self, net, outs, at):
        for one, whole in zip(self.spreads, outs):
            one.forward(net, whole, at)


class Forward:
    def __init__(self, behind, ahead):
        self.inputs = tuple(behind) + tuple(ahead)
        self.outs = [(one.shape, BF) for one in behind]
        self.keeps = []

    def peers(self, at):
        return []

    def start(self, net, ins, outs, at):
        for part, (plus, minus) in enumerate((x_next(at), z_next(at))):
            net.send(ins[part].at[0], outs[part].at[0], plus)
            net.send(ins[2 + part].at[1], outs[part].at[1], minus)

    def forward(self, net, outs, at):
        pass


class Hand:
    def __init__(self, piece, columns, split):
        self.columns, self.cell, self.split = columns, columns // 4, split
        self.inputs = (piece,)
        self.outs = [((2, 2, STRIP, columns), BF)] * 2 if split else [((2, 2, SHARD, columns), BF)]
        self.keeps = [((2, STRIP, columns // 4), BF)] * 2

    def peers(self, at):
        x, z, y_lo, y_hi, core = at
        return [device(x, z, 1 - y_lo, y_hi, core)] + x_next(at) + z_next(at)

    def strip(self, outs, at, part, high, low, j):
        cut = pl.ds(pl.multiple_of(j * self.cell, 128), self.cell)
        if self.split:
            return outs[part].at[high, low, :, cut]
        start = pl.multiple_of(part * PART + at[part] * STRIP, 16)
        return outs[0].at[high, low, pl.ds(start, STRIP), cut]

    def start(self, net, ins, outs, at):
        (mine,) = ins
        self.near = []
        for part in (0, 1):
            spot = self.strip(outs, at, part, slice(None), at[2], at[1 - part])
            self.near.append(net.send(mine.at[:, part], spot, self.peers(at)[0]))
            net.keep(mine.at[:, part], spot)

    def forward(self, net, outs, at):
        sides = (x_next(at), z_next(at))
        rings = []
        for part in (0, 1):
            net.arrived(self.near[part])

            def halves(origin, half, part=part):
                return [self.strip(outs, at, part, half, slice(None), origin)]

            rings.append(Ring(net, halves, at[1 - part], sides[1 - part]).start())
        for ring in rings:
            ring.forward()
        if self.split:
            return
        far_rings = []
        for part in (0, 1):
            rings[part].finish()

            def halves(origin, half, part=part):
                start = pl.multiple_of(part * PART + origin * STRIP, 16)
                return [outs[0].at[half, :, pl.ds(start, STRIP), :]]

            far_rings.append(Ring(net, halves, at[part], sides[part]).start())
        for ring in far_rings:
            ring.forward()


def sum_step(sums, number, name, extras=()):
    count = len(sums)
    steps = [step for _, _, step in sums]
    ringed = [one.pairs[step] != [] for one, _, step in sums]
    keeps = [keep for (one, _, step), late in zip(sums, ringed) if not late for keep in one.keeps[step]]
    keeps += [keep for (one, _, step), late in zip(sums, ringed) if late for keep in one.keeps[step]]
    keeps += [keep for extra in extras for keep in extra.keeps]

    def body(net, ins, outs):
        at = place()
        x, z, y_lo, y_hi, core = at
        peers = []
        if any(step < 2 for step in steps):
            peers += x_peers(at) + z_peers(at)
        column = any(step == 2 and isinstance(one, GradSum) for one, _, step in sums)
        if column:
            for k in range(1, 8):
                peers.append(device(x, z, (y_lo + k // 4) % 2, (y_hi + (k // 2) % 2) % 2, (core + k) % 2))
        elif any(step == 2 for step in steps) and not extras:
            peers.append(device(x, z, 1 - y_lo, y_hi, core))
        for extra in extras:
            peers += extra.peers(at)
        net.greet(peers)
        at_in = at_out = count
        spans = []
        for extra in extras:
            spans.append((at_in, at_in + len(extra.inputs), at_out, at_out + len(extra.outs)))
            at_in, at_out = spans[-1][1], spans[-1][3]
        rings, at_pair = [], len(keeps)
        for (one, _, step), whole, got in zip(sums, ins, outs):
            pairs = net.stage[at_pair : at_pair + len(one.pairs[step])]
            at_pair += len(pairs)
            rings += (one.first, one.second, one.third)[step](net, whole, got, at, pairs) or []
        for ring in rings:
            ring.start()
        for extra, (a, b, c, d) in zip(extras, spans):
            extra.start(net, ins[a:b], outs[c:d], at)
        stores = net.settle()
        for ring in rings:
            ring.forward()
        net.done(stores)
        for extra, (a, b, c, d) in zip(extras, spans):
            extra.forward(net, outs[c:d], at)

    came = exchange(
        body,
        tuple(array for _, array, _ in sums) + tuple(one for extra in extras for one in extra.inputs),
        [one.shapes[step] for one, _, step in sums] + [out for extra in extras for out in extra.outs],
        12 * count + 30 * len(extras),
        keeps,
        number,
        name,
        [pair for one, _, step in sums for pair in one.pairs[step]],
    )
    total = []
    for (one, _, step), got in zip(sums, came):
        if isinstance(one, LossSum):
            total.append(jnp.sum(got, axis=0))
        else:
            total.append(add_up(got, 1 if step < 2 else 0))
    return total + list(came[count:])


SPANS = 16
BLOCK = SPANS * SPAN
QUERIES = GROUPS * SPAN
SMEM = pl.BlockSpec(memory_space=pltpu.SMEM)
VMEM = pl.BlockSpec(memory_space=pltpu.VMEM)
LOW = 32
FIRST = 2


def local_call(kernel, args, outs, name, flops, specs=None, out_specs=None, grid=None, scratch=(), limit=60):
    moved = sum(math.prod(arg.shape) * arg.dtype.itemsize for arg in args)
    moved += sum(math.prod(shape) * jnp.dtype(kind).itemsize for shape, kind in outs)
    extra = {} if grid is None else {"grid": grid}
    return pl.pallas_call(
        kernel,
        out_shape=[jax.ShapeDtypeStruct(shape, kind) for shape, kind in outs],
        in_specs=specs or [VMEM] * len(args),
        out_specs=out_specs or [VMEM] * len(outs),
        scratch_shapes=[pltpu.SMEM((64,), jnp.int32) if one is None else pltpu.VMEM(*one) for one in scratch],
        compiler_params=pltpu.CompilerParams(vmem_limit_bytes=limit << 20),
        cost_estimate=pl.CostEstimate(flops=flops // 1000, transcendentals=0, bytes_accessed=moved // 1000),
        name=name,
        **extra,
    )(*args)


def inverse_root(values):
    return lax.rsqrt(jnp.mean(values * values, axis=-1, keepdims=True) + EPS)


def norm_back(values, gain, grad):
    inv = inverse_root(values)
    scaled = gain * grad
    return inv * (scaled - values * (inv * inv) * jnp.mean(scaled * values, axis=-1, keepdims=True))


def turn(values, cosine, sine):
    return values * cosine + pltpu.roll(values, HD // 2, 1) * sine


def head(index):
    return slice(index * HD, (index + 1) * HD)


def stack_heads(ref, span, kv):
    rows = slice(span * SPAN, (span + 1) * SPAN)
    return jnp.concatenate([ref[rows, head(kv * GROUPS + g)] for g in range(GROUPS)], axis=0)


def unstack_heads(ref, span, kv, values):
    rows = slice(span * SPAN, (span + 1) * SPAN)
    for g in range(GROUPS):
        ref[rows, head(kv * GROUPS + g)] = values[g * SPAN : (g + 1) * SPAN, :]


def expert_lanes():
    return lax.broadcasted_iota(jnp.int32, (1, HD), 1)


def wide_router(small_ref):
    rows = small_ref[...]
    number = lax.broadcasted_iota(jnp.int32, rows.shape, 0)
    rows = jnp.where((number >= FIRST) & (number < FIRST + E), rows.astype(F32), 0.0).astype(BF)
    gap = jnp.zeros((16, D), BF)
    return jnp.concatenate([rows, gap, rows, gap, gap, gap, gap, gap], axis=0)


def chosen(routes):
    lanes = expert_lanes()
    number = jnp.where(lanes >= LOW, lanes - LOW, lanes) - FIRST
    total = jnp.zeros((ROWS, HD), F32)
    for slot in range(4):
        total = total + jnp.where(routes[:, slot : slot + 1] == number, 1.0, 0.0)
    return total


def in_two(values):
    high = values.astype(BF).astype(F32)
    return jnp.where(expert_lanes() < LOW, high, values - high).astype(BF)


def small_kernel(norm_gain, moe_gain, w_router, out):
    out[...] = jnp.concatenate(
        [
            norm_gain[...].astype(F32),
            moe_gain[...].astype(F32),
            w_router[...].astype(F32).T,
            jnp.zeros((16 - 2 - E, SHARD), F32),
        ],
        axis=0,
    ).astype(BF)


def small_rows(*args):
    return local_call(small_kernel, args, [((16, SHARD), BF)], "small_rows", 1000)[0]


def project_kernel(
    place_ref, order, tokens, small, w_query, w_key, w_value, normed, query, keys_values, cosine, sine
):
    lanes = lax.broadcasted_iota(jnp.int32, (SPAN, HD), 1)
    offsets = lax.broadcasted_iota(jnp.int32, (SPAN, HD), 0)
    half_size = HD // 2
    steps = jnp.where(lanes >= half_size, lanes - half_size, lanes).astype(F32)
    frequency = jnp.exp(-(steps * 2.0 / HD) * math.log(BASE))
    for s in range(2):
        rows = slice(s * SPAN, (s + 1) * SPAN)
        angles = (order[2 * place_ref[3] + s] * SPAN + offsets).astype(F32) * frequency
        cosine[rows, :] = jnp.cos(angles)
        turned = jnp.sin(angles)
        sine[rows, :] = jnp.where(lanes >= half_size, turned, -turned)
    inputs = tokens[...].astype(F32)
    gain = small[...].astype(F32)[0:1, :]
    normed[...] = (inputs * inverse_root(inputs) * gain).astype(BF)
    rows = normed[...]
    cos, sin = cosine[...], sine[...]
    raw = jnp.dot(rows, w_key[...], preferred_element_type=F32)
    for k in range(KV):
        keys_values[:, head(k)] = turn(raw[:, head(k)], cos, sin).astype(BF)
    keys_values[:, KV * HD :] = jnp.dot(rows, w_value[...], preferred_element_type=F32).astype(BF)
    for k in range(0, H, 4):
        raw = jnp.dot(rows, w_query[:, k * HD : (k + 4) * HD], preferred_element_type=F32)
        for j in range(4):
            query[:, head(k + j)] = turn(raw[:, head(j)], cos, sin).astype(BF)


def project(*args):
    outs = [((ROWS, D), BF), ((ROWS, H * HD), BF), ((ROWS, 2 * KV * HD), BF), ((ROWS, HD), F32), ((ROWS, HD), F32)]
    return local_call(project_kernel, args, outs, "project", 800_000_000, specs=[SMEM] * 2 + [VMEM] * 5)


def combine_kernel(mixed, hidden, teacher, valid, count, result, d_result, d_low, squared):
    total = hidden[...] + (mixed[0].astype(F32) + mixed[1].astype(F32) + mixed[2].astype(F32))
    result[...] = total.astype(BF)
    error = total - teacher[...].astype(F32)
    valid_rows = valid[...].astype(F32).T
    squared[...] = jnp.full((8, 128), jnp.sum(valid_rows * error * error), F32)
    norm_factor = jnp.full((1, 1), count[0], jnp.int32).astype(F32) * D
    grad = 2.0 * valid_rows * error / norm_factor
    d_result[...] = grad
    d_low[...] = grad.astype(BF)


def combine(*args):
    outs = [((ROWS, D), BF), ((ROWS, D), F32), ((ROWS, D), BF), ((8, 128), F32)]
    return local_call(combine_kernel, args, outs, "combine", 1000, specs=[VMEM] * 4 + [SMEM])


def tail_kernel(normed, d_qkv, attended, d_attn, normed_two, d_router, out):
    for shard in range(4):
        columns = slice(shard * SHARD, (shard + 1) * SHARD)
        out[shard, :, :512] = tn(normed[:, columns], d_qkv[...]).astype(BF)
        out[shard, :, 512 : 512 + SHARD] = tn(attended[:, columns], d_attn[...]).astype(BF)
        out[shard, :, 512 + SHARD :] = tn(normed_two[:, columns], d_router[...]).astype(BF)


def tail_grads(*args):
    return local_call(tail_kernel, args, [((4, SHARD, TAIL), BF)], "tail_grads", 1000)[0]


def nt(a, b):
    return lax.dot_general(a, b, (((1,), (1,)), ((), ())), preferred_element_type=F32)


def tn(a, b):
    return lax.dot_general(a, b, (((0,), (0,)), ((), ())), preferred_element_type=F32)


def block_rows(where, b, ref):
    return jnp.concatenate(
        [ref[pl.ds(pl.multiple_of(where[b * SPANS + i] * SPAN, SPAN), SPAN), :] for i in range(SPANS)], axis=0
    )


def lead_of_keys():
    keys = lax.broadcasted_iota(jnp.int32, (BLOCK, QUERIES), 0)
    queries = lax.broadcasted_iota(jnp.int32, (BLOCK, QUERIES), 1)
    return keys - queries % SPAN


def find_spans(order, where):
    def put(slot, carry):
        where[order[slot]] = slot
        return carry

    lax.fori_loop(0, order.shape[0], put, 0)


def attend_kernel(
    place_ref, order, q_ref, kv_ref, tokens, w_out, small, routes, o_ref, low_ref, lse_ref, hidden_ref, normed_ref, gates_ref, probs_ref, where
):
    find_spans(order, where)
    lead = lead_of_keys()
    for s in range(2):
        span = order[2 * place_ref[3] + s]
        stacked = [stack_heads(q_ref, s, kv) for kv in range(KV)]

        def body(b, carry, last=False):
            keys_values = block_rows(where, b, kv_ref)
            out = []
            for kv in range(KV):
                top, total, acc = carry[kv]
                keys = keys_values[:, head(kv)]
                values = keys_values[:, head(KV + kv)]
                logits = nt(keys, stacked[kv])
                if last:
                    logits = jnp.where(lead <= span * SPAN - b * BLOCK, logits, NEGATIVE)
                new_top = jnp.maximum(top, jnp.max(logits, axis=0, keepdims=True))
                weights = jnp.exp2((logits - new_top) * SCALE_2)
                shrink = jnp.exp2((top - new_top) * SCALE_2)
                total = total * shrink + jnp.sum(weights, axis=0, keepdims=True)
                acc = acc * shrink + tn(values, weights.astype(BF))
                out.append((new_top, total, acc))
            return tuple(out)

        start = tuple(
            (
                jnp.full((1, QUERIES), NEGATIVE, F32),
                jnp.zeros((1, QUERIES), F32),
                jnp.zeros((HD, QUERIES), F32),
            )
            for _ in range(KV)
        )
        final = body(span // SPANS, lax.fori_loop(0, span // SPANS, body, start), last=True)
        for kv in range(KV):
            top, total, acc = final[kv]
            unstack_heads(o_ref, s, kv, (acc / total).T)
            lse_ref[2 * s + kv : 2 * s + kv + 1, :] = top * SCALE_2 + jnp.log(total) * LOG2_E
    lse_ref[4:8, :] = jnp.zeros((4, QUERIES), F32)

    low_ref[...] = o_ref[...].astype(BF)
    for start in range(0, D, 512):
        columns = slice(start, start + 512)
        hidden_ref[:, columns] = tokens[:, columns].astype(F32) + jnp.dot(
            low_ref[...], w_out[:, columns], preferred_element_type=F32
        )
    hidden = hidden_ref[...]
    gain = small[...].astype(F32)[1:2, :]
    normed = (hidden * inverse_root(hidden) * gain).astype(BF)
    normed_ref[...] = normed
    logits = nt(normed, wide_router(small))
    lanes = expert_lanes()
    first = (lanes >= FIRST) & (lanes < FIRST + E)
    second = (lanes >= FIRST + LOW) & (lanes < FIRST + LOW + E)
    top = jnp.max(jnp.where(first, logits, NEGATIVE), axis=1, keepdims=True)
    weights = jnp.where(first | second, jnp.exp(logits - top), 0.0)
    probs = weights / jnp.sum(jnp.where(first, weights, 0.0), axis=1, keepdims=True)
    probs_ref[...] = probs
    gates_ref[...] = in_two(probs * chosen(routes))


def attend(*args):
    outs = [
        ((ROWS, H * HD), F32),
        ((ROWS, H * HD), BF),
        ((8, QUERIES), F32),
        ((ROWS, D), F32),
        ((ROWS, D), BF),
        ((ROWS, HD), BF),
        ((ROWS, HD), F32),
    ]
    return local_call(attend_kernel, args, outs, "attend", 2_400_000_000, specs=[SMEM, SMEM] + [VMEM] * 6, scratch=[None])


GELU = math.sqrt(2.0 / math.pi)


def gate_column(gates, place_ref, h):
    lane = FIRST + (place_ref[0] * 3 + h) // 2
    lanes = expert_lanes()
    here = (lanes == lane) | (lanes == lane + LOW)
    return jnp.sum(jnp.where(here, gates, 0.0), axis=1, keepdims=True)


def experts_kernel(place_ref, rows, gates, w_both, w_down, mixed, made_ref, active_ref, steep_ref, total):
    h = pl.program_id(0)
    raw = jnp.dot(rows[...], w_both[...], preferred_element_type=F32)
    gate, up = raw[:, :HALF], raw[:, HALF:]
    squared = gate * gate
    inner = jnp.tanh(GELU * gate * (1.0 + 0.044715 * squared))
    active = 0.5 * gate * (1.0 + inner)
    slope = 0.5 * (1.0 + inner) + 0.5 * gate * (1.0 - inner * inner) * (GELU + 3 * 0.044715 * GELU * squared)
    made = active * up
    made_ref[...] = made.astype(BF)
    active_ref[...] = active.astype(BF)
    steep_ref[...] = (slope * up).astype(BF)
    weighted = (gate_column(gates[...].astype(F32), place_ref, h) * made).astype(BF)
    out = jnp.dot(weighted, w_down[...], preferred_element_type=F32)

    @pl.when(h == 0)
    def _():
        total[...] = out

    @pl.when(h == 1)
    def _():
        total[...] += out

    @pl.when(h == 2)
    def _():
        mixed[...] = (total[...] + out).astype(BF)


def whole(shape):
    return pl.BlockSpec(shape, lambda h: (0,) * len(shape))


def experts(place_here, rows, gates, wide, low):
    count = 4 * ROWS
    return local_call(
        experts_kernel,
        (place_here, rows, gates, wide, low),
        [((count, D), BF)] + [((count, SLICE), BF)] * 3,
        "experts",
        5_400_000_000,
        specs=[
            SMEM,
            whole((count, D)),
            whole((count, HD)),
            pl.BlockSpec((D, 2 * HALF), lambda h: (0, h)),
            pl.BlockSpec((HALF, D), lambda h: (h, 0)),
        ],
        out_specs=[whole((count, D))] + [pl.BlockSpec((count, HALF), lambda h: (0, h))] * 3,
        grid=(3,),
        scratch=[((count, D), F32)],
    )


def experts_back_kernel(
    place_ref, rows, d_rows, gates, made_ref, active_ref, steep_ref, w_both, w_down, d_normed, gates_sent, *rest
):
    chunks, (total, strip, rows_t, d_rows_t, d_gates) = rest[:10], rest[10:]
    h = pl.program_id(0)

    @pl.when(h == 0)
    def _():
        rows_t[...] = rows[...].T
        d_rows_t[...] = d_rows[...].T

    back = nt(d_rows[...], w_down[...])
    made = made_ref[...].astype(F32)
    weight = gate_column(gates[...].astype(F32), place_ref, h)
    lane = FIRST + (place_ref[0] * 3 + h) // 2
    lanes = expert_lanes()
    here = (lanes == lane) | (lanes == lane + LOW)
    d_weight = jnp.where(here, jnp.sum(made * back, axis=1, keepdims=True), 0.0)
    d_made = weight * back
    d_gate = (d_made * steep_ref[...].astype(F32)).astype(BF)
    d_up = (d_made * active_ref[...].astype(F32)).astype(BF)
    weighted = (weight * made).astype(BF)
    d_raw = jnp.concatenate([d_gate, d_up], axis=1)
    out = nt(d_raw, w_both[...])

    @pl.when(h == 0)
    def _():
        total[...] = out
        d_gates[...] = d_weight

    @pl.when(h != 0)
    def _():
        d_gates[...] += d_weight

    @pl.when(h == 1)
    def _():
        total[...] += out

    @pl.when(h == 2)
    def _():
        d_normed[...] = (total[...] + out).astype(BF)
        gates_sent[...] = in_two(d_gates[...])

    for shard in range(4):
        columns = slice(shard * SHARD, (shard + 1) * SHARD)
        strip[:, : 2 * HALF] = jnp.dot(rows_t[columns, :], d_raw, preferred_element_type=F32).astype(BF)
        strip[:, 2 * HALF :] = jnp.dot(d_rows_t[columns, :], weighted, preferred_element_type=F32).astype(BF)
        for part in (0, 1):
            for n, k in enumerate((0, 1, 3, 2)):
                start = part * PART + ((place_ref[1 + part] + k) % 4) * STRIP
                chunk = chunks[part * 5 + n + (shard // 2 if k == 2 else 0)]
                chunk[shard % 2 if k == 2 else shard] = strip[pl.ds(pl.multiple_of(start, 16), STRIP), :]


def experts_back(place_here, rows, d_rows, gates, made, active, steep, wide, low):
    count = 4 * ROWS
    column = pl.BlockSpec((count, HALF), lambda h: (0, h))
    return local_call(
        experts_back_kernel,
        (place_here, rows, d_rows, gates, made, active, steep, wide, low),
        [((count, D), BF), ((count, HD), BF)] + ([((4, STRIP, 3 * SLICE), BF)] * 3 + [((2, STRIP, 3 * SLICE), BF)] * 2) * 2,
        "experts_back",
        10_800_000_000,
        specs=[
            SMEM,
            whole((count, D)),
            whole((count, D)),
            whole((count, HD)),
            column,
            column,
            column,
            pl.BlockSpec((D, 2 * HALF), lambda h: (0, h)),
            pl.BlockSpec((HALF, D), lambda h: (h, 0)),
        ],
        out_specs=[whole((count, D)), whole((count, HD))]
        + (
            [pl.BlockSpec((4, STRIP, 3 * HALF), lambda h: (0, 0, h))] * 3
            + [pl.BlockSpec((2, STRIP, 3 * HALF), lambda h: (0, 0, h))] * 2
        )
        * 2,
        grid=(3,),
        scratch=[((count, D), F32), ((SHARD, SLICE), BF), ((D, count), BF), ((D, count), BF), ((count, HD), F32)],
    )


def attend_back_kernel(
    place_ref,
    order,
    q_ref,
    kv_ref,
    o_ref,
    lse_ref,
    cosine,
    sine,
    w_out,
    small,
    routes,
    probs_ref,
    hidden_ref,
    d_result,
    two_parts,
    gate_parts,
    d_hidden_ref,
    d_attn_ref,
    d_router_ref,
    dq_ref,
    dkv_ref,
    acc_ref,
    do_ref,
    turned_ref,
    where,
):
    find_spans(order, where)
    d_gates = gate_parts[0].astype(F32) + gate_parts[1].astype(F32) + gate_parts[2].astype(F32)
    lanes = expert_lanes()
    first = (lanes >= FIRST) & (lanes < FIRST + E)
    d_select = jnp.where(first, (d_gates + pltpu.roll(d_gates, HD - LOW, 1)) * chosen(routes), 0.0)
    probs = jnp.where(first, probs_ref[...], 0.0)
    d_router = (probs * (d_select - jnp.sum(probs * d_select, axis=1, keepdims=True))).astype(BF)
    d_router_ref[...] = d_router
    d_normed = two_parts[0].astype(F32) + two_parts[1].astype(F32) + two_parts[2].astype(F32)
    d_normed = d_normed + jnp.dot(d_router, wide_router(small), preferred_element_type=F32)
    gain = small[...].astype(F32)[1:2, :]
    d_hidden = d_result[...] + norm_back(hidden_ref[...], gain, d_normed)
    d_hidden_ref[...] = d_hidden
    d_attn = d_hidden.astype(BF)
    for f in range(4):
        d_attn_ref[f] = d_attn[:, f * SHARD : (f + 1) * SHARD]
    for start in range(0, H * HD, 512):
        columns = slice(start, start + 512)
        do_ref[:, columns] = nt(d_attn, w_out[columns, :]).astype(BF)

    lead = lead_of_keys()
    acc_ref[...] = jnp.zeros_like(acc_ref)
    for s in range(2):
        span = order[2 * place_ref[3] + s]
        stacked = [stack_heads(q_ref, s, kv) for kv in range(KV)]
        d_out = [stack_heads(do_ref, s, kv) for kv in range(KV)]
        delta = [
            jnp.sum((d_out[kv].astype(F32) * stack_heads(o_ref, s, kv)).T, axis=0, keepdims=True) for kv in range(KV)
        ]
        lse = [lse_ref[2 * s + kv : 2 * s + kv + 1, :] for kv in range(KV)]

        def body(b, carry, last=False):
            keys_values = block_rows(where, b, kv_ref)
            out, key_grads, value_grads = [], [], []
            for kv in range(KV):
                keys = keys_values[:, head(kv)]
                values = keys_values[:, head(KV + kv)]
                weights = jnp.exp2(nt(keys, stacked[kv]) * SCALE_2 - lse[kv])
                if last:
                    weights = jnp.where(lead <= span * SPAN - b * BLOCK, weights, 0.0)
                d_weights = nt(values, d_out[kv])
                d_logits = (weights * (d_weights - delta[kv])).astype(BF)
                out.append(carry[kv] + tn(keys, d_logits))
                key_grads.append(jnp.dot(d_logits, stacked[kv], preferred_element_type=F32) * SCALE)
                value_grads.append(jnp.dot(weights.astype(BF), d_out[kv], preferred_element_type=F32))
            grads = jnp.concatenate(key_grads + value_grads, axis=1)
            for i in range(SPANS):
                rows = pl.ds(pl.multiple_of(where[b * SPANS + i] * SPAN, SPAN), SPAN)
                acc_ref[rows, :] += grads[i * SPAN : (i + 1) * SPAN, :]
            return tuple(out)

        start = tuple(jnp.zeros((HD, QUERIES), F32) for _ in range(KV))
        final = body(span // SPANS, lax.fori_loop(0, span // SPANS, body, start), last=True)
        for kv in range(KV):
            unstack_heads(turned_ref, s, kv, (final[kv] * SCALE).T)
    for k in range(H):
        dq_ref[:, head(k)] = turn(turned_ref[:, head(k)], cosine[...], -sine[...]).astype(BF)

    def put(i, carry):
        rows = pl.ds(pl.multiple_of(i * 256, 256), 256)
        dkv_ref[rows, :] = acc_ref[rows, :].astype(BF)
        return carry

    lax.fori_loop(0, acc_ref.shape[0] // 256, put, 0)


def attend_back(*args):
    length = args[3].shape[0]
    outs = [
        ((ROWS, D), F32),
        ((4, ROWS, SHARD), BF),
        ((ROWS, HD), BF),
        ((ROWS, H * HD), BF),
        ((length, 2 * KV * HD), BF),
    ]
    return local_call(
        attend_back_kernel,
        args,
        outs,
        "attend_back",
        5_000_000_000,
        specs=[SMEM, SMEM] + [VMEM] * 14,
        scratch=[((length, 2 * KV * HD), F32), ((ROWS, H * HD), BF), ((ROWS, H * HD), F32), None],
    )


def blocks_kernel(dq_ref, keys, cosine, sine, blocks):
    for f in range(3):
        blocks[f] = dq_ref[:, f * 512 : (f + 1) * 512]
    for k in range(KV):
        turned = turn(keys[0, :, head(k)].astype(F32), cosine[...], -sine[...])
        blocks[3, :, head(k)] = turned.astype(BF)
    blocks[3, :, KV * HD :] = keys[1]


def query_blocks(*args):
    return local_call(blocks_kernel, args, [((4, ROWS, 512), BF)], "query_blocks", 1_000_000)[0]


def inputs_kernel(blocks, w_query, w_key, w_value, tokens, small, d_hidden, out):
    gain = small[...].astype(F32)[0:1, :]
    d_normed = nt(blocks[3, :, : KV * HD], w_key[...]) + nt(blocks[3, :, KV * HD :], w_value[...])
    for f in range(3):
        d_normed = d_normed + nt(blocks[f], w_query[:, f * 512 : (f + 1) * 512])
    out[...] = d_hidden[...] + norm_back(tokens[...].astype(F32), gain, d_normed)


def input_grads(*args):
    return local_call(inputs_kernel, args, [((ROWS, D), F32)], "input_grads", 800_000_000)[0]


def lay_out_kernel(place_ref, *refs):
    w_gate, w_up, w_router, router, gain, gate_out, up_out, down_out, gain_out, turned, sum_ref = refs[16:]
    part_sum = jnp.zeros((SHARD, HD), F32)
    for side in (0, 1):
        columns = slice(side * HALF, (side + 1) * HALF)
        for part in (0, 1):
            for n, k in enumerate((0, 1, 3, 2)):
                start = part * PART + ((place_ref[1 + part] + 4 - k) % 4) * STRIP
                rows = pl.ds(pl.multiple_of(start, 16), STRIP)
                piece = refs[side * 8 + part * 4 + n]
                gate_out[0, rows, columns] = piece[0, :, :HALF].astype(F32)
                up_out[0, rows, columns] = piece[0, :, HALF : 2 * HALF].astype(F32)
                turned[rows, :] = piece[0, :, 2 * HALF :].astype(F32)
        down_out[0, columns, :] = turned[...].T
        both = w_gate[0, :, columns].astype(F32) * gate_out[0, :, columns]
        both = both + w_up[0, :, columns].astype(F32) * up_out[0, :, columns]
        part_sum = part_sum + (both[:, :HD] + both[:, HD : 2 * HD] + both[:, 2 * HD :])

    @pl.when(pl.program_id(0) == 0)
    def _():
        sum_ref[...] = part_sum

    @pl.when(pl.program_id(0) != 0)
    def _():
        sum_ref[...] += part_sum

    @pl.when(pl.program_id(0) == E - 1)
    def _():
        total = jnp.sum(sum_ref[...], axis=1, keepdims=True)
        total = total + jnp.sum(w_router[...].astype(F32) * router[...], axis=1, keepdims=True)
        gain_out[...] = total.T / gain[...].astype(F32)


def lay_out_experts(place_here, pieces, w_gate, w_up, w_router, router, gain):
    def strips(side):
        return [pl.BlockSpec((1, STRIP, SLICE), lambda e: ((2 * e + side) // 3, 0, (2 * e + side) % 3))] * 8

    wide = pl.BlockSpec((1, SHARD, FF), lambda e: (e, 0, 0))
    return local_call(
        lay_out_kernel,
        (place_here,) + tuple(pieces) * 2 + (w_gate, w_up, w_router, router, gain),
        [((E, SHARD, FF), F32), ((E, SHARD, FF), F32), ((E, FF, SHARD), F32), ((1, SHARD), F32)],
        "lay_out_experts",
        20_000_000,
        specs=[SMEM] + strips(0) + strips(1) + [wide, wide, whole((SHARD, E)), whole((SHARD, E)), whole((1, SHARD))],
        out_specs=[wide, wide, pl.BlockSpec((1, FF, SHARD), lambda e: (e, 0, 0)), whole((1, SHARD))],
        grid=(E,),
        scratch=[((SHARD, HALF), F32), ((SHARD, HD), F32)],
    )


def attention_kernel(tail, w_query, w_key, w_value, gain, query, key, value, out, router, gain_out):
    total = jnp.zeros((SHARD, 1), F32)
    for f in range(3):
        columns = slice(f * 512, (f + 1) * 512)
        piece = tail[f, :, :512].astype(F32)
        query[:, columns] = piece
        total = total + jnp.sum(w_query[:, columns].astype(F32) * piece, axis=1, keepdims=True)
    for ref, weight, columns in ((key, w_key, slice(0, 256)), (value, w_value, slice(256, 512))):
        piece = tail[3, :, columns].astype(F32)
        ref[...] = piece
        total = total + jnp.sum(weight[...].astype(F32) * piece, axis=1, keepdims=True)
    gain_out[...] = total.T / gain[...].astype(F32)
    for f in range(4):
        out[:, f * SHARD : (f + 1) * SHARD] = tail[f, :, 512 : 512 + SHARD].astype(F32)
    pieces = [tail[f, :, 512 + SHARD :].astype(F32) for f in range(4)]
    router[...] = (pieces[0] + pieces[1] + pieces[2] + pieces[3])[:, FIRST : FIRST + E]


def lay_out_attention(*args):
    outs = [((SHARD, width), F32) for width in (D, KV * HD, KV * HD, D, E)] + [((1, SHARD), F32)]
    return local_call(attention_kernel, args, outs, "lay_out_attention", 4_000_000)


def add_halves_kernel(*refs):
    for n in range(4):
        refs[8 + n][...] = (refs[n][...].astype(F32) + refs[4 + n][...].astype(F32)).astype(BF)


def add_halves(blocks, halves):
    cell = SLICE
    specs = [pl.BlockSpec((2, STRIP, cell), lambda n, side=side: (side, 0, n)) for side in (0, 1, 0, 1)]
    half_spec = pl.BlockSpec((2, STRIP, cell), lambda n: (0, 0, n))
    return pl.pallas_call(
        add_halves_kernel,
        out_shape=[jax.ShapeDtypeStruct(block.shape, BF) for block in blocks],
        grid=(3,),
        in_specs=specs + [half_spec] * 4,
        out_specs=specs,
        input_output_aliases={n: n for n in range(4)},
        compiler_params=pltpu.CompilerParams(vmem_limit_bytes=32 << 20),
        cost_estimate=pl.CostEstimate(flops=1000, transcendentals=0, bytes_accessed=1000),
        name="add_halves",
    )(*blocks, *halves)


def shift_pairs(axis, k):
    pairs = []
    for ctx in range(32):
        x, z, y_lo = ctx // 8, (ctx // 2) % 4, ctx % 2
        if axis == 0:
            pairs.append((ctx, (x + k) % 4 * 8 + z * 2 + y_lo))
        else:
            pairs.append((ctx, x * 8 + (z + k) % 4 * 2 + y_lo))
    return pairs


def shift(array, axis, k):
    return lax.ppermute(array, "ctx", shift_pairs(axis, k))


def local(
    tokens,
    teacher,
    valid_mask,
    token_count,
    routes,
    span_order,
    w_query,
    w_key,
    w_value,
    w_out,
    norm_gain,
    w_router,
    moe_gain,
    w_gate,
    w_up,
    w_down,
):
    rows = tokens[0]
    ctx = lax.axis_index("ctx")
    shard = lax.axis_index("fsdp")
    x, z, _, _, _ = place()
    place_here = jnp.stack([shard, x, z, ctx])

    small = small_rows(norm_gain[None], moe_gain[None], w_router)
    full_query, full_key, full_value, full_out, small = gather_attention_weights(
        (w_query, w_key, w_value, w_out), small, 1
    )
    input_one, query, keys_values, cosine, sine = project(place_here, span_order, rows, small, full_query, full_key, full_value)
    keys, quarters = gather_keys(keys_values, (w_gate, w_up, w_down), 2)
    keys = keys.reshape(32 * ROWS, 2 * KV * HD)
    attended, attended_low, lse, hidden, input_two, gates_sent, probs = attend(
        place_here, span_order, query, keys, rows, full_out, small, routes[0]
    )

    group_two, gates, wide, low = group_spread(
        (input_two, gates_sent), 3, "group_normed", (w_gate, w_up, w_down, quarters)
    )
    group_two, gates = group_two.reshape(4 * ROWS, D), gates.reshape(4 * ROWS, HD)
    mixed, *kept = experts(place_here, group_two, gates, wide, low)
    (mixed,) = group_sum((mixed.reshape(4, ROWS, D),), 4, "group_mixture")
    result, d_result, d_low, squared = combine(mixed, hidden, teacher[0], valid_mask, token_count)
    (group_d,) = group_spread((d_low,), 5, "group_d_result")
    d_two, d_gates_sent, *chunks = experts_back(
        place_here, group_two, group_d.reshape(4 * ROWS, D), gates, *kept, wide, low
    )
    halfway = [shift(chunks[part * 5 + 3 + n], part, (1, 3)[n]) for n in (0, 1) for part in (0, 1)]
    two_parts, gate_parts, squared = group_sum(
        (d_two.reshape(4, ROWS, D), d_gates_sent.reshape(4, ROWS, HD)), 6, "group_d_normed", squared
    )
    squared = jnp.sum(squared, axis=0)
    halfway, two_parts = lax.optimization_barrier((halfway, two_parts))
    sums = add_halves(
        (chunks[1], chunks[2], chunks[6], chunks[7]), (halfway[0], halfway[2], halfway[1], halfway[3])
    )
    came = [[chunks[part * 5], shift(sums[part * 2], part, 1), shift(sums[part * 2 + 1], part, 3)] for part in (0, 1)]
    d_hidden, d_attn_blocks, d_router, d_query, d_keys = attend_back(
        place_here,
        span_order,
        query,
        keys,
        attended,
        lse,
        cosine,
        sine,
        full_out,
        small,
        routes[0],
        probs,
        hidden,
        d_result,
        two_parts,
        gate_parts,
    )

    expert_sum, tail_sum, key_sum, loss_sum = GradSum(WIDE, 1), GradSum(TAIL, 0), KeySum(), LossSum()
    came, d_keys = lax.optimization_barrier((came, d_keys))
    part = add_strips(came[0] + came[1])
    share = GroupShare((attended_low, input_one), (d_attn_blocks,))
    part, d_keys, squared, group_attended, group_one, group_d_attn = sum_step(
        (
            (expert_sum, part, 1),
            (key_sum, d_keys.reshape(4, 4, 2, ROWS, 2 * KV * HD), 0),
            (loss_sum, squared, 0),
        ),
        7,
        "sums_first",
        (share,),
    )
    d_keys, squared, part = sum_step(
        ((key_sum, d_keys, 1), (loss_sum, squared, 1), (expert_sum, part, 2)), 8, "sums_second"
    )
    d_keys, squared, *strips = sum_step(
        ((key_sum, d_keys, 2), (loss_sum, squared, 2)), 9, "sums_third", (Hand(part, WIDE, True),)
    )
    pieces = [[strips[part], shift(strips[part], part, 1), shift(strips[part], part, 3)] for part in (0, 1)]
    norm_factor = token_count[0].astype(F32) * D
    loss_value = (squared[0, 0] / norm_factor).reshape(1)

    blocks = query_blocks(d_query, d_keys, cosine, sine)
    (group_d_qkv,) = sum_step((), 10, "group_d_qkv", (GroupShare((), (blocks,)),))
    tail = tail_grads(
        group_one.reshape(4 * ROWS, D),
        group_d_qkv.reshape(4 * ROWS, 512),
        group_attended.reshape(4 * ROWS, D),
        group_d_attn.reshape(4 * ROWS, SHARD),
        input_two,
        d_router,
    )
    d_inputs = input_grads(blocks, full_query, full_key, full_value, rows, small, d_hidden)
    pieces, tail, d_inputs = lax.optimization_barrier((pieces, tail, d_inputs))
    tail, *halves = sum_step(
        ((tail_sum, tail, 0),), 11, "tail_a", (Forward([pieces[0][1], pieces[1][1]], [pieces[0][2], pieces[1][2]]),)
    )
    for part in (0, 1):
        pieces[part].append(halves[part])
    (tail,) = sum_step(((tail_sum, tail, 1),), 12, "tail_b")
    (tail,) = sum_step(((tail_sum, tail, 2),), 13, "tail_c")
    (tail,) = sum_step((), 14, "tail_gather", (Hand(tail, TAIL, False),))
    grad_query, grad_key, grad_value, grad_out, grad_router, grad_gain_one = lay_out_attention(
        tail.reshape(4, SHARD, TAIL), w_query, w_key, w_value, norm_gain[None]
    )
    grad_gate, grad_up, grad_down, grad_gain_two = lay_out_experts(
        place_here, [one.reshape((-1,) + one.shape[-2:]) for one in pieces[0] + pieces[1]], w_gate, w_up, w_router, grad_router, moe_gain[None]
    )
    return (
        result[None],
        loss_value,
        d_inputs[None],
        grad_query,
        grad_key,
        grad_value,
        grad_out,
        grad_gain_one[0],
        grad_router,
        grad_gain_two[0],
        grad_gate,
        grad_up,
        grad_down,
    )


def solution(mesh):
    in_specs = (
        P("fsdp", "ctx", None),
        P("fsdp", "ctx", None),
        P("fsdp", "ctx"),
        P(),
        P("fsdp", "ctx", None),
        P(),
        P("fsdp", None),
        P("fsdp", None),
        P("fsdp", None),
        P("fsdp", None),
        P("fsdp"),
        P("fsdp", None),
        P("fsdp"),
        P(None, "fsdp", None),
        P(None, "fsdp", None),
        P(None, None, "fsdp"),
    )
    out_specs = (
        P("fsdp", "ctx", None),
        P(),
        P("fsdp", "ctx", None),
        P("fsdp", None),
        P("fsdp", None),
        P("fsdp", None),
        P("fsdp", None),
        P("fsdp"),
        P("fsdp", None),
        P("fsdp"),
        P(None, "fsdp", None),
        P(None, "fsdp", None),
        P(None, None, "fsdp"),
    )
    return jax.shard_map(local, mesh=mesh, in_specs=in_specs, out_specs=out_specs, check_vma=False)
```
